32 devices in a mesh: pix: 8 (over y, x, core), tm: 4 (over z).
Axes of the slice: x: 2, y: 2, z: 4, core: 2. Of those that a mesh axis runs over, the one named last changes fastest.
Arguments:
- raw_frames: float32 [1024, 65536], P(('tm', 'pix')), may hold values from 1 to 64
- frame_order: int32 [1024], P(('tm', 'pix')), may hold values from 0 to 31, as said below
- owner_map: int32 [512], replicated, may hold values from 0 to 511, each once
- pixel_mask: int32 [65536], replicated, may hold values 0 or 1
- dark: float32 [65536], replicated, may hold values from 0 to 0.5
- flat: float32 [65536], replicated, may hold values from 0.5 to 1.5
- polarization: float32 [65536], replicated, may hold values from 0.5 to 1
- solid_angle: float32 [65536], replicated, may hold values from 0.6 to 1
Outputs:
- g2: float32 [4, 16, 65536], P(None, None, ('pix', 'tm'))
- mean_frame: float32 [65536], P(('pix', 'tm'))
The draws below stay inside these ranges and needn't reach their ends.
Inputs may be any that keep to these rules, and one draw needn't show every extreme that they name: `frame_order`: each aligned block of 32 entries is a permutation of 0 .. 31. `owner_map`: a permutation of the block numbers.
All inputs are finite; a program needn't handle non-finite values.
Results may differ from the reference program's by a relative error of at most 0.0003.
Values sent between devices are 32-bit elements; how exact they have to be, the bound alone decides.
No kernel may reach another device: no remote copies, remote signals or barrier semaphores. Data moves between devices by JAX's collectives and lax.ppermute only.
A program may use at most 128 MiB of HBM per device.

```python
import math
import jax
import jax.numpy as jnp
from jax import lax

FRAMES = 1024
LAGS = 16
LEVELS = 4
BLK = 128
PIX_DEV = 8192
NPIX = 65536
NBLK = 512
READ = 32
N_PIX = 8
N_TM = 4


def draw_frame_order(key, part):
    block_keys = jax.random.split(jax.random.fold_in(key, 17), FRAMES // READ)
    shuffled = jax.vmap(lambda one_key: jax.random.permutation(one_key, READ))(block_keys)
    return shuffled.reshape(FRAMES).astype(jnp.int32)


def place_ends(drawn, stream_key, least, high):
    index_at = [jax.random.randint(jax.random.fold_in(stream_key, axis), (), 0, length) for axis, length in enumerate(drawn.shape)]
    main_axis = drawn.shape.index(max(drawn.shape))
    next_to = index_at[:main_axis] + [(index_at[main_axis] + 1) % drawn.shape[main_axis]] + index_at[main_axis + 1:]
    return drawn.at[tuple(index_at)].set(least).at[tuple(next_to)].set(high)


def block_levels(rng, shape, shards, smallest, top_value):
    def one(position, parts):
        heights = jax.random.uniform(jax.random.fold_in(jax.random.fold_in(rng, 6), position), (parts,), jnp.float32, smallest / len(shards), top_value / len(shards))
        return jnp.repeat(jnp.exp(heights), shape[position] // parts).reshape((-1,) + (1,) * (len(shape) - position - 1))

    level = one(*shards[0])
    for cut in shards[1:]:
        level = level * one(*cut)
    return level


def setup_inputs(seed: int = 0) -> dict:
    key_of = jax.random.split(jax.random.key(seed), 9)
    return {
        "raw_frames": jnp.clip(jnp.exp(math.log(64.0) - 4.158883 * jax.random.uniform(key_of[0], (FRAMES, NPIX), jnp.float32) ** block_levels(key_of[0], (FRAMES, NPIX), ((0, 32),), -0.2, 0.2)), 1.0, 64.0),
        "frame_order": draw_frame_order(jax.random.fold_in(key_of[8], 71), 0),
        "owner_map": jax.random.permutation(key_of[2], NBLK).astype(jnp.int32),
        "pixel_mask": place_ends((jax.random.randint(key_of[3], (NPIX,), 0, 10) < 9).astype(jnp.int32), jax.random.fold_in(key_of[3], 1), 0, 1),
        "dark": jnp.clip(jax.random.uniform(key_of[4], (NPIX,), jnp.float32, 0.0, 0.5), 0.0, 0.5),
        "flat": jnp.clip(1.0 + 0.1 * jax.random.normal(key_of[5], (NPIX,), jnp.float32), 0.5, 1.5),
        "polarization": jnp.clip(jax.random.uniform(key_of[6], (NPIX,), jnp.float32, 0.5, 1.0), 0.5, 1.0),
        "solid_angle": jnp.clip(jax.random.uniform(key_of[7], (NPIX,), jnp.float32, 0.6, 1.0), 0.6, 1.0),
    }


def coarsen(series):
    pairs = series.reshape(series.shape[0] // 2, 2, series.shape[1])
    return 0.5 * (pairs[:, 0] + pairs[:, 1])


def reference(raw_frames, frame_order, owner_map, pixel_mask, dark, flat, polarization, solid_angle):
    read_len = FRAMES // (N_TM * N_PIX)
    rows_idx = (jnp.arange(FRAMES, dtype=jnp.int32) // read_len) * read_len + frame_order.astype(jnp.int32)
    timed = jnp.take(raw_frames, rows_idx, axis=0)
    source = (owner_map[:, None].astype(jnp.int32) * BLK + jnp.arange(BLK, dtype=jnp.int32)[None, :]).reshape(NPIX)
    response = flat * polarization * solid_angle

    def one_group(group_no):
        picked = lax.dynamic_slice_in_dim(source, (group_no * PIX_DEV).astype(jnp.int32), PIX_DEV)
        block_data = jnp.take(timed, picked, axis=1)
        corrected = (block_data - jnp.take(dark, picked)) / jnp.take(response, picked)
        mean_raw = jnp.sum(corrected, axis=0) / FRAMES
        keeper = jnp.take(pixel_mask, picked).astype(jnp.float32)
        series = corrected
        results = []
        for level_no in range(LEVELS):
            length = FRAMES >> level_no
            products = []
            for lag_no in range(1, LAGS + 1):
                products.append(jnp.sum(series[:length - lag_no] * series[lag_no:], axis=0))
            product = jnp.stack(products)
            counts = (length - jnp.arange(1, LAGS + 1, dtype=jnp.int32)).astype(jnp.float32)[:, None]
            results.append(product / (counts * mean_raw * mean_raw) * keeper)
            if level_no + 1 < LEVELS:
                series = coarsen(series)
        return jnp.stack(results), mean_raw * keeper

    corr_all, means_all = lax.map(one_group, jnp.arange(NPIX // PIX_DEV, dtype=jnp.int32))
    g2 = jnp.transpose(corr_all, (1, 2, 0, 3)).reshape(LEVELS, LAGS, NPIX)
    return g2, means_all.reshape(NPIX)
```

```python
import functools

import jax
import jax.numpy as jnp
from jax import lax
from jax.experimental import pallas as pl
from jax.experimental.pallas import tpu as pltpu
from jax.sharding import PartitionSpec as P

FRAMES = 1024
LAGS = 16
LEVELS = 4
ROWS = LEVELS * LAGS
EDGE = LAGS + 8 * (LEVELS - 1)
EDGE_SPAN = LAGS << (LEVELS - 1)

PARTS = (("seg", 2), ("seg", 2), ("seg", 2), ("seg", 2))

SMEM = pl.BlockSpec(memory_space=pltpu.SMEM)
VMEM = pl.BlockSpec(memory_space=pltpu.VMEM)
HBM = pl.BlockSpec(memory_space=pl.ANY)
F32 = jnp.float32


def params(**kw):
    return pltpu.CompilerParams(vmem_limit_bytes=40 << 20, **kw)


def pack_kernel(dims, frames_ref, order_ref, owner_ref, out_ref, held, sem):
    n_pix, share, start, per, count, rows, owned = dims
    total = n_pix * count

    @pl.loop(0, total)
    def _(at):
        dest, pos = at // count, at % count
        block = owner_ref[dest * owned + (pos // per) * share + start + pos % per]
        pltpu.make_async_copy(
            frames_ref.at[:, pl.ds(pl.multiple_of(block * 128, 128), 128)],
            held.at[pl.ds(pl.multiple_of(at * rows, rows), rows), :],
            sem,
        ).start()

    pltpu.make_async_copy(held, held, sem).wait()

    @pl.loop(0, rows)
    def _(row):
        slot = order_ref[row]
        for dest in range(n_pix):
            for group in range(count // 8):
                first = (dest * count + group * 8) * rows
                out_ref[dest, row, pl.ds(group * 8, 8), :] = held[pl.ds(first + slot, 8, stride=rows), :]


def pack_part(raw_frames, frame_order, owner_map, dims):
    n_pix, share, start, per, count, rows, owned = dims
    shape = (n_pix, rows, count, 128)
    size = 4 * n_pix * rows * count * 128
    return pl.pallas_call(
        functools.partial(pack_kernel, dims),
        out_shape=jax.ShapeDtypeStruct(shape, F32),
        in_specs=[HBM, SMEM, SMEM],
        out_specs=VMEM,
        scratch_shapes=[pltpu.VMEM((n_pix * count * rows, 128), F32), pltpu.SemaphoreType.DMA],
        compiler_params=params(),
        cost_estimate=pl.CostEstimate(flops=0, bytes_accessed=2 * size, transcendentals=0),
    )(raw_frames, frame_order, owner_map)


def constants_kernel(
    plan, owned, share, where_ref, owner_ref, dark_ref, flat_ref, pol_ref, solid_ref, mask_ref, dark_out, resp_out, keep_out
):
    base = where_ref[0] * owned
    mine = base + where_ref[1] * share
    for at, shift in enumerate(plan):
        dark_out[at : at + 1, :] = dark_ref[pl.ds(owner_ref[base + shift], 1), :]
    for at in range(share):
        row = pl.ds(owner_ref[mine + at], 1)
        resp_out[at : at + 1, :] = flat_ref[row, :] * pol_ref[row, :] * solid_ref[row, :]
        keep_out[at : at + 1, :] = mask_ref[row, :].astype(F32)


def pair_sums(rows):
    return [rows[2 * i] + rows[2 * i + 1] for i in range(len(rows) // 2)]


def edge_kernel(last, series_ref, dark_ref, out_ref):
    dark = dark_ref[...]
    span = 0
    for level in range(LEVELS):
        count = LAGS if level == 0 else LAGS // 2
        width = 1 << level
        first = EDGE_SPAN - span - count * width if last else span
        for i in range(count):
            at = first + i * width
            rows = [series_ref[at + j] - dark for j in range(width)]
            while len(rows) > 1:
                rows = pair_sums(rows)
            out_ref[0, (LAGS + 8 * (level - 1) if level else 0) + i] = rows[0]
        span += count * width


def edge_part(series, dark, last):
    length, count, _ = series.shape
    groups = count // 8
    block = length // EDGE_SPAN - 1 if last else 0
    return pl.pallas_call(
        functools.partial(edge_kernel, last),
        out_shape=jax.ShapeDtypeStruct((groups, EDGE, 8, 128), F32),
        grid=(groups,),
        in_specs=[
            pl.BlockSpec((EDGE_SPAN, 8, 128), lambda g: (block, g, 0)),
            pl.BlockSpec((8, 128), lambda g: (g, 0)),
        ],
        out_specs=pl.BlockSpec((1, EDGE, 8, 128), lambda g: (g, 0, 0, 0)),
        compiler_params=params(),
        cost_estimate=pl.CostEstimate(
            flops=2 * EDGE_SPAN * count * 128, bytes_accessed=4 * EDGE_SPAN * count * 128, transcendentals=0
        ),
    )(series, dark)


def add_lags(older, newer, sums, cross_only=False):
    both = older + newer
    out = []
    for lag in range(1, LAGS + 1):
        total = sums[lag - 1]
        for i in range(lag if cross_only else LAGS):
            total = total + both[LAGS + i] * both[LAGS + i - lag]
        out.append(total)
    return out


def edge_rows(halo_ref, last):
    rows = [halo_ref[0, i] for i in range(LAGS)]
    levels = [rows]
    for level in range(1, LEVELS):
        own = [halo_ref[0, LAGS + 8 * (level - 1) + i] for i in range(8)]
        rows = own + pair_sums(rows) if last else pair_sums(rows) + own
        levels.append(rows)
    return levels


def sums_kernel(per, last, series_ref, dark_ref, halo_ref, out_ref, up_one, up_two, up_three, flat):
    length = series_ref.shape[0]
    group = pl.program_id(0)
    dark = dark_ref[...]
    zero = jnp.zeros((8, 128), F32)
    stores = (up_one, up_two, up_three, None)
    halo = edge_rows(halo_ref, last)
    total = zero
    for level in range(LEVELS):
        steps = (length >> level) // LAGS
        store = stores[level]
        source = None if level == 0 else stores[level - 1]

        def step(index, carry, source=source, store=store):
            older, sums, total = carry
            at = index * LAGS
            if source is None:
                newer = [series_ref[at + i] - dark for i in range(LAGS)]
            else:
                newer = [source[at + i] for i in range(LAGS)]
            pairs = pair_sums(newer)
            if store is not None:
                half = index * (LAGS // 2)
                for i in range(LAGS // 2):
                    store[half + i] = pairs[i]
            if source is None:
                while len(pairs) > 1:
                    pairs = pair_sums(pairs)
                total = total + pairs[0]
            return newer, add_lags(older, newer, sums), total

        before = halo[level] if last else [zero] * LAGS
        older, sums, total = lax.fori_loop(0, steps, step, (before, [zero] * LAGS, total))
        if not last:
            sums = add_lags(older, halo[level], sums, cross_only=True)
        for lag in range(LAGS):
            flat[pl.ds(level * LAGS + lag, 8, stride=ROWS), :] = sums[lag]

    @pl.when(group == 0)
    def _():
        pad = out_ref.shape[1] - per * ROWS
        out_ref[:, pl.ds(per * ROWS, pad), :] = jnp.zeros((out_ref.shape[0], pad, 128), F32)

    for i in range(8):
        pos = group * 8 + i
        owner, at = pos // per, pos % per
        out_ref[owner, pl.ds(pl.multiple_of(at * ROWS, ROWS), ROWS), :] = flat[i * ROWS : (i + 1) * ROWS, :]
        out_ref[owner, pl.ds(per * ROWS + at, 1), :] = total[i : i + 1, :]


def sum_rows(per):
    return per * ROWS + (per + 7) // 8 * 8


def sums_part(series, dark, halo, per, last):
    length, count, _ = series.shape
    groups = count // 8
    n_tm = count // per
    shape = (n_tm, sum_rows(per), 128)
    return pl.pallas_call(
        functools.partial(sums_kernel, per, last),
        out_shape=jax.ShapeDtypeStruct(shape, F32),
        grid=(groups,),
        in_specs=[
            pl.BlockSpec((length, 8, 128), lambda g: (0, g, 0)),
            pl.BlockSpec((8, 128), lambda g: (g, 0)),
            pl.BlockSpec((1, EDGE, 8, 128), lambda g: (g, 0, 0, 0)),
        ],
        out_specs=pl.BlockSpec(shape, lambda g: (0, 0, 0)),
        scratch_shapes=[
            pltpu.VMEM((length // 2, 8, 128), F32),
            pltpu.VMEM((length // 4, 8, 128), F32),
            pltpu.VMEM((length // 8, 8, 128), F32),
            pltpu.VMEM((8 * ROWS, 128), F32),
        ],
        compiler_params=params(),
        cost_estimate=pl.CostEstimate(
            flops=2 * 2 * LAGS * length * count * 128, bytes_accessed=4 * length * count * 128, transcendentals=0
        ),
    )(series, dark, halo)


def finish_kernel(parts, resp_ref, keep_ref, *refs):
    sums_refs, (g2_ref, mean_ref) = refs[:-2], refs[-2:]
    row = lax.broadcasted_iota(jnp.int32, (ROWS, 128), 0)
    level, lag = row // LAGS, row % LAGS + 1
    counts = (((FRAMES >> level) - lag) << (2 * level)).astype(F32)
    for (start, per), ref in zip(parts, sums_refs):
        for at in range(per):
            product = jnp.sum(ref[:, at * ROWS : (at + 1) * ROWS, :], axis=0)
            total = jnp.sum(ref[:, per * ROWS + at : per * ROWS + at + 1, :], axis=0)
            block = start + at
            keep = keep_ref[block : block + 1, :]
            mean = total * (1.0 / FRAMES)
            g2_ref[:, block * 128 : (block + 1) * 128] = product / (counts * mean * mean) * keep
            mean_ref[block : block + 1, :] = mean / resp_ref[block : block + 1, :] * keep


def body(raw_frames, frame_order, owner_map, pixel_mask, dark, flat, polarization, solid_angle):
    n_pix = lax.axis_size("pix")
    n_tm = lax.axis_size("tm")
    rows = raw_frames.shape[0]
    n_blocks = owner_map.shape[0]
    owned = n_blocks // n_pix
    share = owned // n_tm
    segment = FRAMES // n_tm

    plan = []
    start = 0
    for kind, eighths in PARTS:
        per = share * eighths // 8
        plan.append((kind, start, per))
        start += per

    shifts = [g * share + start + j for _, start, per in plan for g in range(n_tm) for j in range(per)]
    where = jnp.stack([lax.axis_index("pix"), lax.axis_index("tm")]).astype(jnp.int32)
    tables = [t.reshape(n_blocks, 128) for t in (dark, flat, polarization, solid_angle, pixel_mask)]
    dark_own, resp_own, keep_own = pl.pallas_call(
        functools.partial(constants_kernel, shifts, owned, share),
        out_shape=[
            jax.ShapeDtypeStruct((owned, 128), F32),
            jax.ShapeDtypeStruct((share, 128), F32),
            jax.ShapeDtypeStruct((share, 128), F32),
        ],
        in_specs=[SMEM, SMEM] + [VMEM] * 5,
        out_specs=[VMEM] * 3,
        compiler_params=params(),
        cost_estimate=pl.CostEstimate(flops=0, bytes_accessed=5 * 4 * n_blocks * 128, transcendentals=0),
    )(where, owner_map, *tables)

    sums = []
    used = 0
    for index, (kind, start, per) in enumerate(plan):
        count = n_tm * per
        packed = pack_part(raw_frames, frame_order, owner_map, (n_pix, share, start, per, count, rows, owned))
        got = lax.all_to_all(packed, "pix", split_axis=0, concat_axis=0, tiled=True)
        series = got.reshape(segment, count, 128)
        dark_part = dark_own[used : used + count]
        used += count
        last = index % 2 == 0
        edge = edge_part(series, dark_part, last)
        pairs = [(i, i + 1) if last else (i + 1, i) for i in range(n_tm - 1)]
        halo = lax.ppermute(edge, "tm", pairs)
        mine = sums_part(series, dark_part, halo, per, last)
        sums.append(lax.all_to_all(mine, "tm", split_axis=0, concat_axis=0, tiled=True))

    g2, mean = pl.pallas_call(
        functools.partial(finish_kernel, [(start, per) for _, start, per in plan]),
        out_shape=[
            jax.ShapeDtypeStruct((ROWS, share * 128), F32),
            jax.ShapeDtypeStruct((share, 128), F32),
        ],
        in_specs=[VMEM] * (2 + len(sums)),
        out_specs=[VMEM, VMEM],
        compiler_params=params(),
    )(resp_own, keep_own, *sums)
    return g2.reshape(LEVELS, LAGS, share * 128), mean.reshape(share * 128)


def solution(mesh):
    return jax.shard_map(
        body,
        mesh=mesh,
        in_specs=(P(("tm", "pix"), None), P(("tm", "pix")), P(), P(), P(), P(), P(), P()),
        out_specs=(P(None, None, ("pix", "tm")), P(("pix", "tm"))),
        check_vma=False,
    )
```

```python
import functools

import jax
import jax.numpy as jnp
from jax import lax
from jax.experimental import pallas as pl
from jax.experimental.pallas import tpu as pltpu
from jax.sharding import PartitionSpec as P

FRAMES = 1024
LAGS = 16
LEVELS = 4
ROWS = LEVELS * LAGS
EDGE = LAGS + 8 * (LEVELS - 1)
EDGE_SPAN = LAGS << (LEVELS - 1)

PARTS = (("seg", 4), ("seg", 2), ("full", 2))

SMEM = pl.BlockSpec(memory_space=pltpu.SMEM)
VMEM = pl.BlockSpec(memory_space=pltpu.VMEM)
HBM = pl.BlockSpec(memory_space=pl.ANY)
F32 = jnp.float32


def params():
    return pltpu.CompilerParams(vmem_limit_bytes=40 << 20)


def cost(micros):
    return pl.CostEstimate(flops=0, bytes_accessed=int(micros * 3.6e6), transcendentals=0)


def shape(*dims):
    return jax.ShapeDtypeStruct(dims, F32)


def pack_kernel(jobs, owned, share, n_pix, n_tm, where_ref, order_ref, owner_ref, frames_ref, *refs):
    outs, inverse = refs[:-1], refs[-1]
    rows = frames_ref.shape[0]
    pix, tm = where_ref[0], where_ref[1]
    for i in range(rows):
        inverse[order_ref[i]] = i

    def eight(position_of, store):
        blocks = [owner_ref[position_of(i)] for i in range(8)]
        for high in range(rows // 8):
            tiles = [
                frames_ref[high * 8 : high * 8 + 8, pl.ds(pl.multiple_of(block * 128, 128), 128)] for block in blocks
            ]
            turned = jnp.swapaxes(jnp.stack(tiles), 0, 1)
            for low in range(8):
                store(inverse[high * 8 + low], turned[low])

    taken = 0
    for kind, start, per in jobs:
        if kind == "seg":
            for other in range(n_pix):
                out = outs[taken + other]
                base = (pix ^ other) * owned + start

                @pl.loop(0, out.shape[1] // 8)
                def _(group, out=out, base=base, per=per):
                    def position_of(i):
                        pos = group * 8 + i
                        return base + (pos // per) * share + pos % per

                    def store(row, value):
                        out[row, pl.ds(pl.multiple_of(group * 8, 8), 8), :] = value

                    eight(position_of, store)

            taken += n_pix
        else:
            for other in range(n_tm):
                out = outs[taken + other]
                base = (tm ^ other) * share + start
                width = 8 // n_tm

                @pl.loop(0, out.shape[0] * out.shape[1])
                def _(at, out=out, base=base, width=width):
                    unit, group = at // out.shape[1], at % out.shape[1]

                    def position_of(i):
                        pos = group * 8 + i
                        return base + (pos // width) * owned + unit * width + pos % width

                    def store(row, value):
                        out[unit, group, row] = value

                    eight(position_of, store)

            taken += n_tm


def pack_parts(where, raw_frames, frame_order, owner_map, jobs, owned, share, n_pix, n_tm):
    rows = raw_frames.shape[0]
    outs = []
    size = 0
    for kind, _, per in jobs:
        if kind == "seg":
            outs += [shape(rows, n_tm * per, 128)] * n_pix
        else:
            width = 8 // n_tm
            outs += [shape(per // width, n_pix * width // 8, rows, 8, 128)] * n_tm
        size += per
    flat = pl.pallas_call(
        functools.partial(pack_kernel, jobs, owned, share, n_pix, n_tm),
        out_shape=outs,
        in_specs=[SMEM, SMEM, SMEM, VMEM],
        out_specs=[VMEM] * len(outs),
        scratch_shapes=[pltpu.SMEM((rows,), jnp.int32)],
        compiler_params=params(),
        cost_estimate=cost(2.0 + 6.0 * size / share),
    )(where, frame_order, owner_map, raw_frames)
    result = []
    for kind, _, _ in jobs:
        n = n_pix if kind == "seg" else n_tm
        result.append(list(flat[:n]))
        flat = flat[n:]
    return result


def turn_kernel(n_pix, n_tm, where_ref, *refs):
    pieces, outs, (held, staged, sem) = refs[:n_tm], refs[n_tm : n_tm + n_pix], refs[n_tm + n_pix :]
    pix, tm = where_ref[0], where_ref[1]
    units, groups, rows = pieces[0].shape[:3]
    width = 8 // n_tm
    for other in range(n_tm):
        pltpu.make_async_copy(pieces[other], held.at[tm ^ other], sem).start()
    pltpu.make_async_copy(held, held, sem).wait()
    place = lax.broadcasted_iota(jnp.int32, (8, 128), 0) // width

    @pl.loop(0, rows)
    def _(row):
        for unit in range(units):
            for group in range(groups):
                got = [held[m, unit, group, row] for m in range(n_tm)]
                for to in range(n_tm):
                    value = got[to]
                    for m in range(n_tm):
                        if m != to:
                            value = jnp.where(place == m, pltpu.roll(got[m], (m - to) * width % 8, 0), value)
                    staged[group * n_tm + to, row, unit * 8 : unit * 8 + 8, :] = value

    for other in range(n_pix):
        outs[other][...] = staged[pix ^ other]


def turn_part(where, pieces, n_pix, n_tm):
    units, groups, rows = pieces[0].shape[:3]
    return pl.pallas_call(
        functools.partial(turn_kernel, n_pix, n_tm),
        out_shape=[shape(rows, units * 8, 128)] * n_pix,
        in_specs=[SMEM] + [HBM] * n_tm,
        out_specs=[VMEM] * n_pix,
        scratch_shapes=[
            pltpu.VMEM((n_tm,) + pieces[0].shape, F32),
            pltpu.VMEM((n_pix, rows, units * 8, 128), F32),
            pltpu.SemaphoreType.DMA,
        ],
        compiler_params=params(),
        cost_estimate=cost(3.0),
    )(where, *pieces)


def constants_kernel(
    plan, owned, share, where_ref, owner_ref, dark_ref, flat_ref, pol_ref, solid_ref, mask_ref, dark_out, resp_out, keep_out
):
    base = where_ref[0] * owned
    mine = base + where_ref[1] * share
    for at, (from_mine, shift) in enumerate(plan):
        row = pl.ds(owner_ref[(mine if from_mine else base) + shift], 1)
        dark_out[at : at + 1, :] = dark_ref[row, :]
    for at in range(share):
        row = pl.ds(owner_ref[mine + at], 1)
        resp_out[at : at + 1, :] = flat_ref[row, :] * pol_ref[row, :] * solid_ref[row, :]
        keep_out[at : at + 1, :] = mask_ref[row, :].astype(F32)


def pair_sums(rows):
    return [rows[2 * i] + rows[2 * i + 1] for i in range(len(rows) // 2)]


def edge_kernel(last, n_pix, where_ref, dark_ref, *refs):
    pieces, (out_ref, held, sem) = refs[:n_pix], refs[n_pix:]
    rows = pieces[0].shape[0]
    first = n_pix - EDGE_SPAN // rows if last else 0
    for other in range(n_pix):
        at = (where_ref[0] ^ other) - first

        @pl.when((at >= 0) & (at < EDGE_SPAN // rows))
        def _(other=other, at=at):
            pltpu.make_async_copy(pieces[other], held.at[pl.ds(at * rows, rows)], sem).start()

    pltpu.make_async_copy(held, held, sem).wait()

    @pl.loop(0, out_ref.shape[0])
    def _(group):
        lanes = pl.ds(pl.multiple_of(group * 8, 8), 8)
        dark = dark_ref[lanes, :]
        span = 0
        for level in range(LEVELS):
            count = LAGS if level == 0 else LAGS // 2
            width = 1 << level
            begin = EDGE_SPAN - span - count * width if last else span
            for i in range(count):
                at = begin + i * width
                got = [held[at + j, lanes, :] - dark for j in range(width)]
                while len(got) > 1:
                    got = pair_sums(got)
                out_ref[group, (LAGS + 8 * (level - 1) if level else 0) + i] = got[0]
            span += count * width


def edge_part(where, pieces, dark, last):
    n_pix = len(pieces)
    count = pieces[0].shape[1]
    return pl.pallas_call(
        functools.partial(edge_kernel, last, n_pix),
        out_shape=shape(count // 8, EDGE, 8, 128),
        in_specs=[SMEM, VMEM] + [HBM] * n_pix,
        out_specs=VMEM,
        scratch_shapes=[pltpu.VMEM((EDGE_SPAN, count, 128), F32), pltpu.SemaphoreType.DMA],
        compiler_params=params(),
        cost_estimate=cost(2.0),
    )(where, dark, *pieces)


def add_lags(older, newer, sums, cross_only=False):
    both = older + newer
    out = []
    for lag in range(1, LAGS + 1):
        total = sums[lag - 1]
        for i in range(lag if cross_only else LAGS):
            total = total + both[LAGS + i] * both[LAGS + i - lag]
        out.append(total)
    return out


def edge_rows(read, last):
    rows = [read(i) for i in range(LAGS)]
    levels = [rows]
    for level in range(1, LEVELS):
        own = [read(LAGS + 8 * (level - 1) + i) for i in range(8)]
        rows = own + pair_sums(rows) if last else pair_sums(rows) + own
        levels.append(rows)
    return levels


def sums_kernel(kind, last, n_pix, n_tm, per, where_ref, dark_ref, halo_ref, *refs):
    pieces, rest = refs[:n_pix], refs[n_pix:]
    outs, (series, up_one, up_two, up_three, flat, totals, sem) = rest[:-7], rest[-7:]
    rows = pieces[0].shape[0]
    length = rows * n_pix
    for other in range(n_pix):
        pltpu.make_async_copy(
            pieces[other], series.at[pl.ds((where_ref[0] ^ other) * rows, rows)], sem
        ).start()
    pltpu.make_async_copy(series, series, sem).wait()
    zero = jnp.zeros((8, 128), F32)
    stores = (up_one, up_two, up_three, None)
    width = 8 // n_tm
    inner = lax.broadcasted_iota(jnp.int32, (8, 128), 0) < 8 - width

    @pl.loop(0, series.shape[1] // 8)
    def _(group):
        lanes = pl.ds(pl.multiple_of(group * 8, 8), 8)
        dark = dark_ref[lanes, :]
        if kind == "seg":
            halo = edge_rows(lambda i: halo_ref[group, i], last)
        total = zero
        for level in range(LEVELS):
            steps = (length >> level) // LAGS
            store = stores[level]
            source = None if level == 0 else stores[level - 1]

            def read(at, source=source):
                return series[at, lanes, :] - dark if source is None else source[at]

            def step(index, carry, read=read, level=level, store=store):
                older, sums, total = carry
                newer = [read(index * LAGS + i) for i in range(LAGS)]
                pairs = pair_sums(newer)
                if store is not None:
                    for i in range(LAGS // 2):
                        store[index * (LAGS // 2) + i] = pairs[i]
                if level == 0:
                    while len(pairs) > 1:
                        pairs = pair_sums(pairs)
                    total = total + pairs[0]
                return newer, add_lags(older, newer, sums), total

            before = halo[level] if kind == "seg" and last else [zero] * LAGS
            older, sums, total = lax.fori_loop(0, steps, step, (before, [zero] * LAGS, total))
            if kind == "full":
                after = [jnp.where(inner, pltpu.roll(read(i), 8 - width, 0), 0.0) for i in range(LAGS)]
                sums = add_lags(older, after, sums, cross_only=True)
            elif not last:
                sums = add_lags(older, halo[level], sums, cross_only=True)
            for lag in range(LAGS):
                flat[group, pl.ds(level * LAGS + lag, 8, stride=ROWS), :] = sums[lag]
        totals[group] = total

    def put(out, at, block, extra):
        group, low = block // 8, block % 8
        begin = pl.multiple_of(low * ROWS, ROWS)
        value = flat[group, pl.ds(begin, ROWS), :]
        total = totals[group, pl.ds(low, 1), :]
        for m in range(1, extra):
            value = value + flat[group, pl.ds(begin + m * width * ROWS, ROWS), :]
            total = total + totals[group, pl.ds(low + m * width, 1), :]
        out[at * ROWS : (at + 1) * ROWS, :] = value
        out[per * ROWS + at : per * ROWS + at + 1, :] = total

    for other, out in enumerate(outs):
        out[per * ROWS :, :] = jnp.zeros((out.shape[0] - per * ROWS, 128), F32)
        for at in range(per):
            if kind == "seg":
                put(out, at, (where_ref[1] ^ other) * per + at, 1)
            else:
                put(out, at, at // width * 8 + at % width, n_tm)


def sum_rows(per):
    return per * ROWS + (per + 7) // 8 * 8


def sums_part(where, pieces, dark, halo, kind, per, last, n_tm):
    n_pix = len(pieces)
    rows, count, _ = pieces[0].shape
    length = n_pix * rows
    return pl.pallas_call(
        functools.partial(sums_kernel, kind, last, n_pix, n_tm, per),
        out_shape=[shape(sum_rows(per), 128)] * (n_tm if kind == "seg" else 1),
        in_specs=[SMEM, VMEM, VMEM] + [HBM] * n_pix,
        out_specs=[VMEM] * (n_tm if kind == "seg" else 1),
        scratch_shapes=[
            pltpu.VMEM((length, count, 128), F32),
            pltpu.VMEM((length // 2, 8, 128), F32),
            pltpu.VMEM((length // 4, 8, 128), F32),
            pltpu.VMEM((length // 8, 8, 128), F32),
            pltpu.VMEM((count // 8, 8 * ROWS, 128), F32),
            pltpu.VMEM((count // 8, 8, 128), F32),
            pltpu.SemaphoreType.DMA,
        ],
        compiler_params=params(),
        cost_estimate=cost(1.0 + 3.0 * length * count / 2048),
    )(where, dark, halo, *pieces)


def finish_kernel(parts, resp_ref, keep_ref, *refs):
    sums_refs, (g2_ref, mean_ref) = refs[:-2], refs[-2:]
    row = lax.broadcasted_iota(jnp.int32, (ROWS, 128), 0)
    level, lag = row // LAGS, row % LAGS + 1
    counts = (((FRAMES >> level) - lag) << (2 * level)).astype(F32)
    for start, per, terms in parts:
        mine, sums_refs = sums_refs[:terms], sums_refs[terms:]
        for at in range(per):
            product = sum(ref[at * ROWS : (at + 1) * ROWS, :] for ref in mine)
            total = sum(ref[per * ROWS + at : per * ROWS + at + 1, :] for ref in mine)
            block = start + at
            keep = keep_ref[block : block + 1, :]
            mean = total * (1.0 / FRAMES)
            g2_ref[:, block * 128 : (block + 1) * 128] = product / (counts * mean * mean) * keep
            mean_ref[block : block + 1, :] = mean / resp_ref[block : block + 1, :] * keep


def swap(value, axis, other):
    return lax.ppermute(value, axis, [(i, i ^ other) for i in range(lax.axis_size(axis))])


def after(value, earlier):
    return lax.optimization_barrier((value, earlier))


def body(raw_frames, frame_order, owner_map, pixel_mask, dark, flat, polarization, solid_angle):
    n_pix = lax.axis_size("pix")
    n_tm = lax.axis_size("tm")
    n_blocks = owner_map.shape[0]
    owned = n_blocks // n_pix
    share = owned // n_tm
    width = 8 // n_tm

    plan = []
    shifts = []
    start = 0
    for kind, eighths in PARTS:
        per = share * eighths // 8
        plan.append((kind, start, per))
        if kind == "seg":
            shifts += [(False, g * share + start + j) for g in range(n_tm) for j in range(per)]
        else:
            shifts += [
                (True, start + unit * width + j) for unit in range(per // width) for _ in range(n_tm) for j in range(width)
            ]
        start += per

    where = jnp.stack([lax.axis_index("pix"), lax.axis_index("tm")]).astype(jnp.int32)
    tables = [t.reshape(n_blocks, 128) for t in (dark, flat, polarization, solid_angle, pixel_mask)]
    dark_own, resp_own, keep_own = pl.pallas_call(
        functools.partial(constants_kernel, shifts, owned, share),
        out_shape=[shape(owned, 128), shape(share, 128), shape(share, 128)],
        in_specs=[SMEM, SMEM] + [VMEM] * 5,
        out_specs=[VMEM] * 3,
        compiler_params=params(),
        cost_estimate=cost(1.0),
    )(where, owner_map, *tables)

    pack = functools.partial(pack_parts, where, raw_frames, frame_order, owner_map)
    sizes = (owned, share, n_pix, n_tm)
    (first,) = pack(plan[:1], *sizes)
    packed = [first] + pack(plan[1:], *sizes)

    for index, (kind, _, _) in enumerate(plan):
        if kind == "full":
            mine = packed[index]
            got = [mine[0]] + [swap(mine[k], "tm", k) for k in range(1, n_tm)]
            packed[index] = turn_part(where, got, n_pix, n_tm)

    terms = []
    used = 0
    earlier = None
    for index, (kind, start, per) in enumerate(plan):
        mine = packed[index]
        got = [mine[0]]
        for k in range(1, n_pix):
            sent = mine[k]
            if earlier is not None:
                sent, earlier[k] = after(sent, earlier[k])
            got.append(swap(sent, "pix", k))
        earlier = got
        count = n_tm * per
        dark_part = dark_own[used : used + count]
        used += count
        if kind == "seg":
            last = index % 2 == 0
            edge = edge_part(where, got, dark_part, last)
            pairs = [(i, i + 1) if last else (i + 1, i) for i in range(n_tm - 1)]
            halo = lax.ppermute(edge, "tm", pairs)
            mine = sums_part(where, got, dark_part, halo, kind, per, last, n_tm)
            terms.append([mine[0]] + [swap(mine[k], "tm", k) for k in range(1, n_tm)])
        else:
            terms.append(sums_part(where, got, dark_part, dark_part, kind, per, False, n_tm))

    flat_terms = [value for part in terms for value in part]
    g2, mean = pl.pallas_call(
        functools.partial(
            finish_kernel, [(start, per, len(part)) for (_, start, per), part in zip(plan, terms)]
        ),
        out_shape=[shape(ROWS, share * 128), shape(share, 128)],
        in_specs=[VMEM] * (2 + len(flat_terms)),
        out_specs=[VMEM, VMEM],
        compiler_params=params(),
        cost_estimate=cost(2.0),
    )(resp_own, keep_own, *flat_terms)
    return g2.reshape(LEVELS, LAGS, share * 128), mean.reshape(share * 128)


def solution(mesh):
    return jax.shard_map(
        body,
        mesh=mesh,
        in_specs=(P(("tm", "pix"), None), P(("tm", "pix")), P(), P(), P(), P(), P(), P()),
        out_specs=(P(None, None, ("pix", "tm")), P(("pix", "tm"))),
        check_vma=False,
    )
```

```python
import functools

import jax
import jax.numpy as jnp
from jax import lax
from jax.experimental import pallas as pl
from jax.experimental.pallas import tpu as pltpu
from jax.sharding import PartitionSpec as P

FRAMES = 1024
LAGS = 16
LEVELS = 4
ROWS = LEVELS * LAGS
EDGE = LAGS + 8 * (LEVELS - 1)
EDGE_SPAN = LAGS << (LEVELS - 1)

PARTS = (("seg", 4), ("seg", 2), ("full", 2))

SMEM = pl.BlockSpec(memory_space=pltpu.SMEM)
VMEM = pl.BlockSpec(memory_space=pltpu.VMEM)
HBM = pl.BlockSpec(memory_space=pl.ANY)
F32 = jnp.float32


def params():
    return pltpu.CompilerParams(vmem_limit_bytes=40 << 20)


def cost(micros):
    return pl.CostEstimate(flops=0, bytes_accessed=int(micros * 3.6e6), transcendentals=0)


def shape(*dims):
    return jax.ShapeDtypeStruct(dims, F32)


def pack_kernel(jobs, owned, share, n_pix, n_tm, where_ref, order_ref, owner_ref, frames_ref, *refs):
    outs, inverse = refs[:-1], refs[-1]
    rows = frames_ref.shape[0]
    pix = where_ref[0]
    for i in range(rows):
        inverse[order_ref[i]] = i

    def eight(position_of, store):
        blocks = [owner_ref[position_of(i)] for i in range(8)]
        for high in range(rows // 8):
            tiles = [
                frames_ref[high * 8 : high * 8 + 8, pl.ds(pl.multiple_of(block * 128, 128), 128)] for block in blocks
            ]
            turned = jnp.swapaxes(jnp.stack(tiles), 0, 1)
            for low in range(8):
                store(inverse[high * 8 + low], turned[low])

    taken = 0
    for kind, start, per, others in jobs:
        if kind == "seg":
            for at, other in enumerate(others):
                out = outs[taken + at]
                base = (pix ^ other) * owned + start

                @pl.loop(0, out.shape[1] // 8)
                def _(group, out=out, base=base, per=per):
                    def position_of(i):
                        pos = group * 8 + i
                        return base + (pos // per) * share + pos % per

                    def store(row, value):
                        out[row, pl.ds(pl.multiple_of(group * 8, 8), 8), :] = value

                    eight(position_of, store)

            taken += len(others)
        else:
            out = outs[taken]
            width = 8 // n_tm
            for owner in range(n_tm):
                base = owner * share + start

                @pl.loop(0, out.shape[1] * out.shape[2])
                def _(at, out=out, owner=owner, base=base, width=width):
                    unit, group = at // out.shape[2], at % out.shape[2]

                    def position_of(i):
                        pos = group * 8 + i
                        return base + (pos // width) * owned + unit * width + pos % width

                    def store(row, value):
                        out[owner, unit, group, row] = value

                    eight(position_of, store)

            taken += 1


def pack_parts(where, raw_frames, frame_order, owner_map, jobs, owned, share, n_pix, n_tm):
    rows = raw_frames.shape[0]
    outs = []
    size = 0
    for kind, _, per, others in jobs:
        if kind == "seg":
            outs += [shape(rows, n_tm * per, 128)] * len(others)
            size += per * len(others) / n_pix
        else:
            width = 8 // n_tm
            outs.append(shape(n_tm, per // width, n_pix * width // 8, rows, 8, 128))
            size += per
    return pl.pallas_call(
        functools.partial(pack_kernel, jobs, owned, share, n_pix, n_tm),
        out_shape=outs,
        in_specs=[SMEM, SMEM, SMEM, VMEM],
        out_specs=[VMEM] * len(outs),
        scratch_shapes=[pltpu.SMEM((rows,), jnp.int32)],
        compiler_params=params(),
        cost_estimate=cost(1.0 + 8.0 * size / share),
    )(where, frame_order, owner_map, raw_frames)


def turn_kernel(n_pix, n_tm, where_ref, held, *refs):
    outs, staged = refs[:n_pix], refs[n_pix]
    units, groups, rows = held.shape[1:4]
    width = 8 // n_tm
    place = lax.broadcasted_iota(jnp.int32, (8, 128), 0) // width

    @pl.loop(0, rows)
    def _(row):
        for unit in range(units):
            for group in range(groups):
                got = [held[m, unit, group, row] for m in range(n_tm)]
                for to in range(n_tm):
                    value = got[to]
                    for m in range(n_tm):
                        if m != to:
                            value = jnp.where(place == m, pltpu.roll(got[m], (m - to) * width % 8, 0), value)
                    staged[group * n_tm + to, row, unit * 8 : unit * 8 + 8, :] = value

    for other in range(n_pix):
        outs[other][...] = staged[where_ref[0] ^ other]


def turn_part(where, held, n_pix, n_tm):
    units, groups, rows = held.shape[1:4]
    return pl.pallas_call(
        functools.partial(turn_kernel, n_pix, n_tm),
        out_shape=[shape(rows, units * 8, 128)] * n_pix,
        in_specs=[SMEM, VMEM],
        out_specs=[VMEM] * n_pix,
        scratch_shapes=[pltpu.VMEM((n_pix, rows, units * 8, 128), F32)],
        compiler_params=params(),
        cost_estimate=cost(3.0),
    )(where, held)


def constants_kernel(
    plan, owned, share, where_ref, owner_ref, dark_ref, flat_ref, pol_ref, solid_ref, mask_ref, dark_out, resp_out, keep_out
):
    base = where_ref[0] * owned
    mine = base + where_ref[1] * share
    for at, (from_mine, shift) in enumerate(plan):
        row = pl.ds(owner_ref[(mine if from_mine else base) + shift], 1)
        dark_out[at : at + 1, :] = dark_ref[row, :]
    for at in range(share):
        row = pl.ds(owner_ref[mine + at], 1)
        resp_out[at : at + 1, :] = flat_ref[row, :] * pol_ref[row, :] * solid_ref[row, :]
        keep_out[at : at + 1, :] = mask_ref[row, :].astype(F32)


def pair_sums(rows):
    return [rows[2 * i] + rows[2 * i + 1] for i in range(len(rows) // 2)]


def edge_kernel(n_pix, where_ref, dark_ref, *refs):
    pieces, (up_ref, down_ref, held, sem) = refs[:n_pix], refs[n_pix:]
    rows = pieces[0].shape[0]
    blocks = EDGE_SPAN // rows
    half = held.shape[2]
    for other in range(n_pix):
        source = where_ref[0] ^ other
        for side, first in ((0, n_pix - blocks), (1, 0)):

            @pl.when((source >= first) & (source < first + blocks))
            def _(other=other, source=source, side=side, first=first):
                pltpu.make_async_copy(
                    pieces[other].at[:, pl.ds(side * half, half), :],
                    held.at[side, pl.ds((source - first) * rows, rows)],
                    sem,
                ).start()

    pltpu.make_async_copy(held, held, sem).wait()

    for side, out_ref in enumerate((up_ref, down_ref)):

        @pl.loop(0, half // 8)
        def _(group, side=side, out_ref=out_ref):
            lanes = pl.ds(pl.multiple_of(group * 8, 8), 8)
            dark = dark_ref[pl.ds(pl.multiple_of(group * 8 + side * half, 8), 8), :]
            span = 0
            for level in range(LEVELS):
                count = LAGS if level == 0 else LAGS // 2
                width = 1 << level
                begin = span if side else EDGE_SPAN - span - count * width
                for i in range(count):
                    at = begin + i * width
                    got = [held[side, at + j, lanes, :] - dark for j in range(width)]
                    while len(got) > 1:
                        got = pair_sums(got)
                    out_ref[group, (LAGS + 8 * (level - 1) if level else 0) + i] = got[0]
                span += count * width


def edge_part(where, pieces, dark):
    n_pix = len(pieces)
    half = pieces[0].shape[1] // 2
    return pl.pallas_call(
        functools.partial(edge_kernel, n_pix),
        out_shape=[shape(half // 8, EDGE, 8, 128)] * 2,
        in_specs=[SMEM, VMEM] + [HBM] * n_pix,
        out_specs=[VMEM, VMEM],
        scratch_shapes=[pltpu.VMEM((2, EDGE_SPAN, half, 128), F32), pltpu.SemaphoreType.DMA],
        compiler_params=params(),
        cost_estimate=cost(2.0),
    )(where, dark, *pieces)


def add_lags(older, newer, sums, cross_only=False):
    both = older + newer
    out = []
    for lag in range(1, LAGS + 1):
        total = sums[lag - 1]
        for i in range(lag if cross_only else LAGS):
            total = total + both[LAGS + i] * both[LAGS + i - lag]
        out.append(total)
    return out


def edge_rows(read, last):
    rows = [read(i) for i in range(LAGS)]
    levels = [rows]
    for level in range(1, LEVELS):
        own = [read(LAGS + 8 * (level - 1) + i) for i in range(8)]
        rows = own + pair_sums(rows) if last else pair_sums(rows) + own
        levels.append(rows)
    return levels


def sums_kernel(kind, n_pix, n_tm, per, where_ref, dark_ref, up_ref, down_ref, *refs):
    pieces, (out, series, up_one, up_two, up_three, flat, totals, sems) = refs[:n_pix], refs[n_pix:]
    rows = pieces[0].shape[0]
    length = rows * n_pix
    groups = series.shape[1] // 8
    for group in range(groups):
        lanes = pl.ds(group * 8, 8)
        for other in range(n_pix):
            pltpu.make_async_copy(
                pieces[other].at[:, lanes, :],
                series.at[pl.ds((where_ref[0] ^ other) * rows, rows), lanes, :],
                sems.at[group],
            ).start()
    zero = jnp.zeros((8, 128), F32)
    stores = (up_one, up_two, up_three, None)
    width = 8 // n_tm
    inner = lax.broadcasted_iota(jnp.int32, (8, 128), 0) < 8 - width

    def one_group(group, mode, halo_ref):
        lanes = pl.ds(pl.multiple_of(group * 8, 8), 8)
        whole = series.at[:, lanes, :]
        pltpu.make_async_copy(whole, whole, sems.at[group]).wait()
        dark = dark_ref[lanes, :]
        if mode != "full":
            halo_group = group if mode == "up" else group - groups // 2
            halo = edge_rows(lambda i: halo_ref[halo_group, i], mode == "up")
        total = zero
        for level in range(LEVELS):
            steps = (length >> level) // LAGS
            store = stores[level]
            source = None if level == 0 else stores[level - 1]

            def read(at, source=source):
                return series[at, lanes, :] - dark if source is None else source[at]

            def step(index, carry, read=read, level=level, store=store):
                older, sums, total = carry
                newer = [read(index * LAGS + i) for i in range(LAGS)]
                pairs = pair_sums(newer)
                if store is not None:
                    for i in range(LAGS // 2):
                        store[index * (LAGS // 2) + i] = pairs[i]
                if level == 0:
                    while len(pairs) > 1:
                        pairs = pair_sums(pairs)
                    total = total + pairs[0]
                return newer, add_lags(older, newer, sums), total

            before = halo[level] if mode == "up" else [zero] * LAGS
            older, sums, total = lax.fori_loop(0, steps, step, (before, [zero] * LAGS, total))
            if mode == "full":
                after_rows = [jnp.where(inner, pltpu.roll(read(i), 8 - width, 0), 0.0) for i in range(LAGS)]
                sums = add_lags(older, after_rows, sums, cross_only=True)
            elif mode == "down":
                sums = add_lags(older, halo[level], sums, cross_only=True)
            for lag in range(LAGS):
                flat[group, pl.ds(level * LAGS + lag, 8, stride=ROWS), :] = sums[lag]
        totals[group] = total

    if kind == "full":
        pl.loop(0, groups)(lambda group: one_group(group, "full", None))
    else:
        pl.loop(0, groups // 2)(lambda group: one_group(group, "up", up_ref))
        pl.loop(groups // 2, groups)(lambda group: one_group(group, "down", down_ref))

    out[:, per * ROWS :, :] = jnp.zeros((out.shape[0], out.shape[1] - per * ROWS, 128), F32)
    for owner in range(out.shape[0]):
        for at in range(per):
            if kind == "seg":
                blocks = [owner * per + at]
            else:
                blocks = [at // width * 8 + m * width + at % width for m in range(n_tm)]
            out[owner, at * ROWS : (at + 1) * ROWS, :] = sum(
                flat[block // 8, block % 8 * ROWS : (block % 8 + 1) * ROWS, :] for block in blocks
            )
            out[owner, per * ROWS + at : per * ROWS + at + 1, :] = sum(
                totals[block // 8, block % 8 : block % 8 + 1, :] for block in blocks
            )


def sum_rows(per):
    return per * ROWS + (per + 7) // 8 * 8


def sums_part(where, pieces, dark, up, down, kind, per, n_tm):
    n_pix = len(pieces)
    rows, count, _ = pieces[0].shape
    length = n_pix * rows
    return pl.pallas_call(
        functools.partial(sums_kernel, kind, n_pix, n_tm, per),
        out_shape=shape(n_tm if kind == "seg" else 1, sum_rows(per), 128),
        in_specs=[SMEM, VMEM, VMEM, VMEM] + [HBM] * n_pix,
        out_specs=VMEM,
        scratch_shapes=[
            pltpu.VMEM((length, count, 128), F32),
            pltpu.VMEM((length // 2, 8, 128), F32),
            pltpu.VMEM((length // 4, 8, 128), F32),
            pltpu.VMEM((length // 8, 8, 128), F32),
            pltpu.VMEM((count // 8, 8 * ROWS, 128), F32),
            pltpu.VMEM((count // 8, 8, 128), F32),
            pltpu.SemaphoreType.DMA((count // 8,)),
        ],
        compiler_params=params(),
        cost_estimate=cost(1.0 + 3.0 * length * count / 2048),
    )(where, dark, up, down, *pieces)


def finish_kernel(parts, resp_ref, keep_ref, *refs):
    sums_refs, (g2_ref, mean_ref) = refs[:-2], refs[-2:]
    row = lax.broadcasted_iota(jnp.int32, (ROWS, 128), 0)
    level, lag = row // LAGS, row % LAGS + 1
    counts = (((FRAMES >> level) - lag) << (2 * level)).astype(F32)
    for (start, per), ref in zip(parts, sums_refs):
        for at in range(per):
            product = jnp.sum(ref[:, at * ROWS : (at + 1) * ROWS, :], axis=0)
            total = jnp.sum(ref[:, per * ROWS + at : per * ROWS + at + 1, :], axis=0)
            block = start + at
            keep = keep_ref[block : block + 1, :]
            mean = total * (1.0 / FRAMES)
            g2_ref[:, block * 128 : (block + 1) * 128] = product / (counts * mean * mean) * keep
            mean_ref[block : block + 1, :] = mean / resp_ref[block : block + 1, :] * keep


def swap(value, axis, other):
    return lax.ppermute(value, axis, [(i, i ^ other) for i in range(lax.axis_size(axis))])


def swap_all(value, axis):
    return lax.all_to_all(value, axis, split_axis=0, concat_axis=0, tiled=True)


def halos(where, pieces, dark, n_tm):
    up, down = edge_part(where, pieces, dark)
    return (
        lax.ppermute(up, "tm", [(i, i + 1) for i in range(n_tm - 1)]),
        lax.ppermute(down, "tm", [(i + 1, i) for i in range(n_tm - 1)]),
    )


def after(value, earlier):
    return lax.optimization_barrier((value, earlier))


def body(raw_frames, frame_order, owner_map, pixel_mask, dark, flat, polarization, solid_angle):
    n_pix = lax.axis_size("pix")
    n_tm = lax.axis_size("tm")
    n_blocks = owner_map.shape[0]
    owned = n_blocks // n_pix
    share = owned // n_tm
    width = 8 // n_tm

    plan = []
    shifts = []
    start = 0
    for kind, eighths in PARTS:
        per = share * eighths // 8
        plan.append((kind, start, per))
        if kind == "seg":
            shifts += [(False, g * share + start + j) for g in range(n_tm) for j in range(per)]
        else:
            shifts += [
                (True, start + unit * width + j) for unit in range(per // width) for _ in range(n_tm) for j in range(width)
            ]
        start += per

    where = jnp.stack([lax.axis_index("pix"), lax.axis_index("tm")]).astype(jnp.int32)
    tables = [t.reshape(n_blocks, 128) for t in (dark, flat, polarization, solid_angle, pixel_mask)]
    dark_own, resp_own, keep_own = pl.pallas_call(
        functools.partial(constants_kernel, shifts, owned, share),
        out_shape=[shape(owned, 128), shape(share, 128), shape(share, 128)],
        in_specs=[SMEM, SMEM] + [VMEM] * 5,
        out_specs=[VMEM] * 3,
        compiler_params=params(),
        cost_estimate=cost(1.0),
    )(where, owner_map, *tables)

    sizes = (owned, share, n_pix, n_tm)
    order = list(range(n_pix - 1, -1, -1))
    packed = [[None] * n_pix for _ in plan]
    token = where
    jobs = [[plan[0] + (order[: n_pix // 2],)], [plan[0] + (order[n_pix // 2 :],)]]
    jobs.append([part + (order,) for part in reversed(plan[1:])])
    for job in jobs:
        outs = list(pack_parts(token, raw_frames, frame_order, owner_map, job, *sizes))
        outs, token = after(outs, token)
        for part in job:
            kind, _, _, others = part
            index = plan.index(part[:3])
            if kind == "seg":
                for k in others:
                    packed[index][k] = outs.pop(0)
            else:
                got = swap_all(outs.pop(0), "tm")
                packed[index] = list(turn_part(where, got, n_pix, n_tm))

    terms = []
    used = 0
    earlier = None
    for index, (kind, start, per) in enumerate(plan):
        mine = packed[index]
        got = [mine[0]] + [None] * (n_pix - 1)
        for k in order[:-1]:
            sent = mine[k]
            if earlier is not None:
                sent, earlier[k] = after(sent, earlier[k])
            got[k] = swap(sent, "pix", k)
        if earlier is not None:
            up, down = halos(where, earlier, earlier_dark, n_tm)
            sums = sums_part(where, earlier, earlier_dark, up, down, "seg", earlier_per, n_tm)
            got, sums = after(got, sums)
            terms.append(swap_all(sums, "tm"))
        count = n_tm * per
        earlier, earlier_dark, earlier_per = got, dark_own[used : used + count], per
        used += count
    terms.append(sums_part(where, got, earlier_dark, earlier_dark, earlier_dark, "full", per, n_tm))

    g2, mean = pl.pallas_call(
        functools.partial(finish_kernel, [(start, per) for _, start, per in plan]),
        out_shape=[shape(ROWS, share * 128), shape(share, 128)],
        in_specs=[VMEM] * (2 + len(terms)),
        out_specs=[VMEM, VMEM],
        compiler_params=params(),
        cost_estimate=cost(2.0),
    )(resp_own, keep_own, *terms)
    return g2.reshape(LEVELS, LAGS, share * 128), mean.reshape(share * 128)


def solution(mesh):
    return jax.shard_map(
        body,
        mesh=mesh,
        in_specs=(P(("tm", "pix"), None), P(("tm", "pix")), P(), P(), P(), P(), P(), P()),
        out_specs=(P(None, None, ("pix", "tm")), P(("pix", "tm"))),
        check_vma=False,
    )
```

```python
import functools

import jax
import jax.numpy as jnp
from jax import lax
from jax.experimental import pallas as pl
from jax.experimental.pallas import tpu as pltpu
from jax.sharding import PartitionSpec as P

FRAMES = 1024
LAGS = 16
LEVELS = 4
ROWS = LEVELS * LAGS
EDGE = LAGS + 8 * (LEVELS - 1)
EDGE_SPAN = LAGS << (LEVELS - 1)

PARTS = (("seg", 4), ("seg", 2), ("full", 2))

SMEM = pl.BlockSpec(memory_space=pltpu.SMEM)
VMEM = pl.BlockSpec(memory_space=pltpu.VMEM)
HBM = pl.BlockSpec(memory_space=pl.ANY)
F32 = jnp.float32


def params():
    return pltpu.CompilerParams(vmem_limit_bytes=40 << 20)


def cost(micros):
    return pl.CostEstimate(flops=0, bytes_accessed=int(micros * 3.6e5), transcendentals=0)


def shape(*dims):
    return jax.ShapeDtypeStruct(dims, F32)


def pack_kernel(jobs, owned, share, n_pix, n_tm, where_ref, order_ref, owner_ref, frames_ref, *refs):
    outs, inverse = refs[:-1], refs[-1]
    rows = frames_ref.shape[0]
    pix, tm = where_ref[0], where_ref[1]
    for i in range(rows):
        inverse[order_ref[i]] = i

    def eight(position_of, store):
        blocks = [owner_ref[position_of(i)] for i in range(8)]
        for high in range(rows // 8):
            tiles = [
                frames_ref[high * 8 : high * 8 + 8, pl.ds(pl.multiple_of(block * 128, 128), 128)] for block in blocks
            ]
            turned = jnp.swapaxes(jnp.stack(tiles), 0, 1)
            for low in range(8):
                store(inverse[high * 8 + low], turned[low])

    taken = 0
    for kind, start, per, others in jobs:
        if kind == "seg":
            for at, other in enumerate(others):
                out = outs[taken + at]
                base = (pix ^ other) * owned + start

                @pl.loop(0, out.shape[1] // 8)
                def _(group, out=out, base=base, per=per):
                    def position_of(i):
                        pos = group * 8 + i
                        return base + (pos // per) * share + pos % per

                    def store(row, value):
                        out[row, pl.ds(pl.multiple_of(group * 8, 8), 8), :] = value

                    eight(position_of, store)

            taken += len(others)
        else:
            width = 8 // n_tm
            for at, other in enumerate(others):
                out = outs[taken + at]
                base = (tm ^ other) * share + start

                @pl.loop(0, out.shape[0] * out.shape[1])
                def _(at, out=out, base=base, width=width):
                    unit, group = at // out.shape[1], at % out.shape[1]

                    def position_of(i):
                        pos = group * 8 + i
                        return base + (pos // width) * owned + unit * width + pos % width

                    def store(row, value):
                        out[unit, group, row] = value

                    eight(position_of, store)

            taken += len(others)


def pack_parts(raw_frames, frame_order, owner_map, where, jobs, owned, share, n_pix, n_tm):
    rows = raw_frames.shape[0]
    outs = []
    size = 0
    for kind, _, per, others in jobs:
        if kind == "seg":
            outs += [shape(rows, n_tm * per, 128)] * len(others)
            size += per * len(others) / n_pix
        else:
            width = 8 // n_tm
            outs += [shape(per // width, n_pix * width // 8, rows, 8, 128)] * len(others)
            size += per
    return pl.pallas_call(
        functools.partial(pack_kernel, jobs, owned, share, n_pix, n_tm),
        out_shape=outs,
        in_specs=[SMEM, SMEM, SMEM, VMEM],
        out_specs=[VMEM] * len(outs),
        scratch_shapes=[pltpu.SMEM((rows,), jnp.int32)],
        compiler_params=params(),
        cost_estimate=cost(1.0 + 8.0 * size / share),
    )(where, frame_order, owner_map, raw_frames)


def turn_kernel(n_pix, n_tm, where_ref, *refs):
    pieces, outs, (held, staged, sem) = refs[:n_tm], refs[n_tm : n_tm + n_pix], refs[n_tm + n_pix :]
    units, groups, rows = pieces[0].shape[:3]
    width = 8 // n_tm
    for other in range(n_tm):
        pltpu.make_async_copy(pieces[other], held.at[where_ref[1] ^ other], sem).start()
    pltpu.make_async_copy(held, held, sem).wait()
    place = lax.broadcasted_iota(jnp.int32, (8, 128), 0) // width

    @pl.loop(0, rows)
    def _(row):
        for unit in range(units):
            for group in range(groups):
                got = [held[m, unit, group, row] for m in range(n_tm)]
                for to in range(n_tm):
                    value = got[to]
                    for m in range(n_tm):
                        if m != to:
                            value = jnp.where(place == m, pltpu.roll(got[m], (m - to) * width % 8, 0), value)
                    staged[group * n_tm + to, row, unit * 8 : unit * 8 + 8, :] = value

    for other in range(n_pix):
        outs[other][...] = staged[where_ref[0] ^ other]


def turn_part(where, pieces, n_pix, n_tm):
    units, groups, rows = pieces[0].shape[:3]
    return pl.pallas_call(
        functools.partial(turn_kernel, n_pix, n_tm),
        out_shape=[shape(rows, units * 8, 128)] * n_pix,
        in_specs=[SMEM] + [HBM] * n_tm,
        out_specs=[VMEM] * n_pix,
        scratch_shapes=[
            pltpu.VMEM((n_tm,) + pieces[0].shape, F32),
            pltpu.VMEM((n_pix, rows, units * 8, 128), F32),
            pltpu.SemaphoreType.DMA,
        ],
        compiler_params=params(),
        cost_estimate=cost(3.0),
    )(where, *pieces)


def constants_kernel(
    plan, owned, share, where_ref, owner_ref, dark_ref, flat_ref, pol_ref, solid_ref, mask_ref, dark_out, resp_out, keep_out
):
    base = where_ref[0] * owned
    mine = base + where_ref[1] * share
    for at, (from_mine, shift) in enumerate(plan):
        row = pl.ds(owner_ref[(mine if from_mine else base) + shift], 1)
        dark_out[at : at + 1, :] = dark_ref[row, :]
    for at in range(share):
        row = pl.ds(owner_ref[mine + at], 1)
        resp_out[at : at + 1, :] = flat_ref[row, :] * pol_ref[row, :] * solid_ref[row, :]
        keep_out[at : at + 1, :] = mask_ref[row, :].astype(F32)


def constants_part(where, owner_map, dark, flat, polarization, solid_angle, pixel_mask, shifts, owned, share):
    n_blocks = owner_map.shape[0]
    tables = [t.reshape(n_blocks, 128) for t in (dark, flat, polarization, solid_angle, pixel_mask)]
    return pl.pallas_call(
        functools.partial(constants_kernel, shifts, owned, share),
        out_shape=[shape(owned, 128), shape(share, 128), shape(share, 128)],
        in_specs=[SMEM, SMEM] + [VMEM] * 5,
        out_specs=[VMEM] * 3,
        compiler_params=params(),
        cost_estimate=cost(1.0),
    )(where, owner_map, *tables)


def pair_sums(rows):
    return [rows[2 * i] + rows[2 * i + 1] for i in range(len(rows) // 2)]


def edge_kernel(n_pix, where_ref, dark_ref, *refs):
    pieces, (up_ref, down_ref, held, sem) = refs[:n_pix], refs[n_pix:]
    rows = pieces[0].shape[0]
    blocks = EDGE_SPAN // rows
    half = held.shape[2]
    for other in range(n_pix):
        source = where_ref[0] ^ other
        for side, first in ((0, n_pix - blocks), (1, 0)):

            @pl.when((source >= first) & (source < first + blocks))
            def _(other=other, source=source, side=side, first=first):
                pltpu.make_async_copy(
                    pieces[other].at[:, pl.ds(side * half, half), :],
                    held.at[side, pl.ds((source - first) * rows, rows)],
                    sem,
                ).start()

    pltpu.make_async_copy(held, held, sem).wait()

    for side, out_ref in enumerate((up_ref, down_ref)):

        @pl.loop(0, half // 8)
        def _(group, side=side, out_ref=out_ref):
            lanes = pl.ds(pl.multiple_of(group * 8, 8), 8)
            dark = dark_ref[pl.ds(pl.multiple_of(group * 8 + side * half, 8), 8), :]
            span = 0
            for level in range(LEVELS):
                count = LAGS if level == 0 else LAGS // 2
                width = 1 << level
                begin = span if side else EDGE_SPAN - span - count * width
                for i in range(count):
                    at = begin + i * width
                    got = [held[side, at + j, lanes, :] - dark for j in range(width)]
                    while len(got) > 1:
                        got = pair_sums(got)
                    out_ref[group, (LAGS + 8 * (level - 1) if level else 0) + i] = got[0]
                span += count * width


def edge_part(where, pieces, dark):
    n_pix = len(pieces)
    half = pieces[0].shape[1] // 2
    return pl.pallas_call(
        functools.partial(edge_kernel, n_pix),
        out_shape=[shape(half // 8, EDGE, 8, 128)] * 2,
        in_specs=[SMEM, VMEM] + [HBM] * n_pix,
        out_specs=[VMEM, VMEM],
        scratch_shapes=[pltpu.VMEM((2, EDGE_SPAN, half, 128), F32), pltpu.SemaphoreType.DMA],
        compiler_params=params(),
        cost_estimate=cost(2.0),
    )(where, dark, *pieces)


def add_lags(older, newer, sums, cross_only=False):
    both = older + newer
    out = []
    for lag in range(1, LAGS + 1):
        total = sums[lag - 1]
        for i in range(lag if cross_only else LAGS):
            total = total + both[LAGS + i] * both[LAGS + i - lag]
        out.append(total)
    return out


def edge_rows(read, last):
    rows = [read(i) for i in range(LAGS)]
    levels = [rows]
    for level in range(1, LEVELS):
        own = [read(LAGS + 8 * (level - 1) + i) for i in range(8)]
        rows = own + pair_sums(rows) if last else pair_sums(rows) + own
        levels.append(rows)
    return levels


def sums_kernel(kind, n_pix, n_tm, per, where_ref, dark_ref, up_ref, down_ref, *refs):
    pieces, (out, series, up_one, up_two, up_three, flat, totals, sems) = refs[:n_pix], refs[n_pix:]
    rows = pieces[0].shape[0]
    length = rows * n_pix
    groups = series.shape[1] // 8
    for group in range(groups):
        lanes = pl.ds(group * 8, 8)
        for other in range(n_pix):
            pltpu.make_async_copy(
                pieces[other].at[:, lanes, :],
                series.at[pl.ds((where_ref[0] ^ other) * rows, rows), lanes, :],
                sems.at[group],
            ).start()
    zero = jnp.zeros((8, 128), F32)
    stores = (up_one, up_two, up_three, None)
    width = 8 // n_tm
    inner = lax.broadcasted_iota(jnp.int32, (8, 128), 0) < 8 - width

    def one_group(group, mode, halo_ref):
        lanes = pl.ds(pl.multiple_of(group * 8, 8), 8)
        whole = series.at[:, lanes, :]
        pltpu.make_async_copy(whole, whole, sems.at[group]).wait()
        dark = dark_ref[lanes, :]
        if mode != "full":
            halo_group = group if mode == "up" else group - groups // 2
            halo = edge_rows(lambda i: halo_ref[halo_group, i], mode == "up")
        total = zero
        for level in range(LEVELS):
            steps = (length >> level) // LAGS
            store = stores[level]
            source = None if level == 0 else stores[level - 1]

            def read(at, source=source):
                return series[at, lanes, :] - dark if source is None else source[at]

            def step(index, carry, read=read, level=level, store=store):
                older, sums, total = carry
                newer = [read(index * LAGS + i) for i in range(LAGS)]
                pairs = pair_sums(newer)
                if store is not None:
                    for i in range(LAGS // 2):
                        store[index * (LAGS // 2) + i] = pairs[i]
                if level == 0:
                    while len(pairs) > 1:
                        pairs = pair_sums(pairs)
                    total = total + pairs[0]
                return newer, add_lags(older, newer, sums), total

            before = halo[level] if mode == "up" else [zero] * LAGS
            older, sums, total = lax.fori_loop(0, steps, step, (before, [zero] * LAGS, total))
            if mode == "full":
                after_rows = [jnp.where(inner, pltpu.roll(read(i), 8 - width, 0), 0.0) for i in range(LAGS)]
                sums = add_lags(older, after_rows, sums, cross_only=True)
            elif mode == "down":
                sums = add_lags(older, halo[level], sums, cross_only=True)
            for lag in range(LAGS):
                flat[group, pl.ds(level * LAGS + lag, 8, stride=ROWS), :] = sums[lag]
        totals[group] = total

    if kind == "full":
        pl.loop(0, groups)(lambda group: one_group(group, "full", None))
    else:
        pl.loop(0, groups // 2)(lambda group: one_group(group, "up", up_ref))
        pl.loop(groups // 2, groups)(lambda group: one_group(group, "down", down_ref))

    out[:, per * ROWS :, :] = jnp.zeros((out.shape[0], out.shape[1] - per * ROWS, 128), F32)
    for owner in range(out.shape[0]):
        for at in range(per):
            if kind == "seg":
                blocks = [owner * per + at]
            else:
                blocks = [at // width * 8 + m * width + at % width for m in range(n_tm)]
            out[owner, at * ROWS : (at + 1) * ROWS, :] = sum(
                flat[block // 8, block % 8 * ROWS : (block % 8 + 1) * ROWS, :] for block in blocks
            )
            out[owner, per * ROWS + at : per * ROWS + at + 1, :] = sum(
                totals[block // 8, block % 8 : block % 8 + 1, :] for block in blocks
            )


def sum_rows(per):
    return per * ROWS + (per + 7) // 8 * 8


def sums_part(where, pieces, dark, up, down, kind, per, n_tm):
    n_pix = len(pieces)
    rows, count, _ = pieces[0].shape
    length = n_pix * rows
    return pl.pallas_call(
        functools.partial(sums_kernel, kind, n_pix, n_tm, per),
        out_shape=shape(n_tm if kind == "seg" else 1, sum_rows(per), 128),
        in_specs=[SMEM, VMEM, VMEM, VMEM] + [HBM] * n_pix,
        out_specs=VMEM,
        scratch_shapes=[
            pltpu.VMEM((length, count, 128), F32),
            pltpu.VMEM((length // 2, 8, 128), F32),
            pltpu.VMEM((length // 4, 8, 128), F32),
            pltpu.VMEM((length // 8, 8, 128), F32),
            pltpu.VMEM((count // 8, 8 * ROWS, 128), F32),
            pltpu.VMEM((count // 8, 8, 128), F32),
            pltpu.SemaphoreType.DMA((count // 8,)),
        ],
        compiler_params=params(),
        cost_estimate=cost(1.0 + 3.0 * length * count / 2048),
    )(where, dark, up, down, *pieces)


def finish_kernel(parts, resp_ref, keep_ref, *refs):
    sums_refs, (g2_ref, mean_ref) = refs[:-2], refs[-2:]
    row = lax.broadcasted_iota(jnp.int32, (ROWS, 128), 0)
    level, lag = row // LAGS, row % LAGS + 1
    counts = (((FRAMES >> level) - lag) << (2 * level)).astype(F32)
    for (start, per), ref in zip(parts, sums_refs):
        for at in range(per):
            product = jnp.sum(ref[:, at * ROWS : (at + 1) * ROWS, :], axis=0)
            total = jnp.sum(ref[:, per * ROWS + at : per * ROWS + at + 1, :], axis=0)
            block = start + at
            keep = keep_ref[block : block + 1, :]
            mean = total * (1.0 / FRAMES)
            g2_ref[:, block * 128 : (block + 1) * 128] = product / (counts * mean * mean) * keep
            mean_ref[block : block + 1, :] = mean / resp_ref[block : block + 1, :] * keep


class Box:
    def __init__(self, value):
        self.value = value


def unbox(got):
    return [got[k].value for k in range(len(got))]


class Slots:
    def __init__(self, axis, count):
        self.axis, self.size = axis, lax.axis_size(axis)
        self.slots = [None] * count
        self.next = 0

    def send(self, value, pairs):
        at = self.next % len(self.slots)
        self.next += 1
        before = self.slots[at]
        if before is not None:
            value, before.value = lax.optimization_barrier((value, before.value))
        box = Box(lax.ppermute(value, self.axis, pairs))
        self.slots[at] = box
        return box

    def swap(self, value, other):
        return self.send(value, [(i, i ^ other) for i in range(self.size)])


class Line:
    def __init__(self, where):
        self.where = where

    def __call__(self, part, *args):
        outs = part(self.where, *args)
        outs, self.where = lax.optimization_barrier((outs, self.where))
        return outs

    def hold(self, value):
        value, self.where = lax.optimization_barrier((value, self.where))
        return value

    def follow(self, box):
        self.where, box.value = lax.optimization_barrier((self.where, box.value))


def scatter(value):
    return lax.psum_scatter(value, "tm", scatter_dimension=0, tiled=True)


def body(raw_frames, frame_order, owner_map, pixel_mask, dark, flat, polarization, solid_angle):
    n_pix = lax.axis_size("pix")
    n_tm = lax.axis_size("tm")
    n_blocks = owner_map.shape[0]
    owned = n_blocks // n_pix
    share = owned // n_tm
    width = 8 // n_tm

    plan = []
    shifts = []
    start = 0
    for kind, eighths in PARTS:
        per = share * eighths // 8
        plan.append((kind, start, per))
        if kind == "seg":
            shifts += [(False, g * share + start + j) for g in range(n_tm) for j in range(per)]
        else:
            shifts += [
                (True, start + unit * width + j) for unit in range(per // width) for _ in range(n_tm) for j in range(width)
            ]
        start += per

    where = jnp.stack([lax.axis_index("pix"), lax.axis_index("tm")]).astype(jnp.int32)
    sizes = (owned, share, n_pix, n_tm)
    pack = functools.partial(pack_parts, raw_frames, frame_order, owner_map)
    (first, second, full) = plan
    stream = Slots("pix", 3)
    cross = Slots("tm", 2)
    line = Line(where)

    far = list(range(n_pix - 1, 1, -1))
    early, late = [1] + far[: n_pix // 4], far[n_pix // 4 :] + [0]
    mine = dict(zip(early, line(pack, [first + (early,)], *sizes)))
    mine.update(zip(late, line(pack, [first + (late,)], *sizes)))
    got_first = {k: stream.swap(mine[k], k) for k in [1] + far}
    line.follow(got_first[1])
    got_first[0] = Box(mine[0])

    others = list(range(n_tm - 1, -1, -1))
    mine = dict(zip(others, line(pack, [full + (others,)], *sizes)))
    got_full = {k: cross.swap(mine[k], k) for k in mine if k}
    got_full[0] = Box(mine[0])
    order = far + [1, 0]
    mine = dict(zip(order, line(pack, [second + (order,)], *sizes)))
    got_second = {k: stream.swap(mine[k], k) for k in far}
    got_second[0] = Box(mine[0])

    dark_own, resp_own, keep_own = line(
        constants_part, owner_map, dark, flat, polarization, solid_angle, pixel_mask, shifts, owned, share
    )
    darks = []
    used = 0
    for _, _, per in plan:
        darks.append(dark_own[used : used + n_tm * per])
        used += n_tm * per

    def halos(got, dark_part):
        up, down = line(edge_part, unbox(got), dark_part)
        upward = [(i, i + 1) for i in range(n_tm - 1)]
        return cross.send(up, upward).value, cross.send(down, [(j, i) for i, j in upward]).value

    def sums(got, dark_part, up, down, kind, per):
        return line(sums_part, unbox(got), dark_part, up, down, kind, per, n_tm)

    up, down = halos(got_first, darks[0])
    turned = line(turn_part, unbox(got_full), n_pix, n_tm)
    line.follow(got_second[far[0]])
    line.follow(got_second[far[1]])
    terms = [scatter(sums(got_first, darks[0], up, down, "seg", first[2]))]
    got_second[1] = stream.swap(line.hold(mine[1]), 1)
    ahead = order[: n_pix - 3]
    got_full = {k: stream.swap(line.hold(turned[k]), k) for k in ahead}
    up, down = halos(got_second, darks[1])
    line.follow(got_full[far[0]])
    line.follow(got_full[far[1]])
    terms.append(scatter(sums(got_second, darks[1], up, down, "seg", second[2])))
    for k in order[n_pix - 3 : -1]:
        got_full[k] = stream.swap(line.hold(turned[k]), k)
    got_full[0] = Box(turned[0])
    terms.append(sums(got_full, darks[2], darks[2], darks[2], "full", full[2]))

    g2, mean = pl.pallas_call(
        functools.partial(finish_kernel, [(start, per) for _, start, per in plan]),
        out_shape=[shape(ROWS, share * 128), shape(share, 128)],
        in_specs=[VMEM] * (2 + len(terms)),
        out_specs=[VMEM, VMEM],
        compiler_params=params(),
        cost_estimate=cost(2.0),
    )(resp_own, keep_own, *terms)
    return g2.reshape(LEVELS, LAGS, share * 128), mean.reshape(share * 128)


def solution(mesh):
    return jax.shard_map(
        body,
        mesh=mesh,
        in_specs=(P(("tm", "pix"), None), P(("tm", "pix")), P(), P(), P(), P(), P(), P()),
        out_specs=(P(None, None, ("pix", "tm")), P(("pix", "tm"))),
        check_vma=False,
    )
```

```python
import functools

import jax
import jax.numpy as jnp
from jax import lax
from jax.experimental import pallas as pl
from jax.experimental.pallas import tpu as pltpu
from jax.sharding import PartitionSpec as P

FRAMES = 1024
LAGS = 16
LEVELS = 4
ROWS = LEVELS * LAGS
EDGE = LAGS + 8 * (LEVELS - 1)
EDGE_SPAN = LAGS << (LEVELS - 1)

PARTS = (("seg", 4), ("seg", 2), ("full", 2))

SMEM = pl.BlockSpec(memory_space=pltpu.SMEM)
VMEM = pl.BlockSpec(memory_space=pltpu.VMEM)
HBM = pl.BlockSpec(memory_space=pl.ANY)
F32 = jnp.float32


def params():
    return pltpu.CompilerParams(vmem_limit_bytes=40 << 20)


def cost(micros):
    return pl.CostEstimate(flops=0, bytes_accessed=int(micros * 3.6e6), transcendentals=0)


def shape(*dims):
    return jax.ShapeDtypeStruct(dims, F32)


def pack_kernel(jobs, owned, share, n_pix, n_tm, where_ref, order_ref, owner_ref, frames_ref, *refs):
    outs, inverse = refs[:-1], refs[-1]
    rows = frames_ref.shape[0]
    pix, tm = where_ref[0], where_ref[1]
    for i in range(rows):
        inverse[order_ref[i]] = i

    def eight(position_of, store):
        blocks = [owner_ref[position_of(i)] for i in range(8)]
        for high in range(rows // 8):
            tiles = [
                frames_ref[high * 8 : high * 8 + 8, pl.ds(pl.multiple_of(block * 128, 128), 128)] for block in blocks
            ]
            turned = jnp.swapaxes(jnp.stack(tiles), 0, 1)
            for low in range(8):
                store(inverse[high * 8 + low], turned[low])

    taken = 0
    for kind, start, per, others in jobs:
        if kind == "seg":
            for at, other in enumerate(others):
                out = outs[taken + at]
                base = (pix ^ other) * owned + start

                @pl.loop(0, out.shape[1] // 8)
                def _(group, out=out, base=base, per=per):
                    def position_of(i):
                        pos = group * 8 + i
                        return base + (pos // per) * share + pos % per

                    def store(row, value):
                        out[row, pl.ds(pl.multiple_of(group * 8, 8), 8), :] = value

                    eight(position_of, store)

            taken += len(others)
        else:
            width = 8 // n_tm
            for at, other in enumerate(others):
                out = outs[taken + at]
                base = (tm ^ other) * share + start

                @pl.loop(0, out.shape[0] * out.shape[1])
                def _(at, out=out, base=base, width=width):
                    unit, group = at // out.shape[1], at % out.shape[1]

                    def position_of(i):
                        pos = group * 8 + i
                        return base + (pos // width) * owned + unit * width + pos % width

                    def store(row, value):
                        out[unit, group, row] = value

                    eight(position_of, store)

            taken += len(others)


def pack_parts(raw_frames, frame_order, owner_map, where, jobs, owned, share, n_pix, n_tm):
    rows = raw_frames.shape[0]
    outs = []
    size = 0
    for kind, _, per, others in jobs:
        if kind == "seg":
            outs += [shape(rows, n_tm * per, 128)] * len(others)
            size += per * len(others) / n_pix
        else:
            width = 8 // n_tm
            outs += [shape(per // width, n_pix * width // 8, rows, 8, 128)] * len(others)
            size += per
    return pl.pallas_call(
        functools.partial(pack_kernel, jobs, owned, share, n_pix, n_tm),
        out_shape=outs,
        in_specs=[SMEM, SMEM, SMEM, VMEM],
        out_specs=[VMEM] * len(outs),
        scratch_shapes=[pltpu.SMEM((rows,), jnp.int32)],
        compiler_params=params(),
        cost_estimate=cost(1.0 + 8.0 * size / share),
    )(where, frame_order, owner_map, raw_frames)


def turn_kernel(n_pix, n_tm, where_ref, *refs):
    pieces, outs, (held, staged, sem) = refs[:n_tm], refs[n_tm : n_tm + n_pix], refs[n_tm + n_pix :]
    units, groups, rows = pieces[0].shape[:3]
    width = 8 // n_tm
    for other in range(n_tm):
        pltpu.make_async_copy(pieces[other], held.at[where_ref[1] ^ other], sem).start()
    pltpu.make_async_copy(held, held, sem).wait()
    place = lax.broadcasted_iota(jnp.int32, (8, 128), 0) // width

    @pl.loop(0, rows)
    def _(row):
        for unit in range(units):
            for group in range(groups):
                got = [held[m, unit, group, row] for m in range(n_tm)]
                for to in range(n_tm):
                    value = got[to]
                    for m in range(n_tm):
                        if m != to:
                            value = jnp.where(place == m, pltpu.roll(got[m], (m - to) * width % 8, 0), value)
                    staged[group * n_tm + to, row, unit * 8 : unit * 8 + 8, :] = value

    for other in range(n_pix):
        outs[other][...] = staged[where_ref[0] ^ other]


def turn_part(where, pieces, n_pix, n_tm):
    units, groups, rows = pieces[0].shape[:3]
    return pl.pallas_call(
        functools.partial(turn_kernel, n_pix, n_tm),
        out_shape=[shape(rows, units * 8, 128)] * n_pix,
        in_specs=[SMEM] + [HBM] * n_tm,
        out_specs=[VMEM] * n_pix,
        scratch_shapes=[
            pltpu.VMEM((n_tm,) + pieces[0].shape, F32),
            pltpu.VMEM((n_pix, rows, units * 8, 128), F32),
            pltpu.SemaphoreType.DMA,
        ],
        compiler_params=params(),
        cost_estimate=cost(3.0),
    )(where, *pieces)


def constants_kernel(
    plan, owned, share, where_ref, owner_ref, dark_ref, flat_ref, pol_ref, solid_ref, mask_ref, dark_out, resp_out, keep_out
):
    base = where_ref[0] * owned
    mine = base + where_ref[1] * share
    for at, (from_mine, shift) in enumerate(plan):
        row = pl.ds(owner_ref[(mine if from_mine else base) + shift], 1)
        dark_out[at : at + 1, :] = dark_ref[row, :]
    for at in range(share):
        row = pl.ds(owner_ref[mine + at], 1)
        resp_out[at : at + 1, :] = flat_ref[row, :] * pol_ref[row, :] * solid_ref[row, :]
        keep_out[at : at + 1, :] = mask_ref[row, :].astype(F32)


def constants_part(where, owner_map, dark, flat, polarization, solid_angle, pixel_mask, shifts, owned, share):
    n_blocks = owner_map.shape[0]
    tables = [t.reshape(n_blocks, 128) for t in (dark, flat, polarization, solid_angle, pixel_mask)]
    return pl.pallas_call(
        functools.partial(constants_kernel, shifts, owned, share),
        out_shape=[shape(owned, 128), shape(share, 128), shape(share, 128)],
        in_specs=[SMEM, SMEM] + [VMEM] * 5,
        out_specs=[VMEM] * 3,
        compiler_params=params(),
        cost_estimate=cost(1.0),
    )(where, owner_map, *tables)


def pair_sums(rows):
    return [rows[2 * i] + rows[2 * i + 1] for i in range(len(rows) // 2)]


def edge_kernel(n_pix, where_ref, dark_ref, *refs):
    pieces, (up_ref, down_ref, held, sem) = refs[:n_pix], refs[n_pix:]
    rows = pieces[0].shape[0]
    blocks = EDGE_SPAN // rows
    half = held.shape[2]
    for other in range(n_pix):
        source = where_ref[0] ^ other
        for side, first in ((0, n_pix - blocks), (1, 0)):

            @pl.when((source >= first) & (source < first + blocks))
            def _(other=other, source=source, side=side, first=first):
                pltpu.make_async_copy(
                    pieces[other].at[:, pl.ds(side * half, half), :],
                    held.at[side, pl.ds((source - first) * rows, rows)],
                    sem,
                ).start()

    pltpu.make_async_copy(held, held, sem).wait()

    for side, out_ref in enumerate((up_ref, down_ref)):

        @pl.loop(0, half // 8)
        def _(group, side=side, out_ref=out_ref):
            lanes = pl.ds(pl.multiple_of(group * 8, 8), 8)
            dark = dark_ref[pl.ds(pl.multiple_of(group * 8 + side * half, 8), 8), :]
            span = 0
            for level in range(LEVELS):
                count = LAGS if level == 0 else LAGS // 2
                width = 1 << level
                begin = span if side else EDGE_SPAN - span - count * width
                for i in range(count):
                    at = begin + i * width
                    got = [held[side, at + j, lanes, :] - dark for j in range(width)]
                    while len(got) > 1:
                        got = pair_sums(got)
                    out_ref[group, (LAGS + 8 * (level - 1) if level else 0) + i] = got[0]
                span += count * width


def edge_part(where, pieces, dark):
    n_pix = len(pieces)
    half = pieces[0].shape[1] // 2
    return pl.pallas_call(
        functools.partial(edge_kernel, n_pix),
        out_shape=[shape(half // 8, EDGE, 8, 128)] * 2,
        in_specs=[SMEM, VMEM] + [HBM] * n_pix,
        out_specs=[VMEM, VMEM],
        scratch_shapes=[pltpu.VMEM((2, EDGE_SPAN, half, 128), F32), pltpu.SemaphoreType.DMA],
        compiler_params=params(),
        cost_estimate=cost(2.0),
    )(where, dark, *pieces)


def add_lags(older, newer, sums, cross_only=False):
    both = older + newer
    out = []
    for lag in range(1, LAGS + 1):
        total = sums[lag - 1]
        for i in range(lag if cross_only else LAGS):
            total = total + both[LAGS + i] * both[LAGS + i - lag]
        out.append(total)
    return out


def edge_rows(read, last):
    rows = [read(i) for i in range(LAGS)]
    levels = [rows]
    for level in range(1, LEVELS):
        own = [read(LAGS + 8 * (level - 1) + i) for i in range(8)]
        rows = own + pair_sums(rows) if last else pair_sums(rows) + own
        levels.append(rows)
    return levels


def sums_kernel(kind, n_pix, n_tm, per, where_ref, dark_ref, up_ref, down_ref, *refs):
    pieces, rest = refs[:n_pix], refs[n_pix:]
    outs, (series, up_one, up_two, up_three, flat, totals, sems) = rest[:-7], rest[-7:]
    rows = pieces[0].shape[0]
    length = rows * n_pix
    groups = series.shape[1] // 8
    for group in range(groups):
        lanes = pl.ds(group * 8, 8)
        for other in range(n_pix):
            pltpu.make_async_copy(
                pieces[other].at[:, lanes, :],
                series.at[pl.ds((where_ref[0] ^ other) * rows, rows), lanes, :],
                sems.at[group],
            ).start()
    zero = jnp.zeros((8, 128), F32)
    stores = (up_one, up_two, up_three, None)
    width = 8 // n_tm
    inner = lax.broadcasted_iota(jnp.int32, (8, 128), 0) < 8 - width

    def one_group(group, mode, halo_ref):
        lanes = pl.ds(pl.multiple_of(group * 8, 8), 8)
        whole = series.at[:, lanes, :]
        pltpu.make_async_copy(whole, whole, sems.at[group]).wait()
        dark = dark_ref[lanes, :]
        if mode != "full":
            halo_group = group if mode == "up" else group - groups // 2
            halo = edge_rows(lambda i: halo_ref[halo_group, i], mode == "up")
        total = zero
        for level in range(LEVELS):
            steps = (length >> level) // LAGS
            store = stores[level]
            source = None if level == 0 else stores[level - 1]

            def read(at, source=source):
                return series[at, lanes, :] - dark if source is None else source[at]

            def step(index, carry, read=read, level=level, store=store):
                older, sums, total = carry
                newer = [read(index * LAGS + i) for i in range(LAGS)]
                pairs = pair_sums(newer)
                if store is not None:
                    for i in range(LAGS // 2):
                        store[index * (LAGS // 2) + i] = pairs[i]
                if level == 0:
                    while len(pairs) > 1:
                        pairs = pair_sums(pairs)
                    total = total + pairs[0]
                return newer, add_lags(older, newer, sums), total

            before = halo[level] if mode == "up" else [zero] * LAGS
            older, sums, total = lax.fori_loop(0, steps, step, (before, [zero] * LAGS, total))
            if mode == "full":
                after_rows = [jnp.where(inner, pltpu.roll(read(i), 8 - width, 0), 0.0) for i in range(LAGS)]
                sums = add_lags(older, after_rows, sums, cross_only=True)
            elif mode == "down":
                sums = add_lags(older, halo[level], sums, cross_only=True)
            for lag in range(LAGS):
                flat[group, pl.ds(level * LAGS + lag, 8, stride=ROWS), :] = sums[lag]
        totals[group] = total

    if kind == "full":
        pl.loop(0, groups)(lambda group: one_group(group, "full", None))
    else:
        pl.loop(0, groups // 2)(lambda group: one_group(group, "up", up_ref))
        pl.loop(groups // 2, groups)(lambda group: one_group(group, "down", down_ref))

    def put(out, owner, at, blocks):
        out[owner, at * ROWS : (at + 1) * ROWS, :] = sum(
            flat[block // 8, pl.ds(pl.multiple_of(block % 8 * ROWS, ROWS), ROWS), :] for block in blocks
        )
        out[owner, per * ROWS + at : per * ROWS + at + 1, :] = sum(
            totals[block // 8, pl.ds(block % 8, 1), :] for block in blocks
        )

    for side, out in enumerate(outs):
        out[:, per * ROWS :, :] = jnp.zeros((out.shape[0], out.shape[1] - per * ROWS, 128), F32)
        for owner in range(out.shape[0]):
            for at in range(per):
                if kind == "seg":
                    put(out, owner, at, [(2 * owner + ((where_ref[1] & 1) ^ side)) * per + at])
                else:
                    put(out, owner, at, [at // width * 8 + m * width + at % width for m in range(n_tm)])


def sum_rows(per):
    return per * ROWS + (per + 7) // 8 * 8


def sums_part(where, pieces, dark, up, down, kind, per, n_tm):
    n_pix = len(pieces)
    rows, count, _ = pieces[0].shape
    length = n_pix * rows
    return pl.pallas_call(
        functools.partial(sums_kernel, kind, n_pix, n_tm, per),
        out_shape=[shape(n_tm // 2, sum_rows(per), 128)] * 2 if kind == "seg" else [shape(1, sum_rows(per), 128)],
        in_specs=[SMEM, VMEM, VMEM, VMEM] + [HBM] * n_pix,
        out_specs=[VMEM] * (2 if kind == "seg" else 1),
        scratch_shapes=[
            pltpu.VMEM((length, count, 128), F32),
            pltpu.VMEM((length // 2, 8, 128), F32),
            pltpu.VMEM((length // 4, 8, 128), F32),
            pltpu.VMEM((length // 8, 8, 128), F32),
            pltpu.VMEM((count // 8, 8 * ROWS, 128), F32),
            pltpu.VMEM((count // 8, 8, 128), F32),
            pltpu.SemaphoreType.DMA((count // 8,)),
        ],
        compiler_params=params(),
        cost_estimate=cost(1.0 + 3.0 * length * count / 2048),
    )(where, dark, up, down, *pieces)


def add_kernel(step, where_ref, mine_ref, got_ref, keep_ref, send_ref):
    side = (where_ref[1] >> step) & 1
    for owner in range(keep_ref.shape[0]):
        for out, at in ((keep_ref, 2 * owner + side), (send_ref, 2 * owner + (side ^ 1))):
            out[owner] = mine_ref[at] + got_ref[at]


def add_part(where, mine, got, step):
    half = shape(mine.shape[0] // 2, *mine.shape[1:])
    return pl.pallas_call(
        functools.partial(add_kernel, step),
        out_shape=[half, half],
        in_specs=[SMEM, VMEM, VMEM],
        out_specs=[VMEM, VMEM],
        compiler_params=params(),
        cost_estimate=cost(0.5),
    )(where, mine, got)


def finish_kernel(parts, resp_ref, keep_ref, *refs):
    sums_refs, (g2_ref, mean_ref) = refs[:-2], refs[-2:]
    row = lax.broadcasted_iota(jnp.int32, (ROWS, 128), 0)
    level, lag = row // LAGS, row % LAGS + 1
    counts = (((FRAMES >> level) - lag) << (2 * level)).astype(F32)
    for start, per, terms in parts:
        mine, sums_refs = sums_refs[:terms], sums_refs[terms:]
        for at in range(per):
            product = sum(ref[0, at * ROWS : (at + 1) * ROWS, :] for ref in mine)
            total = sum(ref[0, per * ROWS + at : per * ROWS + at + 1, :] for ref in mine)
            block = start + at
            keep = keep_ref[block : block + 1, :]
            mean = total * (1.0 / FRAMES)
            g2_ref[:, block * 128 : (block + 1) * 128] = product / (counts * mean * mean) * keep
            mean_ref[block : block + 1, :] = mean / resp_ref[block : block + 1, :] * keep


class Box:
    def __init__(self, value):
        self.value = value


def unbox(got):
    return [got[k].value for k in range(len(got))]


def send(value, axis, pairs, *before):
    for box in before:
        value, box.value = lax.optimization_barrier((value, box.value))
    return Box(lax.ppermute(value, axis, pairs))


def swap(value, axis, other, *before):
    return send(value, axis, [(i, i ^ other) for i in range(lax.axis_size(axis))], *before)


class Line:
    def __init__(self, where):
        self.where = where

    def __call__(self, part, *args):
        outs = part(self.where, *args)
        outs, self.where = lax.optimization_barrier((outs, self.where))
        return outs

    def hold(self, value):
        value, self.where = lax.optimization_barrier((value, self.where))
        return value

    def follow(self, box):
        self.where, box.value = lax.optimization_barrier((self.where, box.value))


def body(raw_frames, frame_order, owner_map, pixel_mask, dark, flat, polarization, solid_angle):
    n_pix = lax.axis_size("pix")
    n_tm = lax.axis_size("tm")
    n_blocks = owner_map.shape[0]
    owned = n_blocks // n_pix
    share = owned // n_tm
    width = 8 // n_tm

    plan = []
    shifts = []
    start = 0
    for kind, eighths in PARTS:
        per = share * eighths // 8
        plan.append((kind, start, per))
        if kind == "seg":
            shifts += [(False, g * share + start + j) for g in range(n_tm) for j in range(per)]
        else:
            shifts += [
                (True, start + unit * width + j) for unit in range(per // width) for _ in range(n_tm) for j in range(width)
            ]
        start += per

    where = jnp.stack([lax.axis_index("pix"), lax.axis_index("tm")]).astype(jnp.int32)
    sizes = (owned, share, n_pix, n_tm)
    pack = functools.partial(pack_parts, raw_frames, frame_order, owner_map)
    (first, second, full) = plan
    line = Line(where)

    far = list(range(n_pix - 1, 1, -1))
    if n_pix == 8:
        far = [7, 6, 5, 3, 4, 2]
    order = far + [1, 0]
    early, late = [1] + far[:2], far[2:] + [0]
    chain = [k for k in range(2, n_tm)]
    others = chain + [1, 0]

    mine = dict(zip(early, line(pack, [first + (early,)], *sizes)))
    got_first = {k: swap(mine[k], "pix", k) for k in early}
    line.follow(got_first[1])
    packed = line(pack, [first + (late,), full + (others,)], *sizes)
    mine.update(zip(late, packed))
    got_first[0] = Box(mine[0])
    raw = dict(zip(others, packed[len(late) :]))
    got_full = {0: Box(raw[0]), 1: swap(raw[1], "tm", 1)}
    for at, k in enumerate(chain):
        got_full[k] = swap(raw[k], "tm", k, *[got_full[j] for j in chain[:at][-1:]])
    for at in range(2, len(far), 2):
        before = [got_first[j] for j in far[at - 2 : at]]
        if at == 2:
            before += [got_full[1], got_full[chain[0]]]
        for k in far[at : at + 2]:
            got_first[k] = swap(mine[k], "pix", k, *before)

    mine = dict(zip(order, line(pack, [second + (order,)], *sizes)))
    got_second = {0: Box(mine[0])}
    for k in far[:2]:
        got_second[k] = swap(mine[k], "pix", k, *[got_first[j] for j in far[-2:]])

    dark_own, resp_own, keep_own = line(
        constants_part, owner_map, dark, flat, polarization, solid_angle, pixel_mask, shifts, owned, share
    )
    darks = []
    used = 0
    for _, _, per in plan:
        darks.append(dark_own[used : used + n_tm * per])
        used += n_tm * per

    def halos(got, dark_part):
        up, down = line(edge_part, unbox(got), dark_part)
        upward = [(i, i + 1) for i in range(n_tm - 1)]
        return send(up, "tm", upward), send(down, "tm", [(j, i) for i, j in upward])

    def sums(got, dark_part, halo, kind, per):
        up, down = [h.value for h in halo]
        return line(sums_part, unbox(got), dark_part, up, down, kind, per, n_tm)

    halo = halos(got_first, darks[0])
    ahead = [got_second[k] for k in far[:2]]
    for box in ahead:
        line.follow(box)
    for k in far[2:] + [1]:
        got_second[k] = swap(mine[k], "pix", k, *ahead)
    keep, away = sums(got_first, darks[0], halo, "seg", first[2])
    terms = [[keep, swap(away, "tm", 1)], None, None]

    turned = line(turn_part, unbox(got_full), n_pix, n_tm)
    got_full = {0: Box(turned[0])}
    for k in far[:2]:
        got_full[k] = swap(line.hold(turned[k]), "pix", k, *[got_second[j] for j in far[2:]])
    halo = halos(got_second, darks[1])
    for at in range(2, len(far), 2):
        for k in far[at : at + 2] + [1] * (at == len(far) - 2):
            got_full[k] = swap(turned[k], "pix", k, *[got_full[j] for j in far[at - 2 : at]])
    keep, away = sums(got_second, darks[1], halo, "seg", second[2])
    terms[1] = [keep, swap(away, "tm", 1)]

    for step in range(1, n_tm.bit_length() - 1):
        for part in range(2):
            keep, box = terms[part]
            keep, away = line(add_part, keep, box.value, step)
            terms[part] = [keep, swap(away, "tm", 1 << step)]
    terms = [[keep, box.value] for keep, box in terms[:2]]
    no_halo = [Box(darks[2])] * 2
    terms.append(sums(got_full, darks[2], no_halo, "full", full[2]))

    g2, mean = pl.pallas_call(
        functools.partial(
            finish_kernel, [(start, per, len(part)) for (_, start, per), part in zip(plan, terms)]
        ),
        out_shape=[shape(ROWS, share * 128), shape(share, 128)],
        in_specs=[VMEM] * (2 + sum(len(part) for part in terms)),
        out_specs=[VMEM, VMEM],
        compiler_params=params(),
        cost_estimate=cost(1.0),
    )(resp_own, keep_own, *[value for part in terms for value in part])
    return g2.reshape(LEVELS, LAGS, share * 128), mean.reshape(share * 128)


def solution(mesh):
    return jax.shard_map(
        body,
        mesh=mesh,
        in_specs=(P(("tm", "pix"), None), P(("tm", "pix")), P(), P(), P(), P(), P(), P()),
        out_specs=(P(None, None, ("pix", "tm")), P(("pix", "tm"))),
        check_vma=False,
    )
```

```python
import functools

import jax
import jax.numpy as jnp
from jax import lax
from jax.experimental import pallas as pl
from jax.experimental.pallas import tpu as pltpu
from jax.sharding import PartitionSpec as P

FRAMES = 1024
LAGS = 16
LEVELS = 4
ROWS = LEVELS * LAGS
EDGE = LAGS + 8 * (LEVELS - 1)
EDGE_SPAN = LAGS << (LEVELS - 1)

PARTS = (("seg", 4), ("seg", 2), ("full", 2))

SMEM = pl.BlockSpec(memory_space=pltpu.SMEM)
VMEM = pl.BlockSpec(memory_space=pltpu.VMEM)
HBM = pl.BlockSpec(memory_space=pl.ANY)
F32 = jnp.float32


def params():
    return pltpu.CompilerParams(vmem_limit_bytes=40 << 20)


def cost(micros):
    return pl.CostEstimate(flops=0, bytes_accessed=int(micros * 3.6e6), transcendentals=0)


def shape(*dims):
    return jax.ShapeDtypeStruct(dims, F32)


def pack_kernel(jobs, owned, share, n_pix, n_tm, where_ref, order_ref, owner_ref, frames_ref, *refs):
    outs, inverse = refs[:-1], refs[-1]
    rows = frames_ref.shape[0]
    pix, tm = where_ref[0], where_ref[1]
    for i in range(rows):
        inverse[order_ref[i]] = i

    def eight(position_of, store):
        blocks = [owner_ref[position_of(i)] for i in range(8)]
        for high in range(rows // 8):
            tiles = [
                frames_ref[high * 8 : high * 8 + 8, pl.ds(pl.multiple_of(block * 128, 128), 128)] for block in blocks
            ]
            turned = jnp.swapaxes(jnp.stack(tiles), 0, 1)
            for low in range(8):
                store(inverse[high * 8 + low], turned[low])

    taken = 0
    for kind, start, per, others in jobs:
        if kind == "seg":
            for at, other in enumerate(others):
                out = outs[taken + at]
                base = (pix ^ other) * owned + start

                @pl.loop(0, out.shape[1] // 8)
                def _(group, out=out, base=base, per=per):
                    def position_of(i):
                        pos = group * 8 + i
                        return base + (pos // per) * share + pos % per

                    def store(row, value):
                        out[row, pl.ds(pl.multiple_of(group * 8, 8), 8), :] = value

                    eight(position_of, store)

            taken += len(others)
        else:
            width = 8 // n_tm
            for at, other in enumerate(others):
                out = outs[taken + at]
                base = (tm ^ other) * share + start

                @pl.loop(0, out.shape[0] * out.shape[1])
                def _(at, out=out, base=base, width=width):
                    unit, group = at // out.shape[1], at % out.shape[1]

                    def position_of(i):
                        pos = group * 8 + i
                        return base + (pos // width) * owned + unit * width + pos % width

                    def store(row, value):
                        out[unit, group, row] = value

                    eight(position_of, store)

            taken += len(others)


def pack_parts(raw_frames, frame_order, owner_map, where, jobs, owned, share, n_pix, n_tm):
    rows = raw_frames.shape[0]
    outs = []
    size = 0
    for kind, _, per, others in jobs:
        if kind == "seg":
            outs += [shape(rows, n_tm * per, 128)] * len(others)
            size += per * len(others) / n_pix
        else:
            width = 8 // n_tm
            outs += [shape(per // width, n_pix * width // 8, rows, 8, 128)] * len(others)
            size += per
    return pl.pallas_call(
        functools.partial(pack_kernel, jobs, owned, share, n_pix, n_tm),
        out_shape=outs,
        in_specs=[SMEM, SMEM, SMEM, VMEM],
        out_specs=[VMEM] * len(outs),
        scratch_shapes=[pltpu.SMEM((rows,), jnp.int32)],
        compiler_params=params(),
        cost_estimate=cost(1.0 + 8.0 * size / share),
    )(where, frame_order, owner_map, raw_frames)


def turn_kernel(n_pix, n_tm, where_ref, *refs):
    pieces, outs, (held, staged, sem) = refs[:n_tm], refs[n_tm : n_tm + n_pix], refs[n_tm + n_pix :]
    units, groups, rows = pieces[0].shape[:3]
    width = 8 // n_tm
    for other in range(n_tm):
        pltpu.make_async_copy(pieces[other], held.at[where_ref[1] ^ other], sem).start()
    pltpu.make_async_copy(held, held, sem).wait()
    place = lax.broadcasted_iota(jnp.int32, (8, 128), 0) // width

    @pl.loop(0, rows)
    def _(row):
        for unit in range(units):
            for group in range(groups):
                got = [held[m, unit, group, row] for m in range(n_tm)]
                for to in range(n_tm):
                    value = got[to]
                    for m in range(n_tm):
                        if m != to:
                            value = jnp.where(place == m, pltpu.roll(got[m], (m - to) * width % 8, 0), value)
                    staged[group * n_tm + to, row, unit * 8 : unit * 8 + 8, :] = value

    for other in range(n_pix):
        outs[other][...] = staged[where_ref[0] ^ other]


def turn_part(where, pieces, n_pix, n_tm):
    units, groups, rows = pieces[0].shape[:3]
    return pl.pallas_call(
        functools.partial(turn_kernel, n_pix, n_tm),
        out_shape=[shape(rows, units * 8, 128)] * n_pix,
        in_specs=[SMEM] + [HBM] * n_tm,
        out_specs=[VMEM] * n_pix,
        scratch_shapes=[
            pltpu.VMEM((n_tm,) + pieces[0].shape, F32),
            pltpu.VMEM((n_pix, rows, units * 8, 128), F32),
            pltpu.SemaphoreType.DMA,
        ],
        compiler_params=params(),
        cost_estimate=cost(3.0),
    )(where, *pieces)


def constants_kernel(
    plan, owned, share, where_ref, owner_ref, dark_ref, flat_ref, pol_ref, solid_ref, mask_ref, dark_out, resp_out, keep_out
):
    base = where_ref[0] * owned
    mine = base + where_ref[1] * share
    for at, (from_mine, shift) in enumerate(plan):
        row = pl.ds(owner_ref[(mine if from_mine else base) + shift], 1)
        dark_out[at : at + 1, :] = dark_ref[row, :]
    for at in range(share):
        row = pl.ds(owner_ref[mine + at], 1)
        resp_out[at : at + 1, :] = flat_ref[row, :] * pol_ref[row, :] * solid_ref[row, :]
        keep_out[at : at + 1, :] = mask_ref[row, :].astype(F32)


def constants_part(where, owner_map, dark, flat, polarization, solid_angle, pixel_mask, shifts, owned, share):
    n_blocks = owner_map.shape[0]
    tables = [t.reshape(n_blocks, 128) for t in (dark, flat, polarization, solid_angle, pixel_mask)]
    return pl.pallas_call(
        functools.partial(constants_kernel, shifts, owned, share),
        out_shape=[shape(owned, 128), shape(share, 128), shape(share, 128)],
        in_specs=[SMEM, SMEM] + [VMEM] * 5,
        out_specs=[VMEM] * 3,
        compiler_params=params(),
        cost_estimate=cost(1.0),
    )(where, owner_map, *tables)


def pair_sums(rows):
    return [rows[2 * i] + rows[2 * i + 1] for i in range(len(rows) // 2)]


def edge_kernel(n_pix, where_ref, dark_ref, *refs):
    pieces, outs, (held, sem) = refs[:n_pix], refs[n_pix:-2], refs[-2:]
    rows = pieces[0].shape[0]
    blocks = EDGE_SPAN // rows
    half = held.shape[2]
    for other in range(n_pix):
        source = where_ref[0] ^ other
        for side, first in ((0, n_pix - blocks), (1, 0))[: len(outs)]:

            @pl.when((source >= first) & (source < first + blocks))
            def _(other=other, source=source, side=side, first=first):
                pltpu.make_async_copy(
                    pieces[other].at[:, pl.ds(side * half, half), :],
                    held.at[side, pl.ds((source - first) * rows, rows)],
                    sem,
                ).start()

    pltpu.make_async_copy(held, held, sem).wait()

    for side, out_ref in enumerate(outs):

        @pl.loop(0, half // 8)
        def _(group, side=side, out_ref=out_ref):
            lanes = pl.ds(pl.multiple_of(group * 8, 8), 8)
            dark = dark_ref[pl.ds(pl.multiple_of(group * 8 + side * half, 8), 8), :]
            span = 0
            for level in range(LEVELS):
                count = LAGS if level == 0 else LAGS // 2
                width = 1 << level
                begin = span if side else EDGE_SPAN - span - count * width
                for i in range(count):
                    at = begin + i * width
                    got = [held[side, at + j, lanes, :] - dark for j in range(width)]
                    while len(got) > 1:
                        got = pair_sums(got)
                    out_ref[group, (LAGS + 8 * (level - 1) if level else 0) + i] = got[0]
                span += count * width


def edge_part(where, pieces, dark, sides):
    n_pix = len(pieces)
    half = pieces[0].shape[1] // sides
    return pl.pallas_call(
        functools.partial(edge_kernel, n_pix),
        out_shape=[shape(half // 8, EDGE, 8, 128)] * sides,
        in_specs=[SMEM, VMEM] + [HBM] * n_pix,
        out_specs=[VMEM] * sides,
        scratch_shapes=[pltpu.VMEM((sides, EDGE_SPAN, half, 128), F32), pltpu.SemaphoreType.DMA],
        compiler_params=params(),
        cost_estimate=cost(2.0),
    )(where, dark, *pieces)


def add_lags(older, newer, sums, cross_only=False):
    both = older + newer
    out = []
    for lag in range(1, LAGS + 1):
        total = sums[lag - 1]
        for i in range(lag if cross_only else LAGS):
            total = total + both[LAGS + i] * both[LAGS + i - lag]
        out.append(total)
    return out


def edge_rows(read, last):
    rows = [read(i) for i in range(LAGS)]
    levels = [rows]
    for level in range(1, LEVELS):
        own = [read(LAGS + 8 * (level - 1) + i) for i in range(8)]
        rows = own + pair_sums(rows) if last else pair_sums(rows) + own
        levels.append(rows)
    return levels


def sums_kernel(kind, sides, n_pix, n_tm, per, where_ref, dark_ref, *refs):
    halos, pieces, rest = refs[:sides], refs[sides : sides + n_pix], refs[sides + n_pix :]
    outs, (series, up_one, up_two, up_three, flat, totals, sems) = rest[:-7], rest[-7:]
    rows = pieces[0].shape[0]
    length = rows * n_pix
    groups = series.shape[1] // 8
    for group in range(groups):
        lanes = pl.ds(group * 8, 8)
        for other in range(n_pix):
            pltpu.make_async_copy(
                pieces[other].at[:, lanes, :],
                series.at[pl.ds((where_ref[0] ^ other) * rows, rows), lanes, :],
                sems.at[group],
            ).start()
    zero = jnp.zeros((8, 128), F32)
    stores = (up_one, up_two, up_three, None)
    width = 8 // n_tm
    inner = lax.broadcasted_iota(jnp.int32, (8, 128), 0) < 8 - width

    def one_group(group, mode, halo_ref):
        lanes = pl.ds(pl.multiple_of(group * 8, 8), 8)
        whole = series.at[:, lanes, :]
        pltpu.make_async_copy(whole, whole, sems.at[group]).wait()
        dark = dark_ref[lanes, :]
        if mode != "full":
            halo_group = group if mode == "up" else group - groups // sides
            halo = edge_rows(lambda i: halo_ref[halo_group, i], mode == "up")
        total = zero
        for level in range(LEVELS):
            steps = (length >> level) // LAGS
            store = stores[level]
            source = None if level == 0 else stores[level - 1]

            def read(at, source=source):
                return series[at, lanes, :] - dark if source is None else source[at]

            def step(index, carry, read=read, level=level, store=store):
                older, sums, total = carry
                newer = [read(index * LAGS + i) for i in range(LAGS)]
                pairs = pair_sums(newer)
                if store is not None:
                    for i in range(LAGS // 2):
                        store[index * (LAGS // 2) + i] = pairs[i]
                if level == 0:
                    while len(pairs) > 1:
                        pairs = pair_sums(pairs)
                    total = total + pairs[0]
                return newer, add_lags(older, newer, sums), total

            before = halo[level] if mode == "up" else [zero] * LAGS
            older, sums, total = lax.fori_loop(0, steps, step, (before, [zero] * LAGS, total))
            if mode == "full":
                after_rows = [jnp.where(inner, pltpu.roll(read(i), 8 - width, 0), 0.0) for i in range(LAGS)]
                sums = add_lags(older, after_rows, sums, cross_only=True)
            elif mode == "down":
                sums = add_lags(older, halo[level], sums, cross_only=True)
            for lag in range(LAGS):
                flat[group, pl.ds(level * LAGS + lag, 8, stride=ROWS), :] = sums[lag]
        totals[group] = total

    if kind == "full":
        pl.loop(0, groups)(lambda group: one_group(group, "full", None))
    else:
        pl.loop(0, groups // sides)(lambda group: one_group(group, "up", halos[0]))
        if sides > 1:
            pl.loop(groups // sides, groups)(lambda group: one_group(group, "down", halos[1]))

    def put(out, owner, at, blocks):
        out[owner, at * ROWS : (at + 1) * ROWS, :] = sum(
            flat[block // 8, pl.ds(pl.multiple_of(block % 8 * ROWS, ROWS), ROWS), :] for block in blocks
        )
        out[owner, per * ROWS + at : per * ROWS + at + 1, :] = sum(
            totals[block // 8, pl.ds(block % 8, 1), :] for block in blocks
        )

    for side, out in enumerate(outs):
        out[:, per * ROWS :, :] = jnp.zeros((out.shape[0], out.shape[1] - per * ROWS, 128), F32)
        for owner in range(out.shape[0]):
            for at in range(per):
                if kind == "seg":
                    put(out, owner, at, [(2 * owner + ((where_ref[1] & 1) ^ side)) * per + at])
                else:
                    put(out, owner, at, [at // width * 8 + m * width + at % width for m in range(n_tm)])


def sum_rows(per):
    return per * ROWS + (per + 7) // 8 * 8


def sums_part(where, pieces, dark, halos, kind, per, n_tm):
    n_pix = len(pieces)
    rows, count, _ = pieces[0].shape
    length = n_pix * rows
    return pl.pallas_call(
        functools.partial(sums_kernel, kind, len(halos), n_pix, n_tm, per),
        out_shape=[shape(n_tm // 2, sum_rows(per), 128)] * 2 if kind == "seg" else [shape(1, sum_rows(per), 128)],
        in_specs=[SMEM, VMEM] + [VMEM] * len(halos) + [HBM] * n_pix,
        out_specs=[VMEM] * (2 if kind == "seg" else 1),
        scratch_shapes=[
            pltpu.VMEM((length, count, 128), F32),
            pltpu.VMEM((length // 2, 8, 128), F32),
            pltpu.VMEM((length // 4, 8, 128), F32),
            pltpu.VMEM((length // 8, 8, 128), F32),
            pltpu.VMEM((count // 8, 8 * ROWS, 128), F32),
            pltpu.VMEM((count // 8, 8, 128), F32),
            pltpu.SemaphoreType.DMA((count // 8,)),
        ],
        compiler_params=params(),
        cost_estimate=cost(1.0 + 3.0 * length * count / 2048),
    )(where, dark, *halos, *pieces)


def add_kernel(step, where_ref, mine_ref, got_ref, keep_ref, send_ref):
    side = (where_ref[1] >> step) & 1
    for owner in range(keep_ref.shape[0]):
        for out, at in ((keep_ref, 2 * owner + side), (send_ref, 2 * owner + (side ^ 1))):
            out[owner] = mine_ref[at] + got_ref[at]


def add_part(where, mine, got, step):
    half = shape(mine.shape[0] // 2, *mine.shape[1:])
    return pl.pallas_call(
        functools.partial(add_kernel, step),
        out_shape=[half, half],
        in_specs=[SMEM, VMEM, VMEM],
        out_specs=[VMEM, VMEM],
        compiler_params=params(),
        cost_estimate=cost(0.5),
    )(where, mine, got)


def finish_kernel(parts, resp_ref, keep_ref, *refs):
    sums_refs, (g2_ref, mean_ref) = refs[:-2], refs[-2:]
    row = lax.broadcasted_iota(jnp.int32, (ROWS, 128), 0)
    level, lag = row // LAGS, row % LAGS + 1
    counts = (((FRAMES >> level) - lag) << (2 * level)).astype(F32)
    for start, per, terms in parts:
        mine, sums_refs = sums_refs[:terms], sums_refs[terms:]
        for at in range(per):
            product = sum(ref[0, at * ROWS : (at + 1) * ROWS, :] for ref in mine)
            total = sum(ref[0, per * ROWS + at : per * ROWS + at + 1, :] for ref in mine)
            block = start + at
            keep = keep_ref[block : block + 1, :]
            mean = total * (1.0 / FRAMES)
            g2_ref[:, block * 128 : (block + 1) * 128] = product / (counts * mean * mean) * keep
            mean_ref[block : block + 1, :] = mean / resp_ref[block : block + 1, :] * keep


class Box:
    def __init__(self, value):
        self.value = value


def unbox(got):
    return [got[k].value for k in range(len(got))]


def send(value, axis, pairs, *before):
    for box in before:
        value, box.value = lax.optimization_barrier((value, box.value))
    return Box(lax.ppermute(value, axis, pairs))


def swap(value, axis, other, *before):
    return send(value, axis, [(i, i ^ other) for i in range(lax.axis_size(axis))], *before)


class Line:
    def __init__(self, where):
        self.where = where

    def __call__(self, part, *args):
        outs = part(self.where, *args)
        outs, self.where = lax.optimization_barrier((outs, self.where))
        return outs

    def hold(self, value):
        value, self.where = lax.optimization_barrier((value, self.where))
        return value

    def follow(self, box):
        self.where, box.value = lax.optimization_barrier((self.where, box.value))


def body(raw_frames, frame_order, owner_map, pixel_mask, dark, flat, polarization, solid_angle):
    n_pix = lax.axis_size("pix")
    n_tm = lax.axis_size("tm")
    n_blocks = owner_map.shape[0]
    owned = n_blocks // n_pix
    share = owned // n_tm
    width = 8 // n_tm

    plan = []
    shifts = []
    start = 0
    for kind, eighths in PARTS:
        per = share * eighths // 8
        plan.append((kind, start, per))
        if kind == "seg":
            shifts += [(False, g * share + start + j) for g in range(n_tm) for j in range(per)]
        else:
            shifts += [
                (True, start + unit * width + j) for unit in range(per // width) for _ in range(n_tm) for j in range(width)
            ]
        start += per

    where = jnp.stack([lax.axis_index("pix"), lax.axis_index("tm")]).astype(jnp.int32)
    sizes = (owned, share, n_pix, n_tm)
    pack = functools.partial(pack_parts, raw_frames, frame_order, owner_map)
    (first, second, full) = plan
    line = Line(where)

    far = list(range(n_pix - 1, 1, -1))
    ahead, behind = far[0::2], far[1::2]
    chain = [k for k in range(2, n_tm)]
    others = chain + [1, 0]

    early, late = [1] + ahead, far[1::2] + [0]
    mine = dict(zip(early, line(pack, [first + (early,)], *sizes)))
    got_first = {k: swap(mine[k], "pix", k) for k in early}
    line.follow(got_first[1])
    raw = dict(zip(others, line(pack, [full + (others,)], *sizes)))
    got_full = {0: Box(raw[0]), 1: swap(raw[1], "tm", 1)}
    for at, k in enumerate(chain):
        got_full[k] = swap(raw[k], "tm", k, *[got_full[j] for j in chain[:at][-1:]])
    mine.update(zip(late, line(pack, [first + (late,)], *sizes)))
    got_first[0] = Box(mine[0])
    for at, k in enumerate(late[:-1]):
        also = [got_full[1]] if at == 1 else [got_full[chain[0]]] if at == 2 else []
        got_first[k] = swap(mine[k], "pix", k, got_first[k + 1], *also)

    order = ahead + behind + [1, 0]
    mine = dict(zip(order, line(pack, [second + (order,)], *sizes)))
    got_second = {0: Box(mine[0]), 1: swap(mine[1], "pix", 1, got_first[1])}
    for k in ahead:
        also = [got_full[j] for j in chain[1:]] if k == ahead[-1] else [got_second[1]] if k == ahead[0] else []
        got_second[k] = swap(mine[k], "pix", k, got_first[k - 1], *also)

    dark_own, resp_own, keep_own = line(
        constants_part, owner_map, dark, flat, polarization, solid_angle, pixel_mask, shifts, owned, share
    )
    darks = []
    used = 0
    for _, _, per in plan:
        darks.append(dark_own[used : used + n_tm * per])
        used += n_tm * per

    upward = [(i, i + 1) for i in range(n_tm - 1)]
    ways = (upward, [(j, i) for i, j in upward])

    def halos(got, dark_part, sides):
        return [send(edge, "tm", way) for edge, way in zip(line(edge_part, unbox(got), dark_part, sides), ways)]

    def sums(got, dark_part, halo, kind, per):
        return line(sums_part, unbox(got), dark_part, [h.value for h in halo], kind, per, n_tm)

    halo = halos(got_first, darks[0], 2)
    turned = line(turn_part, unbox(got_full), n_pix, n_tm)
    for k in ahead:
        line.follow(got_second[k])
    for k in behind:
        got_second[k] = swap(mine[k], "pix", k, got_second[k + 1])
    keep, away = sums(got_first, darks[0], halo, "seg", first[2])
    terms = [[keep, swap(away, "tm", 1)], None, None]

    got_full = {0: Box(turned[0]), 1: swap(turned[1], "pix", 1, got_second[1])}
    for k in ahead:
        also = [got_full[1]] if k == ahead[0] else []
        got_full[k] = swap(line.hold(turned[k]), "pix", k, got_second[k - 1], *also)
    halo = halos(got_second, darks[1], 1)
    for k in behind:
        got_full[k] = swap(turned[k], "pix", k, got_full[k + 1])
    keep, away = sums(got_second, darks[1], halo, "seg", second[2])
    terms[1] = [keep, swap(away, "tm", 1)]

    for step in range(1, n_tm.bit_length() - 1):
        for part in range(2):
            keep, box = terms[part]
            keep, away = line(add_part, keep, box.value, step)
            terms[part] = [keep, swap(away, "tm", 1 << step)]
    terms = [[keep, box.value] for keep, box in terms[:2]]
    terms.append(sums(got_full, darks[2], [], "full", full[2]))

    g2, mean = pl.pallas_call(
        functools.partial(
            finish_kernel, [(start, per, len(part)) for (_, start, per), part in zip(plan, terms)]
        ),
        out_shape=[shape(ROWS, share * 128), shape(share, 128)],
        in_specs=[VMEM] * (2 + sum(len(part) for part in terms)),
        out_specs=[VMEM, VMEM],
        compiler_params=params(),
        cost_estimate=cost(1.0),
    )(resp_own, keep_own, *[value for part in terms for value in part])
    return g2.reshape(LEVELS, LAGS, share * 128), mean.reshape(share * 128)


def solution(mesh):
    return jax.shard_map(
        body,
        mesh=mesh,
        in_specs=(P(("tm", "pix"), None), P(("tm", "pix")), P(), P(), P(), P(), P(), P()),
        out_specs=(P(None, None, ("pix", "tm")), P(("pix", "tm"))),
        check_vma=False,
    )
```

```python
import functools

import jax
import jax.numpy as jnp
from jax import lax
from jax.experimental import pallas as pl
from jax.experimental.pallas import tpu as pltpu
from jax.sharding import PartitionSpec as P

FRAMES = 1024
LAGS = 16
LEVELS = 4
ROWS = LEVELS * LAGS
EDGE = LAGS + 8 * (LEVELS - 1)
EDGE_SPAN = LAGS << (LEVELS - 1)

PARTS = (("seg", 3), ("seg", 3), ("full", 2))

SMEM = pl.BlockSpec(memory_space=pltpu.SMEM)
VMEM = pl.BlockSpec(memory_space=pltpu.VMEM)
HBM = pl.BlockSpec(memory_space=pl.ANY)
F32 = jnp.float32


def params():
    return pltpu.CompilerParams(vmem_limit_bytes=40 << 20)


def cost(micros):
    return pl.CostEstimate(flops=0, bytes_accessed=int(micros * 3.6e6), transcendentals=0)


def shape(*dims):
    return jax.ShapeDtypeStruct(dims, F32)


def pack_kernel(jobs, owned, share, n_pix, n_tm, where_ref, order_ref, owner_ref, frames_ref, *refs):
    outs, inverse = refs[:-1], refs[-1]
    rows = frames_ref.shape[0]
    pix, tm = where_ref[0], where_ref[1]
    for i in range(rows):
        inverse[order_ref[i]] = i

    def eight(position_of, store):
        blocks = [owner_ref[position_of(i)] for i in range(8)]
        for high in range(rows // 8):
            tiles = [
                frames_ref[high * 8 : high * 8 + 8, pl.ds(pl.multiple_of(block * 128, 128), 128)] for block in blocks
            ]
            turned = jnp.swapaxes(jnp.stack(tiles), 0, 1)
            for low in range(8):
                store(inverse[high * 8 + low], turned[low])

    taken = 0
    for kind, start, per, others in jobs:
        if kind == "seg":
            for at, other in enumerate(others):
                out = outs[taken + at]
                base = (pix ^ other) * owned + start

                @pl.loop(0, out.shape[1] // 8)
                def _(group, out=out, base=base, per=per):
                    def position_of(i):
                        pos = group * 8 + i
                        return base + (pos // per) * share + pos % per

                    def store(row, value):
                        out[row, pl.ds(pl.multiple_of(group * 8, 8), 8), :] = value

                    eight(position_of, store)

            taken += len(others)
        else:
            width = 8 // n_tm
            for at, other in enumerate(others):
                out = outs[taken + at]
                base = (tm ^ other) * share + start

                @pl.loop(0, out.shape[0] * out.shape[1])
                def _(at, out=out, base=base, width=width):
                    unit, group = at // out.shape[1], at % out.shape[1]

                    def position_of(i):
                        pos = group * 8 + i
                        return base + (pos // width) * owned + unit * width + pos % width

                    def store(row, value):
                        out[unit, group, row] = value

                    eight(position_of, store)

            taken += len(others)


def pack_parts(raw_frames, frame_order, owner_map, where, jobs, owned, share, n_pix, n_tm):
    rows = raw_frames.shape[0]
    outs = []
    size = 0
    for kind, _, per, others in jobs:
        if kind == "seg":
            outs += [shape(rows, n_tm * per, 128)] * len(others)
            size += per * len(others) / n_pix
        else:
            width = 8 // n_tm
            outs += [shape(per // width, n_pix * width // 8, rows, 8, 128)] * len(others)
            size += per
    return pl.pallas_call(
        functools.partial(pack_kernel, jobs, owned, share, n_pix, n_tm),
        out_shape=outs,
        in_specs=[SMEM, SMEM, SMEM, VMEM],
        out_specs=[VMEM] * len(outs),
        scratch_shapes=[pltpu.SMEM((rows,), jnp.int32)],
        compiler_params=params(),
        cost_estimate=cost(1.0 + 8.0 * size / share),
    )(where, frame_order, owner_map, raw_frames)


def turn_kernel(n_pix, n_tm, where_ref, *refs):
    pieces, outs, (held, staged, sem) = refs[:n_tm], refs[n_tm : n_tm + n_pix], refs[n_tm + n_pix :]
    units, groups, rows = pieces[0].shape[:3]
    width = 8 // n_tm
    for other in range(n_tm):
        pltpu.make_async_copy(pieces[other], held.at[where_ref[1] ^ other], sem).start()
    pltpu.make_async_copy(held, held, sem).wait()
    place = lax.broadcasted_iota(jnp.int32, (8, 128), 0) // width

    @pl.loop(0, rows)
    def _(row):
        for unit in range(units):
            for group in range(groups):
                got = [held[m, unit, group, row] for m in range(n_tm)]
                for to in range(n_tm):
                    value = got[to]
                    for m in range(n_tm):
                        if m != to:
                            value = jnp.where(place == m, pltpu.roll(got[m], (m - to) * width % 8, 0), value)
                    staged[group * n_tm + to, row, unit * 8 : unit * 8 + 8, :] = value

    for other in range(n_pix):
        outs[other][...] = staged[where_ref[0] ^ other]


def turn_part(where, pieces, n_pix, n_tm):
    units, groups, rows = pieces[0].shape[:3]
    return pl.pallas_call(
        functools.partial(turn_kernel, n_pix, n_tm),
        out_shape=[shape(rows, units * 8, 128)] * n_pix,
        in_specs=[SMEM] + [HBM] * n_tm,
        out_specs=[VMEM] * n_pix,
        scratch_shapes=[
            pltpu.VMEM((n_tm,) + pieces[0].shape, F32),
            pltpu.VMEM((n_pix, rows, units * 8, 128), F32),
            pltpu.SemaphoreType.DMA,
        ],
        compiler_params=params(),
        cost_estimate=cost(3.0),
    )(where, *pieces)


def constants_kernel(
    plan, owned, share, where_ref, owner_ref, dark_ref, flat_ref, pol_ref, solid_ref, mask_ref, dark_out, resp_out, keep_out
):
    base = where_ref[0] * owned
    mine = base + where_ref[1] * share
    for at, (from_mine, shift) in enumerate(plan):
        row = pl.ds(owner_ref[(mine if from_mine else base) + shift], 1)
        dark_out[at : at + 1, :] = dark_ref[row, :]
    for at in range(share):
        row = pl.ds(owner_ref[mine + at], 1)
        resp_out[at : at + 1, :] = flat_ref[row, :] * pol_ref[row, :] * solid_ref[row, :]
        keep_out[at : at + 1, :] = mask_ref[row, :].astype(F32)


def constants_part(where, owner_map, dark, flat, polarization, solid_angle, pixel_mask, shifts, owned, share):
    n_blocks = owner_map.shape[0]
    tables = [t.reshape(n_blocks, 128) for t in (dark, flat, polarization, solid_angle, pixel_mask)]
    return pl.pallas_call(
        functools.partial(constants_kernel, shifts, owned, share),
        out_shape=[shape(owned, 128), shape(share, 128), shape(share, 128)],
        in_specs=[SMEM, SMEM] + [VMEM] * 5,
        out_specs=[VMEM] * 3,
        compiler_params=params(),
        cost_estimate=cost(1.0),
    )(where, owner_map, *tables)


def pair_sums(rows):
    return [rows[2 * i] + rows[2 * i + 1] for i in range(len(rows) // 2)]


def edge_kernel(n_pix, where_ref, dark_ref, *refs):
    pieces, outs, helds, sems = refs[:n_pix], refs[n_pix : n_pix + 2], refs[n_pix + 2 : n_pix + 4], refs[n_pix + 4]
    rows = pieces[0].shape[0]
    blocks = EDGE_SPAN // rows
    split = helds[0].shape[1]
    for other in range(n_pix):
        source = where_ref[0] ^ other
        for side, (first, held) in enumerate(zip((n_pix - blocks, 0), helds)):

            @pl.when((source >= first) & (source < first + blocks))
            def _(other=other, source=source, side=side, first=first, held=held):
                pltpu.make_async_copy(
                    pieces[other].at[:, pl.ds(side * split, held.shape[1]), :],
                    held.at[pl.ds((source - first) * rows, rows)],
                    sems.at[side],
                ).start()

    for side, (out_ref, held) in enumerate(zip(outs, helds)):
        pltpu.make_async_copy(held, held, sems.at[side]).wait()

        @pl.loop(0, held.shape[1] // 8)
        def _(group, side=side, out_ref=out_ref, held=held):
            lanes = pl.ds(pl.multiple_of(group * 8, 8), 8)
            dark = dark_ref[pl.ds(pl.multiple_of(group * 8 + side * split, 8), 8), :]
            span = 0
            for level in range(LEVELS):
                count = LAGS if level == 0 else LAGS // 2
                width = 1 << level
                begin = span if side else EDGE_SPAN - span - count * width
                for i in range(count):
                    at = begin + i * width
                    got = [held[at + j, lanes, :] - dark for j in range(width)]
                    while len(got) > 1:
                        got = pair_sums(got)
                    out_ref[group, (LAGS + 8 * (level - 1) if level else 0) + i] = got[0]
                span += count * width


def edge_part(where, pieces, dark):
    n_pix = len(pieces)
    groups = pieces[0].shape[1] // 8
    sides = (groups // 2, groups - groups // 2)
    return pl.pallas_call(
        functools.partial(edge_kernel, n_pix),
        out_shape=[shape(side, EDGE, 8, 128) for side in sides],
        in_specs=[SMEM, VMEM] + [HBM] * n_pix,
        out_specs=[VMEM, VMEM],
        scratch_shapes=[pltpu.VMEM((EDGE_SPAN, 8 * side, 128), F32) for side in sides]
        + [pltpu.SemaphoreType.DMA((2,))],
        compiler_params=params(),
        cost_estimate=cost(1.0),
    )(where, dark, *pieces)


def add_lags(older, newer, sums, cross_only=False):
    both = older + newer
    out = []
    for lag in range(1, LAGS + 1):
        total = sums[lag - 1]
        for i in range(lag if cross_only else LAGS):
            total = total + both[LAGS + i] * both[LAGS + i - lag]
        out.append(total)
    return out


def edge_rows(read, last):
    rows = [read(i) for i in range(LAGS)]
    levels = [rows]
    for level in range(1, LEVELS):
        own = [read(LAGS + 8 * (level - 1) + i) for i in range(8)]
        rows = own + pair_sums(rows) if last else pair_sums(rows) + own
        levels.append(rows)
    return levels


def sums_kernel(kind, n_halos, n_pix, n_tm, per, where_ref, dark_ref, *refs):
    halos, pieces, rest = refs[:n_halos], refs[n_halos : n_halos + n_pix], refs[n_halos + n_pix :]
    outs, (series, up_one, up_two, up_three, flat, totals, sems) = rest[:-7], rest[-7:]
    rows = pieces[0].shape[0]
    length = rows * n_pix
    groups = series.shape[1] // 8
    split = halos[0].shape[0] if halos else 0
    for group in range(groups):
        lanes = pl.ds(group * 8, 8)
        for other in range(n_pix):
            pltpu.make_async_copy(
                pieces[other].at[:, lanes, :],
                series.at[pl.ds((where_ref[0] ^ other) * rows, rows), lanes, :],
                sems.at[group],
            ).start()
    zero = jnp.zeros((8, 128), F32)
    stores = (up_one, up_two, up_three, None)
    width = 8 // n_tm
    inner = lax.broadcasted_iota(jnp.int32, (8, 128), 0) < 8 - width

    def one_group(group, mode, halo_ref):
        lanes = pl.ds(pl.multiple_of(group * 8, 8), 8)
        whole = series.at[:, lanes, :]
        pltpu.make_async_copy(whole, whole, sems.at[group]).wait()
        dark = dark_ref[lanes, :]
        if mode != "full":
            halo_group = group if mode == "up" else group - split
            halo = edge_rows(lambda i: halo_ref[halo_group, i], mode == "up")
        total = zero
        for level in range(LEVELS):
            steps = (length >> level) // LAGS
            store = stores[level]
            source = None if level == 0 else stores[level - 1]

            def read(at, source=source):
                return series[at, lanes, :] - dark if source is None else source[at]

            def step(index, carry, read=read, level=level, store=store):
                older, sums, total = carry
                newer = [read(index * LAGS + i) for i in range(LAGS)]
                pairs = pair_sums(newer)
                if store is not None:
                    for i in range(LAGS // 2):
                        store[index * (LAGS // 2) + i] = pairs[i]
                if level == 0:
                    while len(pairs) > 1:
                        pairs = pair_sums(pairs)
                    total = total + pairs[0]
                return newer, add_lags(older, newer, sums), total

            before = halo[level] if mode == "up" else [zero] * LAGS
            older, sums, total = lax.fori_loop(0, steps, step, (before, [zero] * LAGS, total))
            if mode == "full":
                after_rows = [jnp.where(inner, pltpu.roll(read(i), 8 - width, 0), 0.0) for i in range(LAGS)]
                sums = add_lags(older, after_rows, sums, cross_only=True)
            elif mode == "down":
                sums = add_lags(older, halo[level], sums, cross_only=True)
            for lag in range(LAGS):
                flat[group, pl.ds(level * LAGS + lag, 8, stride=ROWS), :] = sums[lag]
        totals[group] = total

    if kind == "full":
        pl.loop(0, groups)(lambda group: one_group(group, "full", None))
    else:
        pl.loop(0, split)(lambda group: one_group(group, "up", halos[0]))
        pl.loop(split, groups)(lambda group: one_group(group, "down", halos[1]))

    def put(out, owner, at, blocks):
        out[owner, at * ROWS : (at + 1) * ROWS, :] = sum(
            flat[block // 8, pl.ds(pl.multiple_of(block % 8 * ROWS, ROWS), ROWS), :] for block in blocks
        )
        out[owner, per * ROWS + at : per * ROWS + at + 1, :] = sum(
            totals[block // 8, pl.ds(block % 8, 1), :] for block in blocks
        )

    for side, out in enumerate(outs):
        out[:, per * ROWS :, :] = jnp.zeros((out.shape[0], out.shape[1] - per * ROWS, 128), F32)
        for owner in range(out.shape[0]):
            for at in range(per):
                if kind == "seg":
                    put(out, owner, at, [(2 * owner + ((where_ref[1] & 1) ^ side)) * per + at])
                else:
                    put(out, owner, at, [at // width * 8 + m * width + at % width for m in range(n_tm)])


def sum_rows(per):
    return per * ROWS + (per + 7) // 8 * 8


def sums_part(where, pieces, dark, halos, kind, per, n_tm):
    n_pix = len(pieces)
    rows, count, _ = pieces[0].shape
    length = n_pix * rows
    return pl.pallas_call(
        functools.partial(sums_kernel, kind, len(halos), n_pix, n_tm, per),
        out_shape=[shape(n_tm // 2, sum_rows(per), 128)] * 2 if kind == "seg" else [shape(1, sum_rows(per), 128)],
        in_specs=[SMEM, VMEM] + [VMEM] * len(halos) + [HBM] * n_pix,
        out_specs=[VMEM] * (2 if kind == "seg" else 1),
        scratch_shapes=[
            pltpu.VMEM((length, count, 128), F32),
            pltpu.VMEM((length // 2, 8, 128), F32),
            pltpu.VMEM((length // 4, 8, 128), F32),
            pltpu.VMEM((length // 8, 8, 128), F32),
            pltpu.VMEM((count // 8, 8 * ROWS, 128), F32),
            pltpu.VMEM((count // 8, 8, 128), F32),
            pltpu.SemaphoreType.DMA((count // 8,)),
        ],
        compiler_params=params(),
        cost_estimate=cost(1.0 + 3.0 * length * count / 2048),
    )(where, dark, *halos, *pieces)


def add_kernel(step, where_ref, mine_ref, got_ref, keep_ref, send_ref):
    side = (where_ref[1] >> step) & 1
    for owner in range(keep_ref.shape[0]):
        for out, at in ((keep_ref, 2 * owner + side), (send_ref, 2 * owner + (side ^ 1))):
            out[owner] = mine_ref[at] + got_ref[at]


def add_part(where, mine, got, step):
    half = shape(mine.shape[0] // 2, *mine.shape[1:])
    return pl.pallas_call(
        functools.partial(add_kernel, step),
        out_shape=[half, half],
        in_specs=[SMEM, VMEM, VMEM],
        out_specs=[VMEM, VMEM],
        compiler_params=params(),
        cost_estimate=cost(0.5),
    )(where, mine, got)


def finish_kernel(parts, resp_ref, keep_ref, *refs):
    sums_refs, (g2_ref, mean_ref) = refs[:-2], refs[-2:]
    row = lax.broadcasted_iota(jnp.int32, (ROWS, 128), 0)
    level, lag = row // LAGS, row % LAGS + 1
    counts = (((FRAMES >> level) - lag) << (2 * level)).astype(F32)
    for start, per, terms in parts:
        mine, sums_refs = sums_refs[:terms], sums_refs[terms:]
        for at in range(per):
            product = sum(ref[0, at * ROWS : (at + 1) * ROWS, :] for ref in mine)
            total = sum(ref[0, per * ROWS + at : per * ROWS + at + 1, :] for ref in mine)
            block = start + at
            keep = keep_ref[block : block + 1, :]
            mean = total * (1.0 / FRAMES)
            g2_ref[:, block * 128 : (block + 1) * 128] = product / (counts * mean * mean) * keep
            mean_ref[block : block + 1, :] = mean / resp_ref[block : block + 1, :] * keep


class Box:
    def __init__(self, value):
        self.value = value


def unbox(got):
    return [got[k].value for k in range(len(got))]


def send(value, axis, pairs, *before):
    for box in before:
        value, box.value = lax.optimization_barrier((value, box.value))
    return Box(lax.ppermute(value, axis, pairs))


def swap(value, axis, other, *before):
    return send(value, axis, [(i, i ^ other) for i in range(lax.axis_size(axis))], *before)


class Line:
    def __init__(self, where):
        self.where = where

    def __call__(self, part, *args):
        outs = part(self.where, *args)
        outs, self.where = lax.optimization_barrier((outs, self.where))
        return outs

    def hold(self, value):
        value, self.where = lax.optimization_barrier((value, self.where))
        return value

    def follow(self, box):
        self.where, box.value = lax.optimization_barrier((self.where, box.value))


def body(raw_frames, frame_order, owner_map, pixel_mask, dark, flat, polarization, solid_angle):
    n_pix = lax.axis_size("pix")
    n_tm = lax.axis_size("tm")
    n_blocks = owner_map.shape[0]
    owned = n_blocks // n_pix
    share = owned // n_tm
    width = 8 // n_tm

    plan = []
    shifts = []
    start = 0
    for kind, eighths in PARTS:
        per = share * eighths // 8
        plan.append((kind, start, per))
        if kind == "seg":
            shifts += [(False, g * share + start + j) for g in range(n_tm) for j in range(per)]
        else:
            shifts += [
                (True, start + unit * width + j) for unit in range(per // width) for _ in range(n_tm) for j in range(width)
            ]
        start += per

    where = jnp.stack([lax.axis_index("pix"), lax.axis_index("tm")]).astype(jnp.int32)
    sizes = (owned, share, n_pix, n_tm)
    pack = functools.partial(pack_parts, raw_frames, frame_order, owner_map)
    (first, second, full) = plan
    line = Line(where)

    far = list(range(n_pix - 1, 1, -1))
    if n_pix == 8:
        far = [7, 6, 5, 3, 4, 2]
    early, late = list(range(n_pix - 1, 1, -2)), list(range(n_pix - 2, 1, -2))
    ahead, behind = far[:2], far[2:]
    chain = [k for k in range(2, n_tm)]
    others = chain + [1, 0]

    mine = dict(zip([1] + early, line(pack, [first + ([1] + early,)], *sizes)))
    got_first = {k: swap(mine[k], "pix", k) for k in [1] + early}
    line.follow(got_first[1])
    raw = dict(zip(others, line(pack, [full + (others,)], *sizes)))
    got_full = {0: Box(raw[0]), 1: swap(raw[1], "tm", 1)}
    for at, k in enumerate(chain):
        got_full[k] = swap(raw[k], "tm", k, *[got_full[j] for j in chain[:at][-1:]])
    mine.update(zip(late + [0], line(pack, [first + (late + [0],)], *sizes)))
    got_first[0] = Box(mine[0])
    for k in late:
        got_first[k] = swap(mine[k], "pix", k, got_first[k + 1])

    order = [1] + ahead + behind + [0]
    mine = dict(zip(order, line(pack, [second + (order,)], *sizes)))
    got_second = {0: Box(mine[0]), 1: swap(mine[1], "pix", 1, got_first[1])}
    for k in ahead:
        got_second[k] = swap(mine[k], "pix", k, got_second[1], *[got_first[j] for j in late])

    dark_own, resp_own, keep_own = line(
        constants_part, owner_map, dark, flat, polarization, solid_angle, pixel_mask, shifts, owned, share
    )
    darks = []
    used = 0
    for _, _, per in plan:
        darks.append(dark_own[used : used + n_tm * per])
        used += n_tm * per

    upward = [(i, i + 1) for i in range(n_tm - 1)]
    ways = (upward, [(j, i) for i, j in upward])

    def halos(got, dark_part):
        return [send(edge, "tm", way) for edge, way in zip(line(edge_part, unbox(got), dark_part), ways)]

    def sums(got, dark_part, halo, kind, per):
        return line(sums_part, unbox(got), dark_part, [h.value for h in halo], kind, per, n_tm)

    def reduce(keep, box, step):
        keep, away = line(add_part, keep, box.value, step)
        return [keep, swap(away, "tm", 1 << step)]

    line.follow(got_full[1])
    halo = halos(got_first, darks[0])
    for k in behind:
        also = [got_full[j] for j in chain[1:]] if k == behind[-1] else []
        got_second[k] = swap(mine[k], "pix", k, *[got_second[j] for j in ahead], *also)
    keep, away = sums(got_first, darks[0], halo, "seg", first[2])
    terms = [[keep, swap(away, "tm", 1)]]

    turned = line(turn_part, unbox(got_full), n_pix, n_tm)
    got_full = {0: Box(turned[0]), 1: swap(turned[1], "pix", 1, got_second[1])}
    for k in ahead:
        got_full[k] = swap(turned[k], "pix", k, got_full[1], *[got_second[j] for j in behind])
    for step in range(1, n_tm.bit_length() - 1):
        terms[0] = reduce(*terms[0], step)

    halo = halos(got_second, darks[1])
    for at, k in enumerate(behind):
        got_full[k] = swap(turned[k], "pix", k, *[got_full[j] for j in (ahead if at < 2 else far[2:4])])
    line.follow(terms[0][1])
    keep, away = sums(got_second, darks[1], halo, "seg", second[2])
    terms.append([keep, swap(away, "tm", 1)])
    for step in range(1, n_tm.bit_length() - 1):
        terms[1] = reduce(*terms[1], step)
    terms = [[keep, box.value] for keep, box in terms[:2]]
    terms.append(sums(got_full, darks[2], [], "full", full[2]))

    g2, mean = pl.pallas_call(
        functools.partial(
            finish_kernel, [(start, per, len(part)) for (_, start, per), part in zip(plan, terms)]
        ),
        out_shape=[shape(ROWS, share * 128), shape(share, 128)],
        in_specs=[VMEM] * (2 + sum(len(part) for part in terms)),
        out_specs=[VMEM, VMEM],
        compiler_params=params(),
        cost_estimate=cost(1.0),
    )(resp_own, keep_own, *[value for part in terms for value in part])
    return g2.reshape(LEVELS, LAGS, share * 128), mean.reshape(share * 128)


def solution(mesh):
    return jax.shard_map(
        body,
        mesh=mesh,
        in_specs=(P(("tm", "pix"), None), P(("tm", "pix")), P(), P(), P(), P(), P(), P()),
        out_specs=(P(None, None, ("pix", "tm")), P(("pix", "tm"))),
        check_vma=False,
    )
```

```python
import functools

import jax
import jax.numpy as jnp
from jax import lax
from jax.experimental import pallas as pl
from jax.experimental.pallas import tpu as pltpu
from jax.sharding import PartitionSpec as P

FRAMES = 1024
LAGS = 16
LEVELS = 4
ROWS = LEVELS * LAGS
EDGE = LAGS + 8 * (LEVELS - 1)
EDGE_SPAN = LAGS << (LEVELS - 1)

PARTS = (("seg", 4), ("seg", 2), ("full", 2))

SMEM = pl.BlockSpec(memory_space=pltpu.SMEM)
VMEM = pl.BlockSpec(memory_space=pltpu.VMEM)
HBM = pl.BlockSpec(memory_space=pl.ANY)
F32 = jnp.float32


def params():
    return pltpu.CompilerParams(vmem_limit_bytes=40 << 20)


def cost(micros):
    return pl.CostEstimate(flops=0, bytes_accessed=int(micros * 3.6e6), transcendentals=0)


def shape(*dims):
    return jax.ShapeDtypeStruct(dims, F32)


def pack_kernel(jobs, owned, share, n_pix, n_tm, where_ref, order_ref, owner_ref, frames_ref, *refs):
    outs, inverse = refs[:-1], refs[-1]
    rows = frames_ref.shape[0]
    pix, tm = where_ref[0], where_ref[1]
    for i in range(rows):
        inverse[order_ref[i]] = i

    def eight(position_of, store):
        blocks = [owner_ref[position_of(i)] for i in range(8)]
        for high in range(rows // 8):
            tiles = [
                frames_ref[high * 8 : high * 8 + 8, pl.ds(pl.multiple_of(block * 128, 128), 128)] for block in blocks
            ]
            turned = jnp.swapaxes(jnp.stack(tiles), 0, 1)
            for low in range(8):
                store(inverse[high * 8 + low], turned[low])

    taken = 0
    for kind, start, per, others in jobs:
        if kind == "seg":
            for at, other in enumerate(others):
                out = outs[taken + at]
                base = (pix ^ other) * owned + start

                @pl.loop(0, out.shape[1] // 8)
                def _(group, out=out, base=base, per=per):
                    def position_of(i):
                        pos = group * 8 + i
                        return base + (pos // per) * share + pos % per

                    def store(row, value):
                        out[row, pl.ds(pl.multiple_of(group * 8, 8), 8), :] = value

                    eight(position_of, store)

            taken += len(others)
        else:
            width = 8 // n_tm
            for at, other in enumerate(others):
                out = outs[taken + at]
                base = (tm ^ other) * share + start

                @pl.loop(0, out.shape[0] * out.shape[1])
                def _(at, out=out, base=base, width=width):
                    unit, group = at // out.shape[1], at % out.shape[1]

                    def position_of(i):
                        pos = group * 8 + i
                        return base + (pos // width) * owned + unit * width + pos % width

                    def store(row, value):
                        out[unit, group, row] = value

                    eight(position_of, store)

            taken += len(others)


def pack_parts(raw_frames, frame_order, owner_map, where, jobs, owned, share, n_pix, n_tm):
    rows = raw_frames.shape[0]
    outs = []
    size = 0
    for kind, _, per, others in jobs:
        if kind == "seg":
            outs += [shape(rows, n_tm * per, 128)] * len(others)
            size += per * len(others) / n_pix
        else:
            width = 8 // n_tm
            outs += [shape(per // width, n_pix * width // 8, rows, 8, 128)] * len(others)
            size += per
    return pl.pallas_call(
        functools.partial(pack_kernel, jobs, owned, share, n_pix, n_tm),
        out_shape=outs,
        in_specs=[SMEM, SMEM, SMEM, VMEM],
        out_specs=[VMEM] * len(outs),
        scratch_shapes=[pltpu.SMEM((rows,), jnp.int32)],
        compiler_params=params(),
        cost_estimate=cost(1.0 + 8.0 * size / share),
    )(where, frame_order, owner_map, raw_frames)


def turn_kernel(n_pix, n_tm, where_ref, *refs):
    pieces, outs, (held, staged, sem) = refs[:n_tm], refs[n_tm : n_tm + n_pix], refs[n_tm + n_pix :]
    units, groups, rows = pieces[0].shape[:3]
    width = 8 // n_tm
    for other in range(n_tm):
        pltpu.make_async_copy(pieces[other], held.at[where_ref[1] ^ other], sem).start()
    pltpu.make_async_copy(held, held, sem).wait()
    place = lax.broadcasted_iota(jnp.int32, (8, 128), 0) // width

    @pl.loop(0, rows)
    def _(row):
        for unit in range(units):
            for group in range(groups):
                got = [held[m, unit, group, row] for m in range(n_tm)]
                for to in range(n_tm):
                    value = got[to]
                    for m in range(n_tm):
                        if m != to:
                            value = jnp.where(place == m, pltpu.roll(got[m], (m - to) * width % 8, 0), value)
                    staged[group * n_tm + to, row, unit * 8 : unit * 8 + 8, :] = value

    for other in range(n_pix):
        outs[other][...] = staged[where_ref[0] ^ other]


def turn_part(where, pieces, n_pix, n_tm):
    units, groups, rows = pieces[0].shape[:3]
    return pl.pallas_call(
        functools.partial(turn_kernel, n_pix, n_tm),
        out_shape=[shape(rows, units * 8, 128)] * n_pix,
        in_specs=[SMEM] + [HBM] * n_tm,
        out_specs=[VMEM] * n_pix,
        scratch_shapes=[
            pltpu.VMEM((n_tm,) + pieces[0].shape, F32),
            pltpu.VMEM((n_pix, rows, units * 8, 128), F32),
            pltpu.SemaphoreType.DMA,
        ],
        compiler_params=params(),
        cost_estimate=cost(3.0),
    )(where, *pieces)


def constants_kernel(
    plan, owned, share, where_ref, owner_ref, dark_ref, flat_ref, pol_ref, solid_ref, mask_ref, dark_out, resp_out, keep_out
):
    base = where_ref[0] * owned
    mine = base + where_ref[1] * share
    for at, (from_mine, shift) in enumerate(plan):
        row = pl.ds(owner_ref[(mine if from_mine else base) + shift], 1)
        dark_out[at : at + 1, :] = dark_ref[row, :]
    for at in range(share):
        row = pl.ds(owner_ref[mine + at], 1)
        resp_out[at : at + 1, :] = flat_ref[row, :] * pol_ref[row, :] * solid_ref[row, :]
        keep_out[at : at + 1, :] = mask_ref[row, :].astype(F32)


def constants_part(where, owner_map, dark, flat, polarization, solid_angle, pixel_mask, shifts, owned, share):
    n_blocks = owner_map.shape[0]
    tables = [t.reshape(n_blocks, 128) for t in (dark, flat, polarization, solid_angle, pixel_mask)]
    return pl.pallas_call(
        functools.partial(constants_kernel, shifts, owned, share),
        out_shape=[shape(owned, 128), shape(share, 128), shape(share, 128)],
        in_specs=[SMEM, SMEM] + [VMEM] * 5,
        out_specs=[VMEM] * 3,
        compiler_params=params(),
        cost_estimate=cost(1.0),
    )(where, owner_map, *tables)


def pair_sums(rows):
    return [rows[2 * i] + rows[2 * i + 1] for i in range(len(rows) // 2)]


def edge_kernel(n_pix, where_ref, dark_ref, *refs):
    pieces, outs, (held, sem) = refs[:n_pix], refs[n_pix:-2], refs[-2:]
    rows = pieces[0].shape[0]
    blocks = EDGE_SPAN // rows
    half = held.shape[2]
    for other in range(n_pix):
        source = where_ref[0] ^ other
        for side, first in ((0, n_pix - blocks), (1, 0))[: len(outs)]:

            @pl.when((source >= first) & (source < first + blocks))
            def _(other=other, source=source, side=side, first=first):
                pltpu.make_async_copy(
                    pieces[other].at[:, pl.ds(side * half, half), :],
                    held.at[side, pl.ds((source - first) * rows, rows)],
                    sem,
                ).start()

    pltpu.make_async_copy(held, held, sem).wait()

    for side, out_ref in enumerate(outs):

        @pl.loop(0, half // 8)
        def _(group, side=side, out_ref=out_ref):
            lanes = pl.ds(pl.multiple_of(group * 8, 8), 8)
            dark = dark_ref[pl.ds(pl.multiple_of(group * 8 + side * half, 8), 8), :]
            span = 0
            for level in range(LEVELS):
                count = LAGS if level == 0 else LAGS // 2
                width = 1 << level
                begin = span if side else EDGE_SPAN - span - count * width
                for i in range(count):
                    at = begin + i * width
                    got = [held[side, at + j, lanes, :] - dark for j in range(width)]
                    while len(got) > 1:
                        got = pair_sums(got)
                    out_ref[group, (LAGS + 8 * (level - 1) if level else 0) + i] = got[0]
                span += count * width


def edge_part(where, pieces, dark, sides):
    n_pix = len(pieces)
    half = pieces[0].shape[1] // sides
    return pl.pallas_call(
        functools.partial(edge_kernel, n_pix),
        out_shape=[shape(half // 8, EDGE, 8, 128)] * sides,
        in_specs=[SMEM, VMEM] + [HBM] * n_pix,
        out_specs=[VMEM] * sides,
        scratch_shapes=[pltpu.VMEM((sides, EDGE_SPAN, half, 128), F32), pltpu.SemaphoreType.DMA],
        compiler_params=params(),
        cost_estimate=cost(2.0),
    )(where, dark, *pieces)


def add_lags(older, newer, sums, cross_only=False):
    both = older + newer
    out = []
    for lag in range(1, LAGS + 1):
        total = sums[lag - 1]
        for i in range(lag if cross_only else LAGS):
            total = total + both[LAGS + i] * both[LAGS + i - lag]
        out.append(total)
    return out


def edge_rows(read, last):
    rows = [read(i) for i in range(LAGS)]
    levels = [rows]
    for level in range(1, LEVELS):
        own = [read(LAGS + 8 * (level - 1) + i) for i in range(8)]
        rows = own + pair_sums(rows) if last else pair_sums(rows) + own
        levels.append(rows)
    return levels


def sums_kernel(kind, span, n_tm, per, n_pix, taken, where_ref, dark_ref, *refs):
    refs = list(refs)
    halo_ref = refs.pop(0) if kind != "full" else None
    before_ref = refs.pop(0) if taken else None
    pieces, rest = refs[:n_pix], refs[n_pix:]
    outs, (series, up_one, up_two, up_three, flat, totals, sems) = rest[:-7], rest[-7:]
    rows = pieces[0].shape[0]
    length = rows * n_pix
    begin, groups = span
    for group in range(groups):
        for other in range(n_pix):
            pltpu.make_async_copy(
                pieces[other].at[:, pl.ds((begin + group) * 8, 8), :],
                series.at[pl.ds((where_ref[0] ^ other) * rows, rows), pl.ds(group * 8, 8), :],
                sems.at[group],
            ).start()
    zero = jnp.zeros((8, 128), F32)
    stores = (up_one, up_two, up_three, None)
    width = 8 // n_tm
    inner = lax.broadcasted_iota(jnp.int32, (8, 128), 0) < 8 - width

    @pl.loop(0, groups)
    def _(group):
        lanes = pl.ds(pl.multiple_of(group * 8, 8), 8)
        whole = series.at[:, lanes, :]
        pltpu.make_async_copy(whole, whole, sems.at[group]).wait()
        dark = dark_ref[pl.ds(pl.multiple_of((begin + group) * 8, 8), 8), :]
        if kind != "full":
            halo = edge_rows(lambda i: halo_ref[group, i], kind == "up")
        total = zero
        for level in range(LEVELS):
            steps = (length >> level) // LAGS
            store = stores[level]
            source = None if level == 0 else stores[level - 1]

            def read(at, source=source):
                return series[at, lanes, :] - dark if source is None else source[at]

            def step(index, carry, read=read, level=level, store=store):
                older, sums, total = carry
                newer = [read(index * LAGS + i) for i in range(LAGS)]
                pairs = pair_sums(newer)
                if store is not None:
                    for i in range(LAGS // 2):
                        store[index * (LAGS // 2) + i] = pairs[i]
                if level == 0:
                    while len(pairs) > 1:
                        pairs = pair_sums(pairs)
                    total = total + pairs[0]
                return newer, add_lags(older, newer, sums), total

            before = halo[level] if kind == "up" else [zero] * LAGS
            older, sums, total = lax.fori_loop(0, steps, step, (before, [zero] * LAGS, total))
            if kind == "full":
                after_rows = [jnp.where(inner, pltpu.roll(read(i), 8 - width, 0), 0.0) for i in range(LAGS)]
                sums = add_lags(older, after_rows, sums, cross_only=True)
            elif kind == "down":
                sums = add_lags(older, halo[level], sums, cross_only=True)
            for lag in range(LAGS):
                flat[group, pl.ds(level * LAGS + lag, 8, stride=ROWS), :] = sums[lag]
        totals[group] = total

    def put(out, owner, at, blocks):
        out[owner, at * ROWS : (at + 1) * ROWS, :] = sum(
            flat[block // 8, pl.ds(pl.multiple_of(block % 8 * ROWS, ROWS), ROWS), :] for block in blocks
        )
        out[owner, per * ROWS + at : per * ROWS + at + 1, :] = sum(
            totals[block // 8, pl.ds(block % 8, 1), :] for block in blocks
        )

    for side, out in enumerate(outs):
        out[:, per * ROWS :, :] = jnp.zeros((out.shape[0], out.shape[1] - per * ROWS, 128), F32)
        for owner in range(out.shape[0]):
            if kind == "full":
                for at in range(per):
                    put(out, owner, at, [at // width * 8 + m * width + at % width for m in range(n_tm)])
            elif len(outs) == 1:
                for at in range(per):
                    put(out, owner, at, [owner * per + at])
            else:
                source = 2 * owner + ((where_ref[1] & 1) ^ side)
                if owner < taken // 2:
                    out[owner] = before_ref[source]
                else:
                    for at in range(per):
                        put(out, owner, at, [(source - taken) * per + at])


def sum_rows(per):
    return per * ROWS + (per + 7) // 8 * 8


def sums_part(where, pieces, dark, halo, before, kind, span, per, n_tm):
    n_pix = len(pieces)
    rows = pieces[0].shape[0]
    length = n_pix * rows
    groups = span[1]
    owners = groups * 8 // per
    taken = 0 if before is None else before.shape[0]
    if kind == "full":
        outs = [shape(1, sum_rows(per), 128)]
    elif owners + taken < n_tm:
        outs = [shape(owners, sum_rows(per), 128)]
    else:
        outs = [shape(n_tm // 2, sum_rows(per), 128)] * 2
    extra = ([] if halo is None else [halo]) + ([] if before is None else [before])
    return pl.pallas_call(
        functools.partial(sums_kernel, kind, span, n_tm, per, n_pix, taken),
        out_shape=outs,
        in_specs=[SMEM, VMEM] + [VMEM] * len(extra) + [HBM] * n_pix,
        out_specs=[VMEM] * len(outs),
        scratch_shapes=[
            pltpu.VMEM((length, groups * 8, 128), F32),
            pltpu.VMEM((length // 2, 8, 128), F32),
            pltpu.VMEM((length // 4, 8, 128), F32),
            pltpu.VMEM((length // 8, 8, 128), F32),
            pltpu.VMEM((groups, 8 * ROWS, 128), F32),
            pltpu.VMEM((groups, 8, 128), F32),
            pltpu.SemaphoreType.DMA((groups,)),
        ],
        compiler_params=params(),
        cost_estimate=cost(1.0 + 3.0 * length * groups / 256),
    )(where, dark, *extra, *pieces)


def add_kernel(step, where_ref, mine_ref, got_ref, keep_ref, send_ref):
    side = (where_ref[1] >> step) & 1
    for owner in range(keep_ref.shape[0]):
        for out, at in ((keep_ref, 2 * owner + side), (send_ref, 2 * owner + (side ^ 1))):
            out[owner] = mine_ref[at] + got_ref[at]


def add_part(where, mine, got, step):
    half = shape(mine.shape[0] // 2, *mine.shape[1:])
    return pl.pallas_call(
        functools.partial(add_kernel, step),
        out_shape=[half, half],
        in_specs=[SMEM, VMEM, VMEM],
        out_specs=[VMEM, VMEM],
        compiler_params=params(),
        cost_estimate=cost(0.5),
    )(where, mine, got)


def finish_kernel(parts, resp_ref, keep_ref, *refs):
    sums_refs, (g2_ref, mean_ref) = refs[:-2], refs[-2:]
    row = lax.broadcasted_iota(jnp.int32, (ROWS, 128), 0)
    level, lag = row // LAGS, row % LAGS + 1
    counts = (((FRAMES >> level) - lag) << (2 * level)).astype(F32)
    for start, per, terms in parts:
        mine, sums_refs = sums_refs[:terms], sums_refs[terms:]
        for at in range(per):
            product = sum(ref[0, at * ROWS : (at + 1) * ROWS, :] for ref in mine)
            total = sum(ref[0, per * ROWS + at : per * ROWS + at + 1, :] for ref in mine)
            block = start + at
            keep = keep_ref[block : block + 1, :]
            mean = total * (1.0 / FRAMES)
            g2_ref[:, block * 128 : (block + 1) * 128] = product / (counts * mean * mean) * keep
            mean_ref[block : block + 1, :] = mean / resp_ref[block : block + 1, :] * keep


class Box:
    def __init__(self, value):
        self.value = value


def unbox(got):
    return [got[k].value for k in range(len(got))]


def send(value, axis, pairs, *before):
    for box in before:
        value, box.value = lax.optimization_barrier((value, box.value))
    return Box(lax.ppermute(value, axis, pairs))


def swap(value, axis, other, *before):
    return send(value, axis, [(i, i ^ other) for i in range(lax.axis_size(axis))], *before)


class Line:
    def __init__(self, where):
        self.where = where

    def __call__(self, part, *args):
        outs = part(self.where, *args)
        outs, self.where = lax.optimization_barrier((outs, self.where))
        return outs

    def hold(self, value):
        value, self.where = lax.optimization_barrier((value, self.where))
        return value

    def follow(self, box):
        self.where, box.value = lax.optimization_barrier((self.where, box.value))


def body(raw_frames, frame_order, owner_map, pixel_mask, dark, flat, polarization, solid_angle):
    n_pix = lax.axis_size("pix")
    n_tm = lax.axis_size("tm")
    n_blocks = owner_map.shape[0]
    owned = n_blocks // n_pix
    share = owned // n_tm
    width = 8 // n_tm

    plan = []
    shifts = []
    start = 0
    for kind, eighths in PARTS:
        per = share * eighths // 8
        plan.append((kind, start, per))
        if kind == "seg":
            shifts += [(False, g * share + start + j) for g in range(n_tm) for j in range(per)]
        else:
            shifts += [
                (True, start + unit * width + j) for unit in range(per // width) for _ in range(n_tm) for j in range(width)
            ]
        start += per

    where = jnp.stack([lax.axis_index("pix"), lax.axis_index("tm")]).astype(jnp.int32)
    sizes = (owned, share, n_pix, n_tm)
    pack = functools.partial(pack_parts, raw_frames, frame_order, owner_map)
    (first, second, full) = plan
    line = Line(where)

    far = list(range(n_pix - 1, 1, -1))
    ahead, behind = far[0::2], far[1::2]
    chain = [k for k in range(2, n_tm)]
    others = chain + [1, 0]

    early, late = [1] + ahead, far[1::2] + [0]
    mine = dict(zip(early, line(pack, [first + (early,)], *sizes)))
    got_first = {k: swap(mine[k], "pix", k) for k in early}
    line.follow(got_first[1])
    raw = dict(zip(others, line(pack, [full + (others,)], *sizes)))
    got_full = {0: Box(raw[0]), 1: swap(raw[1], "tm", 1)}
    for at, k in enumerate(chain):
        got_full[k] = swap(raw[k], "tm", k, *[got_full[j] for j in chain[:at][-1:]])
    mine.update(zip(late, line(pack, [first + (late,)], *sizes)))
    got_first[0] = Box(mine[0])
    for at, k in enumerate(late[:-1]):
        also = [got_full[chain[0]]] if at == 2 else []
        got_first[k] = swap(mine[k], "pix", k, got_first[k + 1], *also)

    order = ahead + behind + [1, 0]
    mine = dict(zip(order, line(pack, [second + (order,)], *sizes)))
    got_second = {0: Box(mine[0]), 1: swap(mine[1], "pix", 1, got_first[1])}
    for k in ahead:
        also = [got_full[j] for j in chain[1:]] if k == ahead[-1] else [got_second[1], got_full[1]] if k == ahead[0] else []
        got_second[k] = swap(mine[k], "pix", k, got_first[k - 1], *also)

    dark_own, resp_own, keep_own = line(
        constants_part, owner_map, dark, flat, polarization, solid_angle, pixel_mask, shifts, owned, share
    )
    darks = []
    used = 0
    for _, _, per in plan:
        darks.append(dark_own[used : used + n_tm * per])
        used += n_tm * per

    upward = [(i, i + 1) for i in range(n_tm - 1)]
    ways = (upward, [(j, i) for i, j in upward])

    def halos(got, dark_part, sides):
        return [send(edge, "tm", way) for edge, way in zip(line(edge_part, unbox(got), dark_part, sides), ways)]

    def sums(got, dark_part, halo, before, kind, span, per):
        halo = None if halo is None else halo.value
        return line(sums_part, unbox(got), dark_part, halo, before, kind, span, per, n_tm)

    def reduce(keep, box, step):
        keep, away = line(add_part, keep, box.value, step)
        return [keep, swap(away, "tm", 1 << step)]

    halo = halos(got_first, darks[0], 2)
    half = n_tm * first[2] // 16
    turned = line(turn_part, unbox(got_full), n_pix, n_tm)
    (before,) = sums(got_first, darks[0], halo[0], None, "up", (0, half), first[2])
    for k in ahead:
        line.follow(got_second[k])
    for k in behind:
        got_second[k] = swap(mine[k], "pix", k, got_second[k + 1])
    keep, away = sums(got_first, darks[0], halo[1], before, "down", (half, half), first[2])
    terms = [[keep, swap(away, "tm", 1)]]

    got_full = {0: Box(turned[0]), 1: swap(turned[1], "pix", 1, got_second[1])}
    for k in ahead:
        also = [got_full[1]] if k == ahead[0] else []
        got_full[k] = swap(line.hold(turned[k]), "pix", k, got_second[k - 1], *also)
    halo = halos(got_second, darks[1], 1)
    for k in behind:
        got_full[k] = swap(turned[k], "pix", k, got_full[k + 1])
    for step in range(1, n_tm.bit_length() - 1):
        terms[0] = reduce(*terms[0], step)
    keep, away = sums(got_second, darks[1], halo[0], None, "up", (0, n_tm * second[2] // 8), second[2])
    terms.append([keep, swap(away, "tm", 1)])
    for step in range(1, n_tm.bit_length() - 1):
        terms[1] = reduce(*terms[1], step)
    terms = [[keep, box.value] for keep, box in terms[:2]]
    terms.append(sums(got_full, darks[2], None, None, "full", (0, n_tm * full[2] // 8), full[2]))

    g2, mean = pl.pallas_call(
        functools.partial(
            finish_kernel, [(start, per, len(part)) for (_, start, per), part in zip(plan, terms)]
        ),
        out_shape=[shape(ROWS, share * 128), shape(share, 128)],
        in_specs=[VMEM] * (2 + sum(len(part) for part in terms)),
        out_specs=[VMEM, VMEM],
        compiler_params=params(),
        cost_estimate=cost(1.0),
    )(resp_own, keep_own, *[value for part in terms for value in part])
    return g2.reshape(LEVELS, LAGS, share * 128), mean.reshape(share * 128)


def solution(mesh):
    return jax.shard_map(
        body,
        mesh=mesh,
        in_specs=(P(("tm", "pix"), None), P(("tm", "pix")), P(), P(), P(), P(), P(), P()),
        out_specs=(P(None, None, ("pix", "tm")), P(("pix", "tm"))),
        check_vma=False,
    )
```

```python
import functools

import jax
import jax.numpy as jnp
from jax import lax
from jax.experimental import pallas as pl
from jax.experimental.pallas import tpu as pltpu
from jax.sharding import PartitionSpec as P

FRAMES = 1024
LAGS = 16
LEVELS = 4
ROWS = LEVELS * LAGS
EDGE = LAGS + 8 * (LEVELS - 1)
EDGE_SPAN = LAGS << (LEVELS - 1)

PARTS = (("seg", 4), ("seg", 2), ("full", 2))

SMEM = pl.BlockSpec(memory_space=pltpu.SMEM)
VMEM = pl.BlockSpec(memory_space=pltpu.VMEM)
HBM = pl.BlockSpec(memory_space=pl.ANY)
F32 = jnp.float32


def params():
    return pltpu.CompilerParams(vmem_limit_bytes=40 << 20)


def cost(micros):
    return pl.CostEstimate(flops=0, bytes_accessed=int(micros * 3.6e6), transcendentals=0)


def shape(*dims):
    return jax.ShapeDtypeStruct(dims, F32)


def pack_kernel(jobs, owned, share, n_pix, n_tm, where_ref, order_ref, owner_ref, frames_ref, *refs):
    outs, inverse = refs[:-1], refs[-1]
    rows = frames_ref.shape[0]
    pix, tm = where_ref[0], where_ref[1]
    for i in range(rows):
        inverse[order_ref[i]] = i

    def eight(position_of, store):
        blocks = [owner_ref[position_of(i)] for i in range(8)]
        for high in range(rows // 8):
            tiles = [
                frames_ref[high * 8 : high * 8 + 8, pl.ds(pl.multiple_of(block * 128, 128), 128)] for block in blocks
            ]
            turned = jnp.swapaxes(jnp.stack(tiles), 0, 1)
            for low in range(8):
                store(inverse[high * 8 + low], turned[low])

    taken = 0
    for kind, start, per, others in jobs:
        if kind == "seg":
            for at, other in enumerate(others):
                out = outs[taken + at]
                base = (pix ^ other) * owned + start

                @pl.loop(0, out.shape[1] // 8)
                def _(group, out=out, base=base, per=per):
                    def position_of(i):
                        pos = group * 8 + i
                        return base + (pos // per) * share + pos % per

                    def store(row, value):
                        out[row, pl.ds(pl.multiple_of(group * 8, 8), 8), :] = value

                    eight(position_of, store)

            taken += len(others)
        else:
            width = 8 // n_tm
            for at, other in enumerate(others):
                out = outs[taken + at]
                base = (tm ^ other) * share + start

                @pl.loop(0, out.shape[0] * out.shape[1])
                def _(at, out=out, base=base, width=width):
                    unit, group = at // out.shape[1], at % out.shape[1]

                    def position_of(i):
                        pos = group * 8 + i
                        return base + (pos // width) * owned + unit * width + pos % width

                    def store(row, value):
                        out[unit, group, row] = value

                    eight(position_of, store)

            taken += len(others)


def pack_parts(raw_frames, frame_order, owner_map, where, jobs, owned, share, n_pix, n_tm):
    rows = raw_frames.shape[0]
    outs = []
    size = 0
    for kind, _, per, others in jobs:
        if kind == "seg":
            outs += [shape(rows, n_tm * per, 128)] * len(others)
            size += per * len(others) / n_pix
        else:
            width = 8 // n_tm
            outs += [shape(per // width, n_pix * width // 8, rows, 8, 128)] * len(others)
            size += per
    return pl.pallas_call(
        functools.partial(pack_kernel, jobs, owned, share, n_pix, n_tm),
        out_shape=outs,
        in_specs=[SMEM, SMEM, SMEM, VMEM],
        out_specs=[VMEM] * len(outs),
        scratch_shapes=[pltpu.SMEM((rows,), jnp.int32)],
        compiler_params=params(),
        cost_estimate=cost(1.0 + 8.0 * size / share),
    )(where, frame_order, owner_map, raw_frames)


def turn_kernel(n_pix, n_tm, where_ref, *refs):
    pieces, outs, (held, staged, sem) = refs[:n_tm], refs[n_tm : n_tm + n_pix], refs[n_tm + n_pix :]
    units, groups, rows = pieces[0].shape[:3]
    width = 8 // n_tm
    for other in range(n_tm):
        pltpu.make_async_copy(pieces[other], held.at[where_ref[1] ^ other], sem).start()
    pltpu.make_async_copy(held, held, sem).wait()
    place = lax.broadcasted_iota(jnp.int32, (8, 128), 0) // width

    @pl.loop(0, rows)
    def _(row):
        for unit in range(units):
            for group in range(groups):
                got = [held[m, unit, group, row] for m in range(n_tm)]
                for to in range(n_tm):
                    value = got[to]
                    for m in range(n_tm):
                        if m != to:
                            value = jnp.where(place == m, pltpu.roll(got[m], (m - to) * width % 8, 0), value)
                    staged[group * n_tm + to, row, unit * 8 : unit * 8 + 8, :] = value

    for other in range(n_pix):
        outs[other][...] = staged[where_ref[0] ^ other]


def turn_part(where, pieces, n_pix, n_tm):
    units, groups, rows = pieces[0].shape[:3]
    return pl.pallas_call(
        functools.partial(turn_kernel, n_pix, n_tm),
        out_shape=[shape(rows, units * 8, 128)] * n_pix,
        in_specs=[SMEM] + [HBM] * n_tm,
        out_specs=[VMEM] * n_pix,
        scratch_shapes=[
            pltpu.VMEM((n_tm,) + pieces[0].shape, F32),
            pltpu.VMEM((n_pix, rows, units * 8, 128), F32),
            pltpu.SemaphoreType.DMA,
        ],
        compiler_params=params(),
        cost_estimate=cost(3.0),
    )(where, *pieces)


def constants_kernel(
    plan, owned, share, where_ref, owner_ref, dark_ref, flat_ref, pol_ref, solid_ref, mask_ref, dark_out, resp_out, keep_out
):
    base = where_ref[0] * owned
    mine = base + where_ref[1] * share
    for at, (from_mine, shift) in enumerate(plan):
        row = pl.ds(owner_ref[(mine if from_mine else base) + shift], 1)
        dark_out[at : at + 1, :] = dark_ref[row, :]
    for at in range(share):
        row = pl.ds(owner_ref[mine + at], 1)
        resp_out[at : at + 1, :] = flat_ref[row, :] * pol_ref[row, :] * solid_ref[row, :]
        keep_out[at : at + 1, :] = mask_ref[row, :].astype(F32)


def constants_part(where, owner_map, dark, flat, polarization, solid_angle, pixel_mask, shifts, owned, share):
    n_blocks = owner_map.shape[0]
    tables = [t.reshape(n_blocks, 128) for t in (dark, flat, polarization, solid_angle, pixel_mask)]
    return pl.pallas_call(
        functools.partial(constants_kernel, shifts, owned, share),
        out_shape=[shape(owned, 128), shape(share, 128), shape(share, 128)],
        in_specs=[SMEM, SMEM] + [VMEM] * 5,
        out_specs=[VMEM] * 3,
        compiler_params=params(),
        cost_estimate=cost(1.0),
    )(where, owner_map, *tables)


def pair_sums(rows):
    return [rows[2 * i] + rows[2 * i + 1] for i in range(len(rows) // 2)]


def edge_kernel(n_pix, where_ref, dark_ref, *refs):
    pieces, outs, (held, sem) = refs[:n_pix], refs[n_pix:-2], refs[-2:]
    rows = pieces[0].shape[0]
    blocks = EDGE_SPAN // rows
    half = held.shape[2]
    for other in range(n_pix):
        source = where_ref[0] ^ other
        for side, first in ((0, n_pix - blocks), (1, 0))[: len(outs)]:

            @pl.when((source >= first) & (source < first + blocks))
            def _(other=other, source=source, side=side, first=first):
                pltpu.make_async_copy(
                    pieces[other].at[:, pl.ds(side * half, half), :],
                    held.at[side, pl.ds((source - first) * rows, rows)],
                    sem,
                ).start()

    pltpu.make_async_copy(held, held, sem).wait()

    for side, out_ref in enumerate(outs):

        @pl.loop(0, half // 8)
        def _(group, side=side, out_ref=out_ref):
            lanes = pl.ds(pl.multiple_of(group * 8, 8), 8)
            dark = dark_ref[pl.ds(pl.multiple_of(group * 8 + side * half, 8), 8), :]
            span = 0
            for level in range(LEVELS):
                count = LAGS if level == 0 else LAGS // 2
                width = 1 << level
                begin = span if side else EDGE_SPAN - span - count * width
                for i in range(count):
                    at = begin + i * width
                    got = [held[side, at + j, lanes, :] - dark for j in range(width)]
                    while len(got) > 1:
                        got = pair_sums(got)
                    out_ref[group, (LAGS + 8 * (level - 1) if level else 0) + i] = got[0]
                span += count * width


def edge_part(where, pieces, dark, sides):
    n_pix = len(pieces)
    half = pieces[0].shape[1] // sides
    return pl.pallas_call(
        functools.partial(edge_kernel, n_pix),
        out_shape=[shape(half // 8, EDGE, 8, 128)] * sides,
        in_specs=[SMEM, VMEM] + [HBM] * n_pix,
        out_specs=[VMEM] * sides,
        scratch_shapes=[pltpu.VMEM((sides, EDGE_SPAN, half, 128), F32), pltpu.SemaphoreType.DMA],
        compiler_params=params(),
        cost_estimate=cost(2.0),
    )(where, dark, *pieces)


def add_lags(older, newer, sums, cross_only=False):
    both = older + newer
    out = []
    for lag in range(1, LAGS + 1):
        total = sums[lag - 1]
        for i in range(lag if cross_only else LAGS):
            total = total + both[LAGS + i] * both[LAGS + i - lag]
        out.append(total)
    return out


def edge_rows(read, last):
    rows = [read(i) for i in range(LAGS)]
    levels = [rows]
    for level in range(1, LEVELS):
        own = [read(LAGS + 8 * (level - 1) + i) for i in range(8)]
        rows = own + pair_sums(rows) if last else pair_sums(rows) + own
        levels.append(rows)
    return levels


def sums_kernel(kind, span, n_tm, per, n_pix, taken, where_ref, dark_ref, *refs):
    refs = list(refs)
    halo_ref = refs.pop(0) if kind != "full" else None
    before_ref = refs.pop(0) if taken else None
    pieces, rest = refs[:n_pix], refs[n_pix:]
    outs, (series, up_one, up_two, up_three, flat, totals, gathered, sems) = rest[:-8], rest[-8:]
    rows = pieces[0].shape[0]
    length = rows * n_pix
    begin, groups = span
    for group in range(groups):
        for other in range(n_pix):
            pltpu.make_async_copy(
                pieces[other].at[:, pl.ds((begin + group) * 8, 8), :],
                series.at[pl.ds((where_ref[0] ^ other) * rows, rows), pl.ds(group * 8, 8), :],
                sems.at[group],
            ).start()
    zero = jnp.zeros((8, 128), F32)
    stores = (up_one, up_two, up_three, None)
    width = 8 // n_tm
    inner = lax.broadcasted_iota(jnp.int32, (8, 128), 0) < 8 - width

    @pl.loop(0, groups)
    def _(group):
        lanes = pl.ds(pl.multiple_of(group * 8, 8), 8)
        whole = series.at[:, lanes, :]
        pltpu.make_async_copy(whole, whole, sems.at[group]).wait()
        dark = dark_ref[pl.ds(pl.multiple_of((begin + group) * 8, 8), 8), :]
        if kind != "full":
            halo = edge_rows(lambda i: halo_ref[group + (begin if halo_ref.shape[0] > groups else 0), i], kind == "up")
        total = zero
        for level in range(LEVELS):
            steps = (length >> level) // LAGS
            store = stores[level]
            source = None if level == 0 else stores[level - 1]

            def read(at, source=source):
                return series[at, lanes, :] - dark if source is None else source[at]

            def step(index, carry, read=read, level=level, store=store):
                older, sums, total = carry
                newer = [read(index * LAGS + i) for i in range(LAGS)]
                pairs = pair_sums(newer)
                if store is not None:
                    for i in range(LAGS // 2):
                        store[index * (LAGS // 2) + i] = pairs[i]
                if level == 0:
                    while len(pairs) > 1:
                        pairs = pair_sums(pairs)
                    total = total + pairs[0]
                return newer, add_lags(older, newer, sums), total

            before = halo[level] if kind == "up" else [zero] * LAGS
            older, sums, total = lax.fori_loop(0, steps, step, (before, [zero] * LAGS, total))
            if kind == "full":
                after_rows = [jnp.where(inner, pltpu.roll(read(i), 8 - width, 0), 0.0) for i in range(LAGS)]
                sums = add_lags(older, after_rows, sums, cross_only=True)
            elif kind == "down":
                sums = add_lags(older, halo[level], sums, cross_only=True)
            for lag in range(LAGS):
                flat[group, pl.ds(level * LAGS + lag, 8, stride=ROWS), :] = sums[lag]
        totals[group] = total

    owners = gathered.shape[0]
    for owner in range(owners):
        if owner < taken:
            gathered[owner] = before_ref[owner]
            continue
        gathered[owner, per * ROWS :, :] = jnp.zeros((gathered.shape[1] - per * ROWS, 128), F32)
        for at in range(per):
            if kind == "full":
                blocks = [at // width * 8 + m * width + at % width for m in range(n_tm)]
            else:
                blocks = [(owner - taken) * per + at]
            gathered[owner, at * ROWS : (at + 1) * ROWS, :] = sum(
                flat[block // 8, block % 8 * ROWS : (block % 8 + 1) * ROWS, :] for block in blocks
            )
            gathered[owner, per * ROWS + at : per * ROWS + at + 1, :] = sum(
                totals[block // 8, block % 8 : block % 8 + 1, :] for block in blocks
            )

    for side, out in enumerate(outs):
        if len(outs) == 1:
            out[...] = gathered[...]
        elif out.shape[0] == 1 and len(outs) == owners > 2:
            out[0] = gathered[where_ref[1] ^ side]
        else:
            for owner in range(owners // 2):
                out[owner] = gathered[2 * owner + ((where_ref[1] & 1) ^ side)]


def sum_rows(per):
    return per * ROWS + (per + 7) // 8 * 8


def sums_part(where, pieces, dark, halo, before, split, kind, span, per, n_tm):
    n_pix = len(pieces)
    rows = pieces[0].shape[0]
    length = n_pix * rows
    groups = span[1]
    owners = groups * 8 // per
    taken = 0 if before is None else before.shape[0]
    if kind == "full":
        outs = [shape(1, sum_rows(per), 128)]
    else:
        outs = [shape((owners + taken) // split, sum_rows(per), 128)] * split
    extra = ([] if halo is None else [halo]) + ([] if before is None else [before])
    return pl.pallas_call(
        functools.partial(sums_kernel, kind, span, n_tm, per, n_pix, taken),
        out_shape=outs,
        in_specs=[SMEM, VMEM] + [VMEM] * len(extra) + [HBM] * n_pix,
        out_specs=[VMEM] * len(outs),
        scratch_shapes=[
            pltpu.VMEM((length, groups * 8, 128), F32),
            pltpu.VMEM((length // 2, 8, 128), F32),
            pltpu.VMEM((length // 4, 8, 128), F32),
            pltpu.VMEM((length // 8, 8, 128), F32),
            pltpu.VMEM((groups, 8 * ROWS, 128), F32),
            pltpu.VMEM((groups, 8, 128), F32),
            pltpu.VMEM((1 if kind == "full" else owners + taken, sum_rows(per), 128), F32),
            pltpu.SemaphoreType.DMA((groups,)),
        ],
        compiler_params=params(),
        cost_estimate=cost(1.0 + 3.0 * length * groups / 256),
    )(where, dark, *extra, *pieces)


def add_kernel(step, where_ref, *refs):
    inputs, (keep_ref, send_ref) = refs[:-2], refs[-2:]
    pairs = list(zip(inputs[0::2], inputs[1::2]))
    low = ((where_ref[1] >> step) & 1) == 0
    sums = [(mine, got, i) for mine, got in pairs for i in range(mine.shape[0])]
    for owner in range(keep_ref.shape[0]):
        first, second = [mine[i] + got[i] for mine, got, i in sums[2 * owner : 2 * owner + 2]]
        keep_ref[owner] = jnp.where(low, first, second)
        send_ref[owner] = jnp.where(low, second, first)


def add_part(where, pairs, step):
    total = sum(mine.shape[0] for mine, _ in pairs)
    half = shape(total // 2, *pairs[0][0].shape[1:])
    flat = [value for pair in pairs for value in pair]
    return pl.pallas_call(
        functools.partial(add_kernel, step),
        out_shape=[half, half],
        in_specs=[SMEM] + [VMEM] * len(flat),
        out_specs=[VMEM, VMEM],
        compiler_params=params(),
        cost_estimate=cost(0.5),
    )(where, *flat)


def finish_kernel(parts, resp_ref, keep_ref, *refs):
    sums_refs, (g2_ref, mean_ref) = refs[:-2], refs[-2:]
    row = lax.broadcasted_iota(jnp.int32, (ROWS, 128), 0)
    level, lag = row // LAGS, row % LAGS + 1
    counts = (((FRAMES >> level) - lag) << (2 * level)).astype(F32)
    for start, per, terms in parts:
        mine, sums_refs = sums_refs[:terms], sums_refs[terms:]
        for at in range(per):
            product = sum(ref[0, at * ROWS : (at + 1) * ROWS, :] for ref in mine)
            total = sum(ref[0, per * ROWS + at : per * ROWS + at + 1, :] for ref in mine)
            block = start + at
            keep = keep_ref[block : block + 1, :]
            mean = total * (1.0 / FRAMES)
            g2_ref[:, block * 128 : (block + 1) * 128] = product / (counts * mean * mean) * keep
            mean_ref[block : block + 1, :] = mean / resp_ref[block : block + 1, :] * keep


class Box:
    def __init__(self, value):
        self.value = value


def unbox(got):
    return [got[k].value for k in range(len(got))]


def send(value, axis, pairs, *before):
    for box in before:
        value, box.value = lax.optimization_barrier((value, box.value))
    return Box(lax.ppermute(value, axis, pairs))


def swap(value, axis, other, *before):
    return send(value, axis, [(i, i ^ other) for i in range(lax.axis_size(axis))], *before)


class Line:
    def __init__(self, where):
        self.where = where

    def __call__(self, part, *args):
        outs = part(self.where, *args)
        outs, self.where = lax.optimization_barrier((outs, self.where))
        return outs

    def hold(self, value):
        value, self.where = lax.optimization_barrier((value, self.where))
        return value

    def follow(self, box):
        self.where, box.value = lax.optimization_barrier((self.where, box.value))


def body(raw_frames, frame_order, owner_map, pixel_mask, dark, flat, polarization, solid_angle):
    n_pix = lax.axis_size("pix")
    n_tm = lax.axis_size("tm")
    n_blocks = owner_map.shape[0]
    owned = n_blocks // n_pix
    share = owned // n_tm
    width = 8 // n_tm

    plan = []
    shifts = []
    start = 0
    for kind, eighths in PARTS:
        per = share * eighths // 8
        plan.append((kind, start, per))
        if kind == "seg":
            shifts += [(False, g * share + start + j) for g in range(n_tm) for j in range(per)]
        else:
            shifts += [
                (True, start + unit * width + j) for unit in range(per // width) for _ in range(n_tm) for j in range(width)
            ]
        start += per

    where = jnp.stack([lax.axis_index("pix"), lax.axis_index("tm")]).astype(jnp.int32)
    sizes = (owned, share, n_pix, n_tm)
    pack = functools.partial(pack_parts, raw_frames, frame_order, owner_map)
    (first, second, full) = plan
    line = Line(where)

    far = list(range(n_pix - 1, 1, -1))
    ahead, behind = far[0::2], far[1::2]
    chain = [k for k in range(2, n_tm)]
    others = chain + [1, 0]

    early, late = [1] + ahead, far[1::2] + [0]
    mine = dict(zip(early, line(pack, [first + (early,)], *sizes)))
    got_first = {k: swap(mine[k], "pix", k) for k in early}
    line.follow(got_first[1])
    raw = dict(zip(others, line(pack, [full + (others,)], *sizes)))
    got_full = {0: Box(raw[0]), 1: swap(raw[1], "tm", 1)}
    for at, k in enumerate(chain):
        got_full[k] = swap(raw[k], "tm", k, *[got_full[j] for j in chain[:at][-1:]])
    mine.update(zip(late, line(pack, [first + (late,)], *sizes)))
    got_first[0] = Box(mine[0])
    for at, k in enumerate(late[:-1]):
        also = [got_full[chain[0]]] if at == 2 else []
        got_first[k] = swap(mine[k], "pix", k, got_first[k + 1], *also)

    order = ahead + behind + [1, 0]
    mine = dict(zip(order, line(pack, [second + (order,)], *sizes)))
    got_second = {0: Box(mine[0]), 1: swap(mine[1], "pix", 1, got_first[1])}
    for k in ahead:
        also = [got_second[1]] + [got_full[j] for j in [1] + chain[1:]] if k == ahead[-1] else []
        got_second[k] = swap(mine[k], "pix", k, got_first[k - 1], *also)

    dark_own, resp_own, keep_own = line(
        constants_part, owner_map, dark, flat, polarization, solid_angle, pixel_mask, shifts, owned, share
    )
    darks = []
    used = 0
    for _, _, per in plan:
        darks.append(dark_own[used : used + n_tm * per])
        used += n_tm * per

    upward = [(i, i + 1) for i in range(n_tm - 1)]
    ways = (upward, [(j, i) for i, j in upward])

    def halos(got, dark_part, sides):
        return [send(edge, "tm", way) for edge, way in zip(line(edge_part, unbox(got), dark_part, sides), ways)]

    def sums(got, dark_part, halo, before, split, kind, span, per):
        halo = None if halo is None else halo.value
        return line(sums_part, unbox(got), dark_part, halo, before, split, kind, span, per, n_tm)

    def reduce(pairs):
        for step in range(1, n_tm.bit_length() - 1):
            keep, away = line(add_part, [(mine, box.value) for mine, box in pairs], step)
            pairs = [(keep, swap(away, "tm", 1 << step))]
        return pairs

    halo = halos(got_first, darks[0], 2)
    half = n_tm * first[2] // 16
    turned = line(turn_part, unbox(got_full), n_pix, n_tm)
    keep, away = sums(got_first, darks[0], halo[0], None, 2, "up", (0, half), first[2])
    pairs = [(keep, swap(away, "tm", 1))]
    for k in ahead:
        line.follow(got_second[k])
    for k in behind:
        got_second[k] = swap(mine[k], "pix", k, got_second[k + 1])
    keep, away = sums(got_first, darks[0], halo[1], None, 2, "down", (half, half), first[2])
    pairs.append((keep, swap(away, "tm", 1)))

    got_full = {0: Box(turned[0]), 1: swap(turned[1], "pix", 1, got_second[1])}
    for k in ahead:
        also = [got_full[1]] if k == ahead[0] else []
        got_full[k] = swap(line.hold(turned[k]), "pix", k, got_second[k - 1], *also)
    (halo,) = halos(got_second, darks[1], 1)
    terms = [list(pair) for pair in reduce(pairs)]
    half = n_tm * second[2] // 16
    (before,) = sums(got_second, darks[1], halo, None, 1, "up", (0, half), second[2])
    for k in ahead:
        line.follow(got_full[k])
    for k in behind:
        got_full[k] = swap(turned[k], "pix", k, got_full[k + 1])
    mine = sums(got_second, darks[1], halo, before, n_tm, "up", (half, half), second[2])
    terms.append([mine[0]] + [swap(mine[k], "tm", k) for k in chain + [1]])
    terms = [[value.value if isinstance(value, Box) else value for value in part] for part in terms]
    terms.append(sums(got_full, darks[2], None, None, 1, "full", (0, n_tm * full[2] // 8), full[2]))

    g2, mean = pl.pallas_call(
        functools.partial(
            finish_kernel, [(start, per, len(part)) for (_, start, per), part in zip(plan, terms)]
        ),
        out_shape=[shape(ROWS, share * 128), shape(share, 128)],
        in_specs=[VMEM] * (2 + sum(len(part) for part in terms)),
        out_specs=[VMEM, VMEM],
        compiler_params=params(),
        cost_estimate=cost(1.0),
    )(resp_own, keep_own, *[value for part in terms for value in part])
    return g2.reshape(LEVELS, LAGS, share * 128), mean.reshape(share * 128)


def solution(mesh):
    return jax.shard_map(
        body,
        mesh=mesh,
        in_specs=(P(("tm", "pix"), None), P(("tm", "pix")), P(), P(), P(), P(), P(), P()),
        out_specs=(P(None, None, ("pix", "tm")), P(("pix", "tm"))),
        check_vma=False,
    )
```

```python
import functools

import jax
import jax.numpy as jnp
from jax import lax
from jax.experimental import pallas as pl
from jax.experimental.pallas import tpu as pltpu
from jax.sharding import PartitionSpec as P

FRAMES = 1024
LAGS = 16
LEVELS = 4
ROWS = LEVELS * LAGS
EDGE = LAGS + 8 * (LEVELS - 1)
EDGE_SPAN = LAGS << (LEVELS - 1)

PARTS = (("seg", 4), ("seg", 2), ("full", 2))

SMEM = pl.BlockSpec(memory_space=pltpu.SMEM)
VMEM = pl.BlockSpec(memory_space=pltpu.VMEM)
HBM = pl.BlockSpec(memory_space=pl.ANY)
F32 = jnp.float32


def params():
    return pltpu.CompilerParams(vmem_limit_bytes=40 << 20)


def cost(micros):
    return pl.CostEstimate(flops=0, bytes_accessed=int(micros * 3.6e6), transcendentals=0)


def shape(*dims):
    return jax.ShapeDtypeStruct(dims, F32)


def pack_kernel(jobs, owned, share, n_pix, n_tm, where_ref, order_ref, owner_ref, frames_ref, *refs):
    outs, inverse = refs[:-1], refs[-1]
    rows = frames_ref.shape[0]
    pix, tm = where_ref[0], where_ref[1]
    for i in range(rows):
        inverse[order_ref[i]] = i

    def eight(position_of, store):
        blocks = [owner_ref[position_of(i)] for i in range(8)]
        for high in range(rows // 8):
            tiles = [
                frames_ref[high * 8 : high * 8 + 8, pl.ds(pl.multiple_of(block * 128, 128), 128)] for block in blocks
            ]
            turned = jnp.swapaxes(jnp.stack(tiles), 0, 1)
            for low in range(8):
                store(inverse[high * 8 + low], turned[low])

    taken = 0
    for kind, start, per, others in jobs:
        if kind == "seg":
            for at, other in enumerate(others):
                out = outs[taken + at]
                base = (pix ^ other) * owned + start

                @pl.loop(0, out.shape[1] // 8)
                def _(group, out=out, base=base, per=per):
                    def position_of(i):
                        pos = group * 8 + i
                        return base + (pos // per) * share + pos % per

                    def store(row, value):
                        out[row, pl.ds(pl.multiple_of(group * 8, 8), 8), :] = value

                    eight(position_of, store)

            taken += len(others)
        else:
            width = 8 // n_tm
            for at, other in enumerate(others):
                out = outs[taken + at]
                base = (tm ^ other) * share + start

                @pl.loop(0, out.shape[0] * out.shape[1])
                def _(at, out=out, base=base, width=width):
                    unit, group = at // out.shape[1], at % out.shape[1]

                    def position_of(i):
                        pos = group * 8 + i
                        return base + (pos // width) * owned + unit * width + pos % width

                    def store(row, value):
                        out[unit, group, row] = value

                    eight(position_of, store)

            taken += len(others)


def pack_parts(raw_frames, frame_order, owner_map, where, jobs, owned, share, n_pix, n_tm):
    rows = raw_frames.shape[0]
    outs = []
    size = 0
    for kind, _, per, others in jobs:
        if kind == "seg":
            outs += [shape(rows, n_tm * per, 128)] * len(others)
            size += per * len(others) / n_pix
        else:
            width = 8 // n_tm
            outs += [shape(per // width, n_pix * width // 8, rows, 8, 128)] * len(others)
            size += per
    return pl.pallas_call(
        functools.partial(pack_kernel, jobs, owned, share, n_pix, n_tm),
        out_shape=outs,
        in_specs=[SMEM, SMEM, SMEM, VMEM],
        out_specs=[VMEM] * len(outs),
        scratch_shapes=[pltpu.SMEM((rows,), jnp.int32)],
        compiler_params=params(),
        cost_estimate=cost(1.0 + 8.0 * size / share),
    )(where, frame_order, owner_map, raw_frames)


def turn_kernel(n_pix, n_tm, where_ref, *refs):
    pieces, outs, (held, staged, sem) = refs[:n_tm], refs[n_tm : n_tm + n_pix], refs[n_tm + n_pix :]
    units, groups, rows = pieces[0].shape[:3]
    width = 8 // n_tm
    for other in range(n_tm):
        pltpu.make_async_copy(pieces[other], held.at[where_ref[1] ^ other], sem).start()
    pltpu.make_async_copy(held, held, sem).wait()
    place = lax.broadcasted_iota(jnp.int32, (8, 128), 0) // width

    @pl.loop(0, rows)
    def _(row):
        for unit in range(units):
            for group in range(groups):
                got = [held[m, unit, group, row] for m in range(n_tm)]
                for to in range(n_tm):
                    value = got[to]
                    for m in range(n_tm):
                        if m != to:
                            value = jnp.where(place == m, pltpu.roll(got[m], (m - to) * width % 8, 0), value)
                    staged[group * n_tm + to, row, unit * 8 : unit * 8 + 8, :] = value

    for other in range(n_pix):
        outs[other][...] = staged[where_ref[0] ^ other]


def turn_part(where, pieces, n_pix, n_tm):
    units, groups, rows = pieces[0].shape[:3]
    return pl.pallas_call(
        functools.partial(turn_kernel, n_pix, n_tm),
        out_shape=[shape(rows, units * 8, 128)] * n_pix,
        in_specs=[SMEM] + [HBM] * n_tm,
        out_specs=[VMEM] * n_pix,
        scratch_shapes=[
            pltpu.VMEM((n_tm,) + pieces[0].shape, F32),
            pltpu.VMEM((n_pix, rows, units * 8, 128), F32),
            pltpu.SemaphoreType.DMA,
        ],
        compiler_params=params(),
        cost_estimate=cost(3.0),
    )(where, *pieces)


def constants_kernel(
    plan, owned, share, where_ref, owner_ref, dark_ref, flat_ref, pol_ref, solid_ref, mask_ref, dark_out, resp_out, keep_out
):
    base = where_ref[0] * owned
    mine = base + where_ref[1] * share
    for at, (from_mine, shift) in enumerate(plan):
        row = pl.ds(owner_ref[(mine if from_mine else base) + shift], 1)
        dark_out[at : at + 1, :] = dark_ref[row, :]
    for at in range(share):
        row = pl.ds(owner_ref[mine + at], 1)
        resp_out[at : at + 1, :] = flat_ref[row, :] * pol_ref[row, :] * solid_ref[row, :]
        keep_out[at : at + 1, :] = mask_ref[row, :].astype(F32)


def constants_part(where, owner_map, dark, flat, polarization, solid_angle, pixel_mask, shifts, owned, share):
    n_blocks = owner_map.shape[0]
    tables = [t.reshape(n_blocks, 128) for t in (dark, flat, polarization, solid_angle, pixel_mask)]
    return pl.pallas_call(
        functools.partial(constants_kernel, shifts, owned, share),
        out_shape=[shape(owned, 128), shape(share, 128), shape(share, 128)],
        in_specs=[SMEM, SMEM] + [VMEM] * 5,
        out_specs=[VMEM] * 3,
        compiler_params=params(),
        cost_estimate=cost(1.0),
    )(where, owner_map, *tables)


def pair_sums(rows):
    return [rows[2 * i] + rows[2 * i + 1] for i in range(len(rows) // 2)]


def edge_kernel(n_pix, where_ref, dark_ref, *refs):
    pieces, outs, (held, sem) = refs[:n_pix], refs[n_pix:-2], refs[-2:]
    rows = pieces[0].shape[0]
    blocks = EDGE_SPAN // rows
    half = held.shape[2]
    for other in range(n_pix):
        source = where_ref[0] ^ other
        for side, first in ((0, n_pix - blocks), (1, 0))[: len(outs)]:

            @pl.when((source >= first) & (source < first + blocks))
            def _(other=other, source=source, side=side, first=first):
                pltpu.make_async_copy(
                    pieces[other].at[:, pl.ds(side * half, half), :],
                    held.at[side, pl.ds((source - first) * rows, rows)],
                    sem,
                ).start()

    pltpu.make_async_copy(held, held, sem).wait()

    for side, out_ref in enumerate(outs):

        @pl.loop(0, half // 8)
        def _(group, side=side, out_ref=out_ref):
            lanes = pl.ds(pl.multiple_of(group * 8, 8), 8)
            dark = dark_ref[pl.ds(pl.multiple_of(group * 8 + side * half, 8), 8), :]
            span = 0
            for level in range(LEVELS):
                count = LAGS if level == 0 else LAGS // 2
                width = 1 << level
                begin = span if side else EDGE_SPAN - span - count * width
                for i in range(count):
                    at = begin + i * width
                    got = [held[side, at + j, lanes, :] - dark for j in range(width)]
                    while len(got) > 1:
                        got = pair_sums(got)
                    out_ref[group, (LAGS + 8 * (level - 1) if level else 0) + i] = got[0]
                span += count * width


def edge_part(where, pieces, dark, sides):
    n_pix = len(pieces)
    half = pieces[0].shape[1] // sides
    return pl.pallas_call(
        functools.partial(edge_kernel, n_pix),
        out_shape=[shape(half // 8, EDGE, 8, 128)] * sides,
        in_specs=[SMEM, VMEM] + [HBM] * n_pix,
        out_specs=[VMEM] * sides,
        scratch_shapes=[pltpu.VMEM((sides, EDGE_SPAN, half, 128), F32), pltpu.SemaphoreType.DMA],
        compiler_params=params(),
        cost_estimate=cost(2.0),
    )(where, dark, *pieces)


def add_lags(older, newer, sums, cross_only=False):
    both = older + newer
    out = []
    for lag in range(1, LAGS + 1):
        total = sums[lag - 1]
        for i in range(lag if cross_only else LAGS):
            total = total + both[LAGS + i] * both[LAGS + i - lag]
        out.append(total)
    return out


def edge_rows(read, last):
    rows = [read(i) for i in range(LAGS)]
    levels = [rows]
    for level in range(1, LEVELS):
        own = [read(LAGS + 8 * (level - 1) + i) for i in range(8)]
        rows = own + pair_sums(rows) if last else pair_sums(rows) + own
        levels.append(rows)
    return levels


def sums_kernel(kind, span, n_tm, per, n_pix, taken, where_ref, dark_ref, *refs):
    refs = list(refs)
    halo_ref = refs.pop(0) if kind != "full" else None
    before_ref = refs.pop(0) if taken else None
    pieces, rest = refs[:n_pix], refs[n_pix:]
    outs, (series, up_one, up_two, up_three, flat, totals, gathered, sems) = rest[:-8], rest[-8:]
    rows = pieces[0].shape[0]
    length = rows * n_pix
    begin, groups = span
    for group in range(groups):
        for other in range(n_pix):
            pltpu.make_async_copy(
                pieces[other].at[:, pl.ds((begin + group) * 8, 8), :],
                series.at[pl.ds((where_ref[0] ^ other) * rows, rows), pl.ds(group * 8, 8), :],
                sems.at[group],
            ).start()
    zero = jnp.zeros((8, 128), F32)
    stores = (up_one, up_two, up_three, None)
    width = 8 // n_tm
    inner = lax.broadcasted_iota(jnp.int32, (8, 128), 0) < 8 - width

    @pl.loop(0, groups)
    def _(group):
        lanes = pl.ds(pl.multiple_of(group * 8, 8), 8)
        whole = series.at[:, lanes, :]
        pltpu.make_async_copy(whole, whole, sems.at[group]).wait()
        dark = dark_ref[pl.ds(pl.multiple_of((begin + group) * 8, 8), 8), :]
        if kind != "full":
            halo = edge_rows(lambda i: halo_ref[group + (begin if halo_ref.shape[0] > groups else 0), i], kind == "up")
        total = zero
        for level in range(LEVELS):
            steps = (length >> level) // LAGS
            store = stores[level]
            source = None if level == 0 else stores[level - 1]

            def read(at, source=source):
                return series[at, lanes, :] - dark if source is None else source[at]

            def step(index, carry, read=read, level=level, store=store):
                older, sums, total = carry
                newer = [read(index * LAGS + i) for i in range(LAGS)]
                pairs = pair_sums(newer)
                if store is not None:
                    for i in range(LAGS // 2):
                        store[index * (LAGS // 2) + i] = pairs[i]
                if level == 0:
                    while len(pairs) > 1:
                        pairs = pair_sums(pairs)
                    total = total + pairs[0]
                return newer, add_lags(older, newer, sums), total

            before = halo[level] if kind == "up" else [zero] * LAGS
            older, sums, total = lax.fori_loop(0, steps, step, (before, [zero] * LAGS, total))
            if kind == "full":
                after_rows = [jnp.where(inner, pltpu.roll(read(i), 8 - width, 0), 0.0) for i in range(LAGS)]
                sums = add_lags(older, after_rows, sums, cross_only=True)
            elif kind == "down":
                sums = add_lags(older, halo[level], sums, cross_only=True)
            for lag in range(LAGS):
                flat[group, pl.ds(level * LAGS + lag, 8, stride=ROWS), :] = sums[lag]
        totals[group] = total

    owners = gathered.shape[0]
    for owner in range(owners):
        if owner < taken:
            gathered[owner] = before_ref[owner]
            continue
        gathered[owner, per * ROWS :, :] = jnp.zeros((gathered.shape[1] - per * ROWS, 128), F32)
        for at in range(per):
            if kind == "full":
                blocks = [at // width * 8 + m * width + at % width for m in range(n_tm)]
            else:
                blocks = [(owner - taken) * per + at]
            gathered[owner, at * ROWS : (at + 1) * ROWS, :] = sum(
                flat[block // 8, block % 8 * ROWS : (block % 8 + 1) * ROWS, :] for block in blocks
            )
            gathered[owner, per * ROWS + at : per * ROWS + at + 1, :] = sum(
                totals[block // 8, block % 8 : block % 8 + 1, :] for block in blocks
            )

    for side, out in enumerate(outs):
        if len(outs) == 1:
            out[...] = gathered[...]
        elif out.shape[0] == 1 and len(outs) == owners > 2:
            out[0] = gathered[where_ref[1] ^ side]
        else:
            for owner in range(owners // 2):
                out[owner] = gathered[2 * owner + ((where_ref[1] & 1) ^ side)]


def sum_rows(per):
    return per * ROWS + (per + 7) // 8 * 8


def sums_part(where, pieces, dark, halo, before, split, kind, span, per, n_tm):
    n_pix = len(pieces)
    rows = pieces[0].shape[0]
    length = n_pix * rows
    groups = span[1]
    owners = groups * 8 // per
    taken = 0 if before is None else before.shape[0]
    if kind == "full":
        outs = [shape(1, sum_rows(per), 128)]
    else:
        outs = [shape((owners + taken) // split, sum_rows(per), 128)] * split
    extra = ([] if halo is None else [halo]) + ([] if before is None else [before])
    return pl.pallas_call(
        functools.partial(sums_kernel, kind, span, n_tm, per, n_pix, taken),
        out_shape=outs,
        in_specs=[SMEM, VMEM] + [VMEM] * len(extra) + [HBM] * n_pix,
        out_specs=[VMEM] * len(outs),
        scratch_shapes=[
            pltpu.VMEM((length, groups * 8, 128), F32),
            pltpu.VMEM((length // 2, 8, 128), F32),
            pltpu.VMEM((length // 4, 8, 128), F32),
            pltpu.VMEM((length // 8, 8, 128), F32),
            pltpu.VMEM((groups, 8 * ROWS, 128), F32),
            pltpu.VMEM((groups, 8, 128), F32),
            pltpu.VMEM((1 if kind == "full" else owners + taken, sum_rows(per), 128), F32),
            pltpu.SemaphoreType.DMA((groups,)),
        ],
        compiler_params=params(),
        cost_estimate=cost(1.0 + 3.0 * length * groups / 256),
    )(where, dark, *extra, *pieces)


def add_kernel(step, where_ref, *refs):
    inputs, (keep_ref, send_ref) = refs[:-2], refs[-2:]
    pairs = list(zip(inputs[0::2], inputs[1::2]))
    low = ((where_ref[1] >> step) & 1) == 0
    sums = [(mine, got, i) for mine, got in pairs for i in range(mine.shape[0])]
    for owner in range(keep_ref.shape[0]):
        first, second = [mine[i] + got[i] for mine, got, i in sums[2 * owner : 2 * owner + 2]]
        keep_ref[owner] = jnp.where(low, first, second)
        send_ref[owner] = jnp.where(low, second, first)


def add_part(where, pairs, step):
    total = sum(mine.shape[0] for mine, _ in pairs)
    half = shape(total // 2, *pairs[0][0].shape[1:])
    flat = [value for pair in pairs for value in pair]
    return pl.pallas_call(
        functools.partial(add_kernel, step),
        out_shape=[half, half],
        in_specs=[SMEM] + [VMEM] * len(flat),
        out_specs=[VMEM, VMEM],
        compiler_params=params(),
        cost_estimate=cost(0.5),
    )(where, *flat)


def finish_kernel(parts, resp_ref, keep_ref, *refs):
    sums_refs, (g2_ref, mean_ref) = refs[:-2], refs[-2:]
    row = lax.broadcasted_iota(jnp.int32, (ROWS, 128), 0)
    level, lag = row // LAGS, row % LAGS + 1
    counts = (((FRAMES >> level) - lag) << (2 * level)).astype(F32)
    for start, per, terms in parts:
        mine, sums_refs = sums_refs[:terms], sums_refs[terms:]
        for at in range(per):
            product = sum(ref[0, at * ROWS : (at + 1) * ROWS, :] for ref in mine)
            total = sum(ref[0, per * ROWS + at : per * ROWS + at + 1, :] for ref in mine)
            block = start + at
            keep = keep_ref[block : block + 1, :]
            mean = total * (1.0 / FRAMES)
            g2_ref[:, block * 128 : (block + 1) * 128] = product / (counts * mean * mean) * keep
            mean_ref[block : block + 1, :] = mean / resp_ref[block : block + 1, :] * keep


class Box:
    def __init__(self, value):
        self.value = value


def unbox(got):
    return [got[k].value for k in range(len(got))]


def send(value, axis, pairs, *before):
    for box in before:
        value, box.value = lax.optimization_barrier((value, box.value))
    return Box(lax.ppermute(value, axis, pairs))


def swap(value, axis, other, *before):
    return send(value, axis, [(i, i ^ other) for i in range(lax.axis_size(axis))], *before)


class Line:
    def __init__(self, where):
        self.where = where

    def __call__(self, part, *args):
        outs = part(self.where, *args)
        outs, self.where = lax.optimization_barrier((outs, self.where))
        return outs

    def hold(self, value):
        value, self.where = lax.optimization_barrier((value, self.where))
        return value

    def follow(self, box):
        self.where, box.value = lax.optimization_barrier((self.where, box.value))


def body(raw_frames, frame_order, owner_map, pixel_mask, dark, flat, polarization, solid_angle):
    n_pix = lax.axis_size("pix")
    n_tm = lax.axis_size("tm")
    n_blocks = owner_map.shape[0]
    owned = n_blocks // n_pix
    share = owned // n_tm
    width = 8 // n_tm

    plan = []
    shifts = []
    start = 0
    for kind, eighths in PARTS:
        per = share * eighths // 8
        plan.append((kind, start, per))
        if kind == "seg":
            shifts += [(False, g * share + start + j) for g in range(n_tm) for j in range(per)]
        else:
            shifts += [
                (True, start + unit * width + j) for unit in range(per // width) for _ in range(n_tm) for j in range(width)
            ]
        start += per

    where = jnp.stack([lax.axis_index("pix"), lax.axis_index("tm")]).astype(jnp.int32)
    sizes = (owned, share, n_pix, n_tm)
    pack = functools.partial(pack_parts, raw_frames, frame_order, owner_map)
    (first, second, full) = plan
    line = Line(where)

    far = list(range(n_pix - 1, 1, -1))
    ahead, behind = far[0::2], far[1::2]
    chain = [k for k in range(2, n_tm)]
    others = chain + [1, 0]

    early, late = [1] + ahead, far[1::2] + [0]
    mine = dict(zip(early, line(pack, [first + (early,)], *sizes)))
    got_first = {k: swap(mine[k], "pix", k) for k in early}
    line.follow(got_first[1])
    raw = dict(zip(others, line(pack, [full + (others,)], *sizes)))
    got_full = {0: Box(raw[0]), 1: swap(raw[1], "tm", 1)}
    for at, k in enumerate(chain):
        got_full[k] = swap(raw[k], "tm", k, *[got_full[j] for j in chain[:at][-1:]])
    mine.update(zip(late, line(pack, [first + (late,)], *sizes)))
    got_first[0] = Box(mine[0])
    for k in late[:-1]:
        got_first[k] = swap(mine[k], "pix", k, got_first[k + 1])

    order = ahead + behind + [1, 0]
    mine = dict(zip(order, line(pack, [second + (order,)], *sizes)))
    got_second = {0: Box(mine[0]), 1: swap(mine[1], "pix", 1, got_first[1])}
    for k in ahead:
        also = [got_second[1]] + [got_full[j] for j in [1] + chain[1:]] if k == ahead[-1] else []
        got_second[k] = swap(mine[k], "pix", k, got_first[k - 1], *also)

    dark_own, resp_own, keep_own = line(
        constants_part, owner_map, dark, flat, polarization, solid_angle, pixel_mask, shifts, owned, share
    )
    darks = []
    used = 0
    for _, _, per in plan:
        darks.append(dark_own[used : used + n_tm * per])
        used += n_tm * per

    upward = [(i, i + 1) for i in range(n_tm - 1)]
    ways = (upward, [(j, i) for i, j in upward])

    def halos(got, dark_part, sides):
        return [send(edge, "tm", way) for edge, way in zip(line(edge_part, unbox(got), dark_part, sides), ways)]

    def sums(got, dark_part, halo, before, split, kind, span, per):
        halo = None if halo is None else halo.value
        return line(sums_part, unbox(got), dark_part, halo, before, split, kind, span, per, n_tm)

    def reduce(pairs):
        for step in range(1, n_tm.bit_length() - 1):
            keep, away = line(add_part, [(mine, box.value) for mine, box in pairs], step)
            pairs = [(keep, swap(away, "tm", 1 << step))]
        return pairs

    line.follow(got_second[1])
    line.follow(got_full[1])
    halo = halos(got_first, darks[0], 2)
    half = n_tm * first[2] // 16
    turned = line(turn_part, unbox(got_full), n_pix, n_tm)
    (before,) = sums(got_first, darks[0], halo[0], None, 1, "up", (0, half), first[2])
    for k in ahead:
        line.follow(got_second[k])
    for k in behind:
        got_second[k] = swap(mine[k], "pix", k, got_second[k + 1])
    keep, away = sums(got_first, darks[0], halo[1], before, 2, "down", (half, half), first[2])
    pairs = [(keep, swap(away, "tm", 1))]

    got_full = {0: Box(turned[0]), 1: swap(turned[1], "pix", 1, got_second[1])}
    for k in ahead:
        also = [got_full[1]] if k == ahead[0] else []
        got_full[k] = swap(line.hold(turned[k]), "pix", k, got_second[k - 1], *also)
    (halo,) = halos(got_second, darks[1], 1)
    half = n_tm * second[2] // 16
    (before,) = sums(got_second, darks[1], halo, None, 1, "up", (0, half), second[2])
    terms = [list(pair) for pair in reduce(pairs)]
    for k in ahead:
        line.follow(got_full[k])
    for k in behind:
        got_full[k] = swap(turned[k], "pix", k, got_full[k + 1])
    mine = sums(got_second, darks[1], halo, before, n_tm, "up", (half, half), second[2])
    terms.append([mine[0]] + [swap(mine[k], "tm", k) for k in chain + [1]])
    terms = [[value.value if isinstance(value, Box) else value for value in part] for part in terms]
    terms.append(sums(got_full, darks[2], None, None, 1, "full", (0, n_tm * full[2] // 8), full[2]))

    g2, mean = pl.pallas_call(
        functools.partial(
            finish_kernel, [(start, per, len(part)) for (_, start, per), part in zip(plan, terms)]
        ),
        out_shape=[shape(ROWS, share * 128), shape(share, 128)],
        in_specs=[VMEM] * (2 + sum(len(part) for part in terms)),
        out_specs=[VMEM, VMEM],
        compiler_params=params(),
        cost_estimate=cost(1.0),
    )(resp_own, keep_own, *[value for part in terms for value in part])
    return g2.reshape(LEVELS, LAGS, share * 128), mean.reshape(share * 128)


def solution(mesh):
    return jax.shard_map(
        body,
        mesh=mesh,
        in_specs=(P(("tm", "pix"), None), P(("tm", "pix")), P(), P(), P(), P(), P(), P()),
        out_specs=(P(None, None, ("pix", "tm")), P(("pix", "tm"))),
        check_vma=False,
    )
```

```python
import functools

import jax
import jax.numpy as jnp
from jax import lax
from jax.experimental import pallas as pl
from jax.experimental.pallas import tpu as pltpu
from jax.sharding import PartitionSpec as P

FRAMES = 1024
LAGS = 16
LEVELS = 4
ROWS = LEVELS * LAGS
EDGE = LAGS + 8 * (LEVELS - 1)
EDGE_SPAN = LAGS << (LEVELS - 1)

PARTS = (("seg", 4), ("seg", 2), ("full", 2))

SMEM = pl.BlockSpec(memory_space=pltpu.SMEM)
VMEM = pl.BlockSpec(memory_space=pltpu.VMEM)
HBM = pl.BlockSpec(memory_space=pl.ANY)
F32 = jnp.float32


def params():
    return pltpu.CompilerParams(vmem_limit_bytes=40 << 20)


def cost(micros):
    return pl.CostEstimate(flops=0, bytes_accessed=int(micros * 3.6e6), transcendentals=0)


def shape(*dims):
    return jax.ShapeDtypeStruct(dims, F32)


def pack_kernel(jobs, owned, share, n_pix, n_tm, where_ref, frames_ref, *refs):
    outs, inverse = refs[:-1], refs[-1]
    rows = frames_ref.shape[0]
    pix, tm = where_ref[0], where_ref[1]
    for i in range(rows):
        inverse[where_ref[2 + i]] = i

    def eight(position_of, store):
        blocks = [where_ref[2 + rows + position_of(i)] for i in range(8)]
        for high in range(rows // 8):
            tiles = [
                frames_ref[high * 8 : high * 8 + 8, pl.ds(pl.multiple_of(block * 128, 128), 128)] for block in blocks
            ]
            turned = jnp.swapaxes(jnp.stack(tiles), 0, 1)
            for low in range(8):
                store(inverse[high * 8 + low], turned[low])

    taken = 0
    for kind, start, per, others in jobs:
        if kind == "seg":
            for at, other in enumerate(others):
                out = outs[taken + at]
                base = (pix ^ other) * owned + start

                @pl.loop(0, out.shape[1] // 8)
                def _(group, out=out, base=base, per=per):
                    def position_of(i):
                        pos = group * 8 + i
                        return base + (pos // per) * share + pos % per

                    def store(row, value):
                        out[row, pl.ds(pl.multiple_of(group * 8, 8), 8), :] = value

                    eight(position_of, store)

            taken += len(others)
        else:
            width = 8 // n_tm
            for at, other in enumerate(others):
                out = outs[taken + at]
                base = (tm ^ other) * share + start

                @pl.loop(0, out.shape[0] * out.shape[1])
                def _(at, out=out, base=base, width=width):
                    unit, group = at // out.shape[1], at % out.shape[1]

                    def position_of(i):
                        pos = group * 8 + i
                        return base + (pos // width) * owned + unit * width + pos % width

                    def store(row, value):
                        out[unit, group, row] = value

                    eight(position_of, store)

            taken += len(others)


def pack_parts(raw_frames, where, jobs, owned, share, n_pix, n_tm):
    rows = raw_frames.shape[0]
    outs = []
    size = 0
    for kind, _, per, others in jobs:
        if kind == "seg":
            outs += [shape(rows, n_tm * per, 128)] * len(others)
            size += per * len(others) / n_pix
        else:
            width = 8 // n_tm
            outs += [shape(per // width, n_pix * width // 8, rows, 8, 128)] * len(others)
            size += per
    return pl.pallas_call(
        functools.partial(pack_kernel, jobs, owned, share, n_pix, n_tm),
        out_shape=outs,
        in_specs=[SMEM, VMEM],
        out_specs=[VMEM] * len(outs),
        scratch_shapes=[pltpu.SMEM((rows,), jnp.int32)],
        compiler_params=params(),
        cost_estimate=cost(1.0 + 8.0 * size / share),
    )(where, raw_frames)


def turn_kernel(n_pix, n_tm, where_ref, *refs):
    pieces, outs, (held, staged, sem) = refs[:n_tm], refs[n_tm : n_tm + n_pix], refs[n_tm + n_pix :]
    units, groups, rows = pieces[0].shape[:3]
    width = 8 // n_tm
    for other in range(n_tm):
        pltpu.make_async_copy(pieces[other], held.at[where_ref[1] ^ other], sem).start()
    pltpu.make_async_copy(held, held, sem).wait()
    place = lax.broadcasted_iota(jnp.int32, (8, 128), 0) // width

    @pl.loop(0, rows)
    def _(row):
        for unit in range(units):
            for group in range(groups):
                got = [held[m, unit, group, row] for m in range(n_tm)]
                for to in range(n_tm):
                    value = got[to]
                    for m in range(n_tm):
                        if m != to:
                            value = jnp.where(place == m, pltpu.roll(got[m], (m - to) * width % 8, 0), value)
                    staged[group * n_tm + to, row, unit * 8 : unit * 8 + 8, :] = value

    for other in range(n_pix):
        outs[other][...] = staged[where_ref[0] ^ other]


def turn_part(where, pieces, n_pix, n_tm):
    units, groups, rows = pieces[0].shape[:3]
    return pl.pallas_call(
        functools.partial(turn_kernel, n_pix, n_tm),
        out_shape=[shape(rows, units * 8, 128)] * n_pix,
        in_specs=[SMEM] + [HBM] * n_tm,
        out_specs=[VMEM] * n_pix,
        scratch_shapes=[
            pltpu.VMEM((n_tm,) + pieces[0].shape, F32),
            pltpu.VMEM((n_pix, rows, units * 8, 128), F32),
            pltpu.SemaphoreType.DMA,
        ],
        compiler_params=params(),
        cost_estimate=cost(3.0),
    )(where, *pieces)


def constants_kernel(
    plan, owned, share, skip, where_ref, dark_ref, flat_ref, pol_ref, solid_ref, mask_ref, dark_out, resp_out, keep_out
):
    base = where_ref[0] * owned
    mine = base + where_ref[1] * share
    for at, (from_mine, shift) in enumerate(plan):
        row = pl.ds(where_ref[skip + (mine if from_mine else base) + shift], 1)
        dark_out[at : at + 1, :] = dark_ref[row, :]
    for at in range(share):
        row = pl.ds(where_ref[skip + mine + at], 1)
        resp_out[at : at + 1, :] = flat_ref[row, :] * pol_ref[row, :] * solid_ref[row, :]
        keep_out[at : at + 1, :] = mask_ref[row, :].astype(F32)


def constants_part(where, dark, flat, polarization, solid_angle, pixel_mask, shifts, owned, share, skip):
    n_blocks = where.shape[0] - skip
    tables = [t.reshape(n_blocks, 128) for t in (dark, flat, polarization, solid_angle, pixel_mask)]
    return pl.pallas_call(
        functools.partial(constants_kernel, shifts, owned, share, skip),
        out_shape=[shape(owned, 128), shape(share, 128), shape(share, 128)],
        in_specs=[SMEM] + [VMEM] * 5,
        out_specs=[VMEM] * 3,
        compiler_params=params(),
        cost_estimate=cost(1.0),
    )(where, *tables)


def pair_sums(rows):
    return [rows[2 * i] + rows[2 * i + 1] for i in range(len(rows) // 2)]


def edge_kernel(n_pix, where_ref, dark_ref, *refs):
    pieces, outs, (held, sem) = refs[:n_pix], refs[n_pix:-2], refs[-2:]
    rows = pieces[0].shape[0]
    blocks = EDGE_SPAN // rows
    half = held.shape[2]
    for other in range(n_pix):
        source = where_ref[0] ^ other
        for side, first in ((0, n_pix - blocks), (1, 0))[: len(outs)]:

            @pl.when((source >= first) & (source < first + blocks))
            def _(other=other, source=source, side=side, first=first):
                pltpu.make_async_copy(
                    pieces[other].at[:, pl.ds(side * half, half), :],
                    held.at[side, pl.ds((source - first) * rows, rows)],
                    sem,
                ).start()

    pltpu.make_async_copy(held, held, sem).wait()

    for side, out_ref in enumerate(outs):

        @pl.loop(0, half // 8)
        def _(group, side=side, out_ref=out_ref):
            lanes = pl.ds(pl.multiple_of(group * 8, 8), 8)
            dark = dark_ref[pl.ds(pl.multiple_of(group * 8 + side * half, 8), 8), :]
            span = 0
            for level in range(LEVELS):
                count = LAGS if level == 0 else LAGS // 2
                width = 1 << level
                begin = span if side else EDGE_SPAN - span - count * width
                for i in range(count):
                    at = begin + i * width
                    got = [held[side, at + j, lanes, :] - dark for j in range(width)]
                    while len(got) > 1:
                        got = pair_sums(got)
                    out_ref[group, (LAGS + 8 * (level - 1) if level else 0) + i] = got[0]
                span += count * width


def edge_part(where, pieces, dark, sides):
    n_pix = len(pieces)
    half = pieces[0].shape[1] // sides
    return pl.pallas_call(
        functools.partial(edge_kernel, n_pix),
        out_shape=[shape(half // 8, EDGE, 8, 128)] * sides,
        in_specs=[SMEM, VMEM] + [HBM] * n_pix,
        out_specs=[VMEM] * sides,
        scratch_shapes=[pltpu.VMEM((sides, EDGE_SPAN, half, 128), F32), pltpu.SemaphoreType.DMA],
        compiler_params=params(),
        cost_estimate=cost(2.0),
    )(where, dark, *pieces)


def add_lags(older, newer, sums, cross_only=False):
    both = older + newer
    out = []
    for lag in range(1, LAGS + 1):
        total = sums[lag - 1]
        for i in range(lag if cross_only else LAGS):
            total = total + both[LAGS + i] * both[LAGS + i - lag]
        out.append(total)
    return out


def edge_rows(read, last):
    rows = [read(i) for i in range(LAGS)]
    levels = [rows]
    for level in range(1, LEVELS):
        own = [read(LAGS + 8 * (level - 1) + i) for i in range(8)]
        rows = own + pair_sums(rows) if last else pair_sums(rows) + own
        levels.append(rows)
    return levels


def sums_kernel(kind, span, n_tm, per, n_pix, taken, where_ref, dark_ref, *refs):
    refs = list(refs)
    halo_ref = refs.pop(0) if kind != "full" else None
    before_ref = refs.pop(0) if taken else None
    pieces, rest = refs[:n_pix], refs[n_pix:]
    outs, (series, up_one, up_two, up_three, flat, totals, gathered, sems) = rest[:-8], rest[-8:]
    rows = pieces[0].shape[0]
    length = rows * n_pix
    begin, groups = span
    for group in range(groups):
        for other in range(n_pix):
            pltpu.make_async_copy(
                pieces[other].at[:, pl.ds((begin + group) * 8, 8), :],
                series.at[pl.ds((where_ref[0] ^ other) * rows, rows), pl.ds(group * 8, 8), :],
                sems.at[group],
            ).start()
    zero = jnp.zeros((8, 128), F32)
    stores = (up_one, up_two, up_three, None)
    width = 8 // n_tm
    inner = lax.broadcasted_iota(jnp.int32, (8, 128), 0) < 8 - width

    @pl.loop(0, groups)
    def _(group):
        lanes = pl.ds(pl.multiple_of(group * 8, 8), 8)
        whole = series.at[:, lanes, :]
        pltpu.make_async_copy(whole, whole, sems.at[group]).wait()
        dark = dark_ref[pl.ds(pl.multiple_of((begin + group) * 8, 8), 8), :]
        if kind != "full":
            halo = edge_rows(lambda i: halo_ref[group + (begin if halo_ref.shape[0] > groups else 0), i], kind == "up")
        total = zero
        for level in range(LEVELS):
            steps = (length >> level) // LAGS
            store = stores[level]
            source = None if level == 0 else stores[level - 1]

            def read(at, source=source):
                return series[at, lanes, :] - dark if source is None else source[at]

            def step(index, carry, read=read, level=level, store=store):
                older, sums, total = carry
                newer = [read(index * LAGS + i) for i in range(LAGS)]
                pairs = pair_sums(newer)
                if store is not None:
                    for i in range(LAGS // 2):
                        store[index * (LAGS // 2) + i] = pairs[i]
                if level == 0:
                    while len(pairs) > 1:
                        pairs = pair_sums(pairs)
                    total = total + pairs[0]
                return newer, add_lags(older, newer, sums), total

            before = halo[level] if kind == "up" else [zero] * LAGS
            older, sums, total = lax.fori_loop(0, steps, step, (before, [zero] * LAGS, total))
            if kind == "full":
                after_rows = [jnp.where(inner, pltpu.roll(read(i), 8 - width, 0), 0.0) for i in range(LAGS)]
                sums = add_lags(older, after_rows, sums, cross_only=True)
            elif kind == "down":
                sums = add_lags(older, halo[level], sums, cross_only=True)
            for lag in range(LAGS):
                flat[group, pl.ds(level * LAGS + lag, 8, stride=ROWS), :] = sums[lag]
        totals[group] = total

    owners = gathered.shape[0]
    for owner in range(owners):
        if owner < taken:
            gathered[owner] = before_ref[owner]
            continue
        gathered[owner, per * ROWS :, :] = jnp.zeros((gathered.shape[1] - per * ROWS, 128), F32)
        for at in range(per):
            if kind == "full":
                blocks = [at // width * 8 + m * width + at % width for m in range(n_tm)]
            else:
                blocks = [(owner - taken) * per + at]
            gathered[owner, at * ROWS : (at + 1) * ROWS, :] = sum(
                flat[block // 8, block % 8 * ROWS : (block % 8 + 1) * ROWS, :] for block in blocks
            )
            gathered[owner, per * ROWS + at : per * ROWS + at + 1, :] = sum(
                totals[block // 8, block % 8 : block % 8 + 1, :] for block in blocks
            )

    for side, out in enumerate(outs):
        if len(outs) == 1:
            out[...] = gathered[...]
        elif out.shape[0] == 1 and len(outs) == owners > 2:
            out[0] = gathered[where_ref[1] ^ side]
        else:
            for owner in range(owners // 2):
                out[owner] = gathered[2 * owner + ((where_ref[1] & 1) ^ side)]


def sum_rows(per):
    return per * ROWS + (per + 7) // 8 * 8


def sums_part(where, pieces, dark, halo, before, split, kind, span, per, n_tm):
    n_pix = len(pieces)
    rows = pieces[0].shape[0]
    length = n_pix * rows
    groups = span[1]
    owners = groups * 8 // per
    taken = 0 if before is None else before.shape[0]
    if kind == "full":
        outs = [shape(1, sum_rows(per), 128)]
    else:
        outs = [shape((owners + taken) // split, sum_rows(per), 128)] * split
    extra = ([] if halo is None else [halo]) + ([] if before is None else [before])
    return pl.pallas_call(
        functools.partial(sums_kernel, kind, span, n_tm, per, n_pix, taken),
        out_shape=outs,
        in_specs=[SMEM, VMEM] + [VMEM] * len(extra) + [HBM] * n_pix,
        out_specs=[VMEM] * len(outs),
        scratch_shapes=[
            pltpu.VMEM((length, groups * 8, 128), F32),
            pltpu.VMEM((length // 2, 8, 128), F32),
            pltpu.VMEM((length // 4, 8, 128), F32),
            pltpu.VMEM((length // 8, 8, 128), F32),
            pltpu.VMEM((groups, 8 * ROWS, 128), F32),
            pltpu.VMEM((groups, 8, 128), F32),
            pltpu.VMEM((1 if kind == "full" else owners + taken, sum_rows(per), 128), F32),
            pltpu.SemaphoreType.DMA((groups,)),
        ],
        compiler_params=params(),
        cost_estimate=cost(1.0 + 3.0 * length * groups / 256),
    )(where, dark, *extra, *pieces)


def add_kernel(step, where_ref, *refs):
    inputs, (keep_ref, send_ref) = refs[:-2], refs[-2:]
    pairs = list(zip(inputs[0::2], inputs[1::2]))
    low = ((where_ref[1] >> step) & 1) == 0
    sums = [(mine, got, i) for mine, got in pairs for i in range(mine.shape[0])]
    for owner in range(keep_ref.shape[0]):
        first, second = [mine[i] + got[i] for mine, got, i in sums[2 * owner : 2 * owner + 2]]
        keep_ref[owner] = jnp.where(low, first, second)
        send_ref[owner] = jnp.where(low, second, first)


def add_part(where, pairs, step):
    total = sum(mine.shape[0] for mine, _ in pairs)
    half = shape(total // 2, *pairs[0][0].shape[1:])
    flat = [value for pair in pairs for value in pair]
    return pl.pallas_call(
        functools.partial(add_kernel, step),
        out_shape=[half, half],
        in_specs=[SMEM] + [VMEM] * len(flat),
        out_specs=[VMEM, VMEM],
        compiler_params=params(),
        cost_estimate=cost(0.5),
    )(where, *flat)


def finish_kernel(parts, resp_ref, keep_ref, *refs):
    sums_refs, (g2_ref, mean_ref) = refs[:-2], refs[-2:]
    row = lax.broadcasted_iota(jnp.int32, (ROWS, 128), 0)
    level, lag = row // LAGS, row % LAGS + 1
    counts = (((FRAMES >> level) - lag) << (2 * level)).astype(F32)
    for start, per, terms in parts:
        mine, sums_refs = sums_refs[:terms], sums_refs[terms:]
        for at in range(per):
            product = sum(ref[0, at * ROWS : (at + 1) * ROWS, :] for ref in mine)
            total = sum(ref[0, per * ROWS + at : per * ROWS + at + 1, :] for ref in mine)
            block = start + at
            keep = keep_ref[block : block + 1, :]
            mean = total * (1.0 / FRAMES)
            g2_ref[:, block * 128 : (block + 1) * 128] = product / (counts * mean * mean) * keep
            mean_ref[block : block + 1, :] = mean / resp_ref[block : block + 1, :] * keep


class Box:
    def __init__(self, value):
        self.value = value


def unbox(got):
    return [got[k].value for k in range(len(got))]


def send(value, axis, pairs, *before):
    for box in before:
        value, box.value = lax.optimization_barrier((value, box.value))
    return Box(lax.ppermute(value, axis, pairs))


def swap(value, axis, other, *before):
    return send(value, axis, [(i, i ^ other) for i in range(lax.axis_size(axis))], *before)


class Line:
    def __init__(self, where):
        self.where = where

    def __call__(self, part, *args):
        outs = part(self.where, *args)
        outs, self.where = lax.optimization_barrier((outs, self.where))
        return outs

    def hold(self, value):
        value, self.where = lax.optimization_barrier((value, self.where))
        return value

    def follow(self, box):
        self.where, box.value = lax.optimization_barrier((self.where, box.value))


def body(raw_frames, frame_order, owner_map, pixel_mask, dark, flat, polarization, solid_angle):
    n_pix = lax.axis_size("pix")
    n_tm = lax.axis_size("tm")
    n_blocks = owner_map.shape[0]
    owned = n_blocks // n_pix
    share = owned // n_tm
    width = 8 // n_tm

    plan = []
    shifts = []
    start = 0
    for kind, eighths in PARTS:
        per = share * eighths // 8
        plan.append((kind, start, per))
        if kind == "seg":
            shifts += [(False, g * share + start + j) for g in range(n_tm) for j in range(per)]
        else:
            shifts += [
                (True, start + unit * width + j) for unit in range(per // width) for _ in range(n_tm) for j in range(width)
            ]
        start += per

    where = jnp.stack([lax.axis_index("pix"), lax.axis_index("tm")]).astype(jnp.int32)
    where = jnp.concatenate([where, frame_order, owner_map])
    sizes = (owned, share, n_pix, n_tm)
    pack = functools.partial(pack_parts, raw_frames)
    (first, second, full) = plan
    line = Line(where)

    far = list(range(n_pix - 1, 1, -1))
    chain = [k for k in range(2, n_tm)]
    others = chain + [1, 0]

    early, late = [1] + far[0::2], far[1::2] + [0]
    mine = dict(zip(early, line(pack, [first + (early,)], *sizes)))
    got_first = {k: swap(mine[k], "pix", k) for k in early}
    line.follow(got_first[1])
    raw = dict(zip(others, line(pack, [full + (others,)], *sizes)))
    got_full = {0: Box(raw[0]), 1: swap(raw[1], "tm", 1)}
    for at, k in enumerate(chain):
        got_full[k] = swap(raw[k], "tm", k, *[got_full[j] for j in chain[:at][-1:]])
    mine.update(zip(late, line(pack, [first + (late,)], *sizes)))
    got_first[0] = Box(mine[0])
    for k in late[:-1]:
        got_first[k] = swap(mine[k], "pix", k, got_first[k + 1])

    lead, ahead, behind = far[0], far[2::2] + [far[1]], far[3::2]
    order = far + [1, 0]
    mine = dict(zip(order, line(pack, [second + (order,)], *sizes)))
    got_second = {0: Box(mine[0]), lead: swap(mine[lead], "pix", lead, got_full[1], got_first[lead])}
    for k in ahead:
        also = [got_full[j] for j in chain[1:]] if k == ahead[1] else []
        got_second[k] = swap(mine[k], "pix", k, got_first[k if k == far[1] else k - 1], *also)

    dark_own, resp_own, keep_own = line(
        constants_part, dark, flat, polarization, solid_angle, pixel_mask, shifts, owned, share, 2 + raw_frames.shape[0]
    )
    darks = []
    used = 0
    for _, _, per in plan:
        darks.append(dark_own[used : used + n_tm * per])
        used += n_tm * per

    upward = [(i, i + 1) for i in range(n_tm - 1)]
    ways = (upward, [(j, i) for i, j in upward])

    def halos(got, dark_part, sides):
        return [send(edge, "tm", way) for edge, way in zip(line(edge_part, unbox(got), dark_part, sides), ways)]

    def sums(got, dark_part, halo, before, split, kind, span, per):
        halo = None if halo is None else halo.value
        return line(sums_part, unbox(got), dark_part, halo, before, split, kind, span, per, n_tm)

    def reduce(pairs):
        for step in range(1, n_tm.bit_length() - 1):
            keep, away = line(add_part, [(mine, box.value) for mine, box in pairs], step)
            pairs = [(keep, swap(away, "tm", 1 << step))]
        return pairs

    line.follow(got_full[1])
    halo = halos(got_first, darks[0], 2)
    half = n_tm * first[2] // 16
    turned = line(turn_part, unbox(got_full), n_pix, n_tm)
    (before,) = sums(got_first, darks[0], halo[0], None, 1, "up", (0, half), first[2])
    for k in ahead:
        line.follow(got_second[k])
    for k in behind:
        got_second[k] = swap(mine[k], "pix", k, got_second[k + 1])
    got_second[1] = swap(mine[1], "pix", 1, got_second[ahead[0]])
    got_full = {0: Box(turned[0]), lead: swap(turned[lead], "pix", lead, got_second[far[1]])}
    keep, away = sums(got_first, darks[0], halo[1], before, 2, "down", (half, half), first[2])
    pairs = [(keep, swap(away, "tm", 1))]

    for k in ahead:
        before_it = got_full[lead] if k == far[1] else got_second[k - 1]
        got_full[k] = swap(line.hold(turned[k]), "pix", k, before_it)
    (halo,) = halos(got_second, darks[1], 1)
    half = n_tm * second[2] // 16
    (before,) = sums(got_second, darks[1], halo, None, 1, "up", (0, half), second[2])
    terms = [list(pair) for pair in reduce(pairs)]
    for k in ahead:
        line.follow(got_full[k])
    for k in behind:
        got_full[k] = swap(turned[k], "pix", k, got_full[k + 1])
    got_full[1] = swap(turned[1], "pix", 1, got_full[ahead[0]])
    mine = sums(got_second, darks[1], halo, before, n_tm, "up", (half, half), second[2])
    terms.append([mine[0]] + [swap(mine[k], "tm", k) for k in chain + [1]])
    terms = [[value.value if isinstance(value, Box) else value for value in part] for part in terms]
    terms.append(sums(got_full, darks[2], None, None, 1, "full", (0, n_tm * full[2] // 8), full[2]))

    g2, mean = pl.pallas_call(
        functools.partial(
            finish_kernel, [(start, per, len(part)) for (_, start, per), part in zip(plan, terms)]
        ),
        out_shape=[shape(ROWS, share * 128), shape(share, 128)],
        in_specs=[VMEM] * (2 + sum(len(part) for part in terms)),
        out_specs=[VMEM, VMEM],
        compiler_params=params(),
        cost_estimate=cost(1.0),
    )(resp_own, keep_own, *[value for part in terms for value in part])
    return g2.reshape(LEVELS, LAGS, share * 128), mean.reshape(share * 128)


def solution(mesh):
    return jax.shard_map(
        body,
        mesh=mesh,
        in_specs=(P(("tm", "pix"), None), P(("tm", "pix")), P(), P(), P(), P(), P(), P()),
        out_specs=(P(None, None, ("pix", "tm")), P(("pix", "tm"))),
        check_vma=False,
    )
```

```python
import functools

import jax
import jax.numpy as jnp
from jax import lax
from jax.experimental import pallas as pl
from jax.experimental.pallas import tpu as pltpu
from jax.sharding import PartitionSpec as P

FRAMES = 1024
LAGS = 16
LEVELS = 4
ROWS = LEVELS * LAGS
EDGE = LAGS + 8 * (LEVELS - 1)
EDGE_SPAN = LAGS << (LEVELS - 1)

PARTS = (("seg", 4), ("seg", 2), ("full", 2))

SMEM = pl.BlockSpec(memory_space=pltpu.SMEM)
VMEM = pl.BlockSpec(memory_space=pltpu.VMEM)
HBM = pl.BlockSpec(memory_space=pl.ANY)
F32 = jnp.float32


def params():
    return pltpu.CompilerParams(vmem_limit_bytes=40 << 20)


def cost(micros):
    return pl.CostEstimate(flops=0, bytes_accessed=int(micros * 3.6e6), transcendentals=0)


def shape(*dims):
    return jax.ShapeDtypeStruct(dims, F32)


def pack_kernel(jobs, owned, share, n_pix, n_tm, where_ref, frames_ref, *refs):
    outs, inverse = refs[:-1], refs[-1]
    rows = frames_ref.shape[0]
    pix, tm = where_ref[0], where_ref[1]
    for i in range(rows):
        inverse[where_ref[2 + i]] = i

    def eight(position_of, store):
        blocks = [where_ref[2 + rows + position_of(i)] for i in range(8)]
        for high in range(rows // 8):
            tiles = [
                frames_ref[high * 8 : high * 8 + 8, pl.ds(pl.multiple_of(block * 128, 128), 128)] for block in blocks
            ]
            turned = jnp.swapaxes(jnp.stack(tiles), 0, 1)
            for low in range(8):
                store(inverse[high * 8 + low], turned[low])

    taken = 0
    for kind, start, per, others in jobs:
        if kind == "seg":
            for at, other in enumerate(others):
                out = outs[taken + at]
                base = (pix ^ other) * owned + start

                @pl.loop(0, out.shape[1] // 8)
                def _(group, out=out, base=base, per=per):
                    def position_of(i):
                        pos = group * 8 + i
                        return base + (pos // per) * share + pos % per

                    def store(row, value):
                        out[row, pl.ds(pl.multiple_of(group * 8, 8), 8), :] = value

                    eight(position_of, store)

            taken += len(others)
        else:
            width = 8 // n_tm
            for at, other in enumerate(others):
                out = outs[taken + at]
                base = (tm ^ other) * share + start

                @pl.loop(0, out.shape[0] * out.shape[1])
                def _(at, out=out, base=base, width=width):
                    unit, group = at // out.shape[1], at % out.shape[1]

                    def position_of(i):
                        pos = group * 8 + i
                        return base + (pos // width) * owned + unit * width + pos % width

                    def store(row, value):
                        out[unit, group, row] = value

                    eight(position_of, store)

            taken += len(others)


def pack_parts(raw_frames, where, jobs, owned, share, n_pix, n_tm):
    rows = raw_frames.shape[0]
    outs = []
    size = 0
    for kind, _, per, others in jobs:
        if kind == "seg":
            outs += [shape(rows, n_tm * per, 128)] * len(others)
            size += per * len(others) / n_pix
        else:
            width = 8 // n_tm
            outs += [shape(per // width, n_pix * width // 8, rows, 8, 128)] * len(others)
            size += per
    return pl.pallas_call(
        functools.partial(pack_kernel, jobs, owned, share, n_pix, n_tm),
        out_shape=outs,
        in_specs=[SMEM, VMEM],
        out_specs=[VMEM] * len(outs),
        scratch_shapes=[pltpu.SMEM((rows,), jnp.int32)],
        compiler_params=params(),
        cost_estimate=cost(1.0 + 8.0 * size / share),
    )(where, raw_frames)


def turn_kernel(n_pix, n_tm, where_ref, *refs):
    pieces, outs, (held, staged, sem) = refs[:n_tm], refs[n_tm : n_tm + n_pix], refs[n_tm + n_pix :]
    units, groups, rows = pieces[0].shape[:3]
    width = 8 // n_tm
    for other in range(n_tm):
        pltpu.make_async_copy(pieces[other], held.at[where_ref[1] ^ other], sem).start()
    pltpu.make_async_copy(held, held, sem).wait()
    place = lax.broadcasted_iota(jnp.int32, (8, 128), 0) // width

    @pl.loop(0, rows)
    def _(row):
        for unit in range(units):
            for group in range(groups):
                got = [held[m, unit, group, row] for m in range(n_tm)]
                for to in range(n_tm):
                    value = got[to]
                    for m in range(n_tm):
                        if m != to:
                            value = jnp.where(place == m, pltpu.roll(got[m], (m - to) * width % 8, 0), value)
                    staged[group * n_tm + to, row, unit * 8 : unit * 8 + 8, :] = value

    for other in range(n_pix):
        outs[other][...] = staged[where_ref[0] ^ other]


def turn_part(where, pieces, n_pix, n_tm):
    units, groups, rows = pieces[0].shape[:3]
    return pl.pallas_call(
        functools.partial(turn_kernel, n_pix, n_tm),
        out_shape=[shape(rows, units * 8, 128)] * n_pix,
        in_specs=[SMEM] + [HBM] * n_tm,
        out_specs=[VMEM] * n_pix,
        scratch_shapes=[
            pltpu.VMEM((n_tm,) + pieces[0].shape, F32),
            pltpu.VMEM((n_pix, rows, units * 8, 128), F32),
            pltpu.SemaphoreType.DMA,
        ],
        compiler_params=params(),
        cost_estimate=cost(3.0),
    )(where, *pieces)


def constants_kernel(
    plan, owned, share, skip, where_ref, dark_ref, flat_ref, pol_ref, solid_ref, mask_ref, dark_out, resp_out, keep_out
):
    base = where_ref[0] * owned
    mine = base + where_ref[1] * share
    for at, (from_mine, shift) in enumerate(plan):
        row = pl.ds(where_ref[skip + (mine if from_mine else base) + shift], 1)
        dark_out[at : at + 1, :] = dark_ref[row, :]
    for at in range(share):
        row = pl.ds(where_ref[skip + mine + at], 1)
        resp_out[at : at + 1, :] = flat_ref[row, :] * pol_ref[row, :] * solid_ref[row, :]
        keep_out[at : at + 1, :] = mask_ref[row, :].astype(F32)


def constants_part(where, dark, flat, polarization, solid_angle, pixel_mask, shifts, owned, share, skip):
    n_blocks = where.shape[0] - skip
    tables = [t.reshape(n_blocks, 128) for t in (dark, flat, polarization, solid_angle, pixel_mask)]
    return pl.pallas_call(
        functools.partial(constants_kernel, shifts, owned, share, skip),
        out_shape=[shape(owned, 128), shape(share, 128), shape(share, 128)],
        in_specs=[SMEM] + [VMEM] * 5,
        out_specs=[VMEM] * 3,
        compiler_params=params(),
        cost_estimate=cost(1.0),
    )(where, *tables)


def pair_sums(rows):
    return [rows[2 * i] + rows[2 * i + 1] for i in range(len(rows) // 2)]


def edge_kernel(n_pix, where_ref, dark_ref, *refs):
    pieces, outs, (held, sem) = refs[:n_pix], refs[n_pix:-2], refs[-2:]
    rows = pieces[0].shape[0]
    blocks = EDGE_SPAN // rows
    half = held.shape[2]
    for other in range(n_pix):
        source = where_ref[0] ^ other
        for side, first in ((0, n_pix - blocks), (1, 0))[: len(outs)]:

            @pl.when((source >= first) & (source < first + blocks))
            def _(other=other, source=source, side=side, first=first):
                pltpu.make_async_copy(
                    pieces[other].at[:, pl.ds(side * half, half), :],
                    held.at[side, pl.ds((source - first) * rows, rows)],
                    sem,
                ).start()

    pltpu.make_async_copy(held, held, sem).wait()

    for side, out_ref in enumerate(outs):

        @pl.loop(0, half // 8)
        def _(group, side=side, out_ref=out_ref):
            lanes = pl.ds(pl.multiple_of(group * 8, 8), 8)
            dark = dark_ref[pl.ds(pl.multiple_of(group * 8 + side * half, 8), 8), :]
            span = 0
            for level in range(LEVELS):
                count = LAGS if level == 0 else LAGS // 2
                width = 1 << level
                begin = span if side else EDGE_SPAN - span - count * width
                for i in range(count):
                    at = begin + i * width
                    got = [held[side, at + j, lanes, :] - dark for j in range(width)]
                    while len(got) > 1:
                        got = pair_sums(got)
                    out_ref[group, (LAGS + 8 * (level - 1) if level else 0) + i] = got[0]
                span += count * width


def edge_part(where, pieces, dark, sides):
    n_pix = len(pieces)
    half = pieces[0].shape[1] // sides
    return pl.pallas_call(
        functools.partial(edge_kernel, n_pix),
        out_shape=[shape(half // 8, EDGE, 8, 128)] * sides,
        in_specs=[SMEM, VMEM] + [HBM] * n_pix,
        out_specs=[VMEM] * sides,
        scratch_shapes=[pltpu.VMEM((sides, EDGE_SPAN, half, 128), F32), pltpu.SemaphoreType.DMA],
        compiler_params=params(),
        cost_estimate=cost(2.0),
    )(where, dark, *pieces)


def add_lags(older, newer, sums, cross_only=False):
    both = older + newer
    out = []
    for lag in range(1, LAGS + 1):
        total = sums[lag - 1]
        for i in range(lag if cross_only else LAGS):
            total = total + both[LAGS + i] * both[LAGS + i - lag]
        out.append(total)
    return out


def edge_rows(read, last):
    rows = [read(i) for i in range(LAGS)]
    levels = [rows]
    for level in range(1, LEVELS):
        own = [read(LAGS + 8 * (level - 1) + i) for i in range(8)]
        rows = own + pair_sums(rows) if last else pair_sums(rows) + own
        levels.append(rows)
    return levels


def sums_kernel(kind, span, n_tm, per, n_pix, taken, where_ref, dark_ref, *refs):
    refs = list(refs)
    halo_ref = refs.pop(0) if kind != "full" else None
    before_ref = refs.pop(0) if taken else None
    pieces, rest = refs[:n_pix], refs[n_pix:]
    outs, (series, up_one, up_two, up_three, flat, totals, gathered, sems) = rest[:-8], rest[-8:]
    rows = pieces[0].shape[0]
    length = rows * n_pix
    begin, groups = span
    for group in range(groups):
        for other in range(n_pix):
            pltpu.make_async_copy(
                pieces[other].at[:, pl.ds((begin + group) * 8, 8), :],
                series.at[pl.ds((where_ref[0] ^ other) * rows, rows), pl.ds(group * 8, 8), :],
                sems.at[group],
            ).start()
    zero = jnp.zeros((8, 128), F32)
    stores = (up_one, up_two, up_three, None)
    width = 8 // n_tm
    inner = lax.broadcasted_iota(jnp.int32, (8, 128), 0) < 8 - width

    @pl.loop(0, groups)
    def _(group):
        lanes = pl.ds(pl.multiple_of(group * 8, 8), 8)
        whole = series.at[:, lanes, :]
        pltpu.make_async_copy(whole, whole, sems.at[group]).wait()
        dark = dark_ref[pl.ds(pl.multiple_of((begin + group) * 8, 8), 8), :]
        if kind != "full":
            halo = edge_rows(lambda i: halo_ref[group + (begin if halo_ref.shape[0] > groups else 0), i], kind == "up")
        total = zero
        for level in range(LEVELS):
            steps = (length >> level) // LAGS
            store = stores[level]
            source = None if level == 0 else stores[level - 1]

            def read(at, source=source):
                return series[at, lanes, :] - dark if source is None else source[at]

            def step(index, carry, read=read, level=level, store=store):
                older, sums, total = carry
                newer = [read(index * LAGS + i) for i in range(LAGS)]
                pairs = pair_sums(newer)
                if store is not None:
                    for i in range(LAGS // 2):
                        store[index * (LAGS // 2) + i] = pairs[i]
                if level == 0:
                    while len(pairs) > 1:
                        pairs = pair_sums(pairs)
                    total = total + pairs[0]
                return newer, add_lags(older, newer, sums), total

            before = halo[level] if kind == "up" else [zero] * LAGS
            older, sums, total = lax.fori_loop(0, steps, step, (before, [zero] * LAGS, total))
            if kind == "full":
                after_rows = [jnp.where(inner, pltpu.roll(read(i), 8 - width, 0), 0.0) for i in range(LAGS)]
                sums = add_lags(older, after_rows, sums, cross_only=True)
            elif kind == "down":
                sums = add_lags(older, halo[level], sums, cross_only=True)
            for lag in range(LAGS):
                flat[group, pl.ds(level * LAGS + lag, 8, stride=ROWS), :] = sums[lag]
        totals[group] = total

    owners = gathered.shape[0]
    for owner in range(owners):
        if owner < taken:
            gathered[owner] = before_ref[owner]
            continue
        gathered[owner, per * ROWS :, :] = jnp.zeros((gathered.shape[1] - per * ROWS, 128), F32)
        for at in range(per):
            if kind == "full":
                blocks = [at // width * 8 + m * width + at % width for m in range(n_tm)]
            else:
                blocks = [(owner - taken) * per + at]
            gathered[owner, at * ROWS : (at + 1) * ROWS, :] = sum(
                flat[block // 8, block % 8 * ROWS : (block % 8 + 1) * ROWS, :] for block in blocks
            )
            gathered[owner, per * ROWS + at : per * ROWS + at + 1, :] = sum(
                totals[block // 8, block % 8 : block % 8 + 1, :] for block in blocks
            )

    for side, out in enumerate(outs):
        if len(outs) == 1:
            out[...] = gathered[...]
        elif out.shape[0] == 1 and len(outs) == owners > 2:
            out[0] = gathered[where_ref[1] ^ side]
        else:
            for owner in range(owners // 2):
                out[owner] = gathered[2 * owner + ((where_ref[1] & 1) ^ side)]


def sum_rows(per):
    return per * ROWS + (per + 7) // 8 * 8


def sums_part(where, pieces, dark, halo, before, split, kind, span, per, n_tm):
    n_pix = len(pieces)
    rows = pieces[0].shape[0]
    length = n_pix * rows
    groups = span[1]
    owners = groups * 8 // per
    taken = 0 if before is None else before.shape[0]
    if kind == "full":
        outs = [shape(1, sum_rows(per), 128)]
    else:
        outs = [shape((owners + taken) // split, sum_rows(per), 128)] * split
    extra = ([] if halo is None else [halo]) + ([] if before is None else [before])
    return pl.pallas_call(
        functools.partial(sums_kernel, kind, span, n_tm, per, n_pix, taken),
        out_shape=outs,
        in_specs=[SMEM, VMEM] + [VMEM] * len(extra) + [HBM] * n_pix,
        out_specs=[VMEM] * len(outs),
        scratch_shapes=[
            pltpu.VMEM((length, groups * 8, 128), F32),
            pltpu.VMEM((length // 2, 8, 128), F32),
            pltpu.VMEM((length // 4, 8, 128), F32),
            pltpu.VMEM((length // 8, 8, 128), F32),
            pltpu.VMEM((groups, 8 * ROWS, 128), F32),
            pltpu.VMEM((groups, 8, 128), F32),
            pltpu.VMEM((1 if kind == "full" else owners + taken, sum_rows(per), 128), F32),
            pltpu.SemaphoreType.DMA((groups,)),
        ],
        compiler_params=params(),
        cost_estimate=cost(1.0 + 3.0 * length * groups / 256),
    )(where, dark, *extra, *pieces)


def add_kernel(step, where_ref, *refs):
    inputs, (keep_ref, send_ref) = refs[:-2], refs[-2:]
    pairs = list(zip(inputs[0::2], inputs[1::2]))
    low = ((where_ref[1] >> step) & 1) == 0
    sums = [(mine, got, i) for mine, got in pairs for i in range(mine.shape[0])]
    for owner in range(keep_ref.shape[0]):
        first, second = [mine[i] + got[i] for mine, got, i in sums[2 * owner : 2 * owner + 2]]
        keep_ref[owner] = jnp.where(low, first, second)
        send_ref[owner] = jnp.where(low, second, first)


def add_part(where, pairs, step):
    total = sum(mine.shape[0] for mine, _ in pairs)
    half = shape(total // 2, *pairs[0][0].shape[1:])
    flat = [value for pair in pairs for value in pair]
    return pl.pallas_call(
        functools.partial(add_kernel, step),
        out_shape=[half, half],
        in_specs=[SMEM] + [VMEM] * len(flat),
        out_specs=[VMEM, VMEM],
        compiler_params=params(),
        cost_estimate=cost(0.5),
    )(where, *flat)


def finish_kernel(parts, resp_ref, keep_ref, *refs):
    sums_refs, (g2_ref, mean_ref) = refs[:-2], refs[-2:]
    row = lax.broadcasted_iota(jnp.int32, (ROWS, 128), 0)
    level, lag = row // LAGS, row % LAGS + 1
    counts = (((FRAMES >> level) - lag) << (2 * level)).astype(F32)
    for start, per, terms in parts:
        mine, sums_refs = sums_refs[:terms], sums_refs[terms:]
        for at in range(per):
            product = sum(ref[0, at * ROWS : (at + 1) * ROWS, :] for ref in mine)
            total = sum(ref[0, per * ROWS + at : per * ROWS + at + 1, :] for ref in mine)
            block = start + at
            keep = keep_ref[block : block + 1, :]
            mean = total * (1.0 / FRAMES)
            g2_ref[:, block * 128 : (block + 1) * 128] = product / (counts * mean * mean) * keep
            mean_ref[block : block + 1, :] = mean / resp_ref[block : block + 1, :] * keep


class Box:
    def __init__(self, value):
        self.value = value


def unbox(got):
    return [got[k].value for k in range(len(got))]


def send(value, axis, pairs, *before):
    for box in before:
        value, box.value = lax.optimization_barrier((value, box.value))
    return Box(lax.ppermute(value, axis, pairs))


def swap(value, axis, other, *before):
    return send(value, axis, [(i, i ^ other) for i in range(lax.axis_size(axis))], *before)


class Line:
    def __init__(self, where):
        self.where = where

    def __call__(self, part, *args):
        outs = part(self.where, *args)
        outs, self.where = lax.optimization_barrier((outs, self.where))
        return outs

    def hold(self, value):
        value, self.where = lax.optimization_barrier((value, self.where))
        return value

    def follow(self, box):
        self.where, box.value = lax.optimization_barrier((self.where, box.value))


def body(raw_frames, frame_order, owner_map, pixel_mask, dark, flat, polarization, solid_angle):
    n_pix = lax.axis_size("pix")
    n_tm = lax.axis_size("tm")
    n_blocks = owner_map.shape[0]
    owned = n_blocks // n_pix
    share = owned // n_tm
    width = 8 // n_tm

    plan = []
    shifts = []
    start = 0
    for kind, eighths in PARTS:
        per = share * eighths // 8
        plan.append((kind, start, per))
        if kind == "seg":
            shifts += [(False, g * share + start + j) for g in range(n_tm) for j in range(per)]
        else:
            shifts += [
                (True, start + unit * width + j) for unit in range(per // width) for _ in range(n_tm) for j in range(width)
            ]
        start += per

    where = jnp.stack([lax.axis_index("pix"), lax.axis_index("tm")]).astype(jnp.int32)
    where = jnp.concatenate([where, frame_order, owner_map])
    sizes = (owned, share, n_pix, n_tm)
    pack = functools.partial(pack_parts, raw_frames)
    (first, second, full) = plan
    line = Line(where)

    far = list(range(n_pix - 1, 1, -1))
    chain = [k for k in range(2, n_tm)]
    others = chain + [1, 0]

    early, late = [1] + far[0::2], far[1::2] + [0]
    mine = dict(zip(early, line(pack, [first + (early,)], *sizes)))
    got_first = {k: swap(mine[k], "pix", k) for k in early}
    line.follow(got_first[1])
    raw = dict(zip(others, line(pack, [full + (others,)], *sizes)))
    got_full = {0: Box(raw[0]), 1: swap(raw[1], "tm", 1)}
    for at, k in enumerate(chain):
        got_full[k] = swap(raw[k], "tm", k, *[got_full[j] for j in chain[:at][-1:]])
    mine.update(zip(late, line(pack, [first + (late,)], *sizes)))
    got_first[0] = Box(mine[0])
    for k in late[:-1]:
        got_first[k] = swap(mine[k], "pix", k, got_first[k + 1])

    lead, ahead, behind = far[0], far[2::2] + [far[1]], far[3::2]
    order = far + [1, 0]
    mine = dict(zip(order, line(pack, [second + (order,)], *sizes)))
    got_second = {0: Box(mine[0]), lead: swap(mine[lead], "pix", lead, got_full[1], got_first[lead])}
    for k in ahead:
        also = [got_full[j] for j in chain[1:]] if k == ahead[1] else []
        got_second[k] = swap(mine[k], "pix", k, got_first[k if k == far[1] else k - 1], *also)

    dark_own, resp_own, keep_own = line(
        constants_part, dark, flat, polarization, solid_angle, pixel_mask, shifts, owned, share, 2 + raw_frames.shape[0]
    )
    darks = []
    used = 0
    for _, _, per in plan:
        darks.append(dark_own[used : used + n_tm * per])
        used += n_tm * per

    upward = [(i, i + 1) for i in range(n_tm - 1)]
    ways = (upward, [(j, i) for i, j in upward])

    def halos(got, dark_part, sides):
        return [send(edge, "tm", way) for edge, way in zip(line(edge_part, unbox(got), dark_part, sides), ways)]

    def sums(got, dark_part, halo, before, split, kind, span, per):
        halo = None if halo is None else halo.value
        return line(sums_part, unbox(got), dark_part, halo, before, split, kind, span, per, n_tm)

    def reduce(pairs):
        for step in range(1, n_tm.bit_length() - 1):
            keep, away = line(add_part, [(mine, box.value) for mine, box in pairs], step)
            pairs = [(keep, swap(away, "tm", 1 << step))]
        return pairs

    line.follow(got_full[1])
    halo = halos(got_first, darks[0], 2)
    half = n_tm * first[2] // 16
    turned = line(turn_part, unbox(got_full), n_pix, n_tm)
    (before,) = sums(got_first, darks[0], halo[0], None, 1, "up", (0, half), first[2])
    for k in ahead:
        line.follow(got_second[k])
    for k in behind:
        got_second[k] = swap(mine[k], "pix", k, got_second[k + 1])
    got_second[1] = swap(mine[1], "pix", 1, got_second[ahead[0]])
    got_full = {0: Box(turned[0]), lead: swap(turned[lead], "pix", lead, got_second[far[1]])}
    keep, away = sums(got_first, darks[0], halo[1], before, 2, "down", (half, half), first[2])
    pairs = [(keep, swap(away, "tm", 1))]

    for k in ahead:
        before_it = got_full[lead] if k == far[1] else got_second[k - 1]
        got_full[k] = swap(line.hold(turned[k]), "pix", k, before_it)
    (halo,) = halos(got_second, darks[1], 1)
    terms = [list(pair) for pair in reduce(pairs)]
    mine = sums(got_second, darks[1], halo, None, n_tm, "up", (0, n_tm * second[2] // 8), second[2])
    for k in behind:
        got_full[k] = swap(turned[k], "pix", k, got_full[k + 1])
    got_full[1] = swap(turned[1], "pix", 1, got_full[ahead[0]])
    terms.append([mine[0]] + [swap(mine[k], "tm", k) for k in chain + [1]])
    terms = [[value.value if isinstance(value, Box) else value for value in part] for part in terms]
    terms.append(sums(got_full, darks[2], None, None, 1, "full", (0, n_tm * full[2] // 8), full[2]))

    g2, mean = pl.pallas_call(
        functools.partial(
            finish_kernel, [(start, per, len(part)) for (_, start, per), part in zip(plan, terms)]
        ),
        out_shape=[shape(ROWS, share * 128), shape(share, 128)],
        in_specs=[VMEM] * (2 + sum(len(part) for part in terms)),
        out_specs=[VMEM, VMEM],
        compiler_params=params(),
        cost_estimate=cost(1.0),
    )(resp_own, keep_own, *[value for part in terms for value in part])
    return g2.reshape(LEVELS, LAGS, share * 128), mean.reshape(share * 128)


def solution(mesh):
    return jax.shard_map(
        body,
        mesh=mesh,
        in_specs=(P(("tm", "pix"), None), P(("tm", "pix")), P(), P(), P(), P(), P(), P()),
        out_specs=(P(None, None, ("pix", "tm")), P(("pix", "tm"))),
        check_vma=False,
    )
```
